512 devices in a mesh: segment: 2 (over core), row: 16 (over z_lo, y), col: 16 (over z_hi, x).
Axes of the slice: x: 4, y: 4, z: 16 (z_hi: 4, z_lo: 4; z = z_hi * 4 + z_lo), core: 2. Of those that a mesh axis runs over, the one named last changes fastest.
Arguments:
- activations: bfloat16 [2, 384, 384, 128], P('segment', 'row', 'col'), may hold values from -6 to 6
- cotangent: bfloat16 [2, 384, 384, 128], P('segment', 'row', 'col'), may hold values from -6 to 6
- conv_weight: bfloat16 [2, 9, 128, 64], P('segment'), may hold values from -0.1875 to 0.1875
- conv_bias: bfloat16 [2, 64], P('segment'), may hold values from -3 to 3
- out_weight: bfloat16 [2, 64, 128], P('segment'), may hold values from -0.75 to 0.75
Outputs:
- input_gradient: bfloat16 [2, 384, 384, 128], P('segment', 'row', 'col')
- conv_gradient: float32 [2, 9, 128, 64], P('segment')
- bias_gradient: float32 [2, 64], P('segment')
- output_weight_gradient: float32 [2, 64, 128], P('segment')
The draws below stay inside these ranges and needn't reach their ends.
All inputs are finite; a program needn't handle non-finite values.
Results may differ from the reference program's by a relative error of at most 0.022.
The reference program's roundings to bfloat16 on the way (of `hidden`, `bottle`, `branch_sum`, `sym`, `grad_branch` and `grad_pre`) count: a program that leaves them out, or rounds other values in their place, can miss the bound.
Values may be sent and summed in bfloat16 or wider, within the bound.
A program may use at most 64 MiB of HBM per device.

```python
import jax
import jax.numpy as jnp
from jax import lax

C = 128
K = 64
FIRST_DILATION = 2
SECOND_DILATION = 8
MB = 2
NB = 384


def with_spikes(drawn, own_key, source, target, blocks, factor):
    def block_of(position):
        return (jnp.arange(drawn.shape[position]) // (drawn.shape[position] // blocks)).reshape((-1,) + (1,) * (drawn.ndim - 1 - position))

    one_side = jax.random.permutation(own_key, blocks)[block_of(target)]
    second = (block_of(target) + blocks // 2) % blocks
    return jnp.where((block_of(source) == one_side) | (block_of(source) == second), factor * drawn, drawn)


def steps_of(own_key, extent, shards, low, high):
    level = 1.0
    for axis_at, shards_of in shards:
        heights = jax.random.uniform(jax.random.fold_in(jax.random.fold_in(own_key, 6), axis_at), (shards_of,), jnp.float32, low / len(shards), high / len(shards))
        level = level * jnp.repeat(jnp.exp(heights), extent[axis_at] // shards_of).reshape((-1,) + (1,) * (len(extent) - 1 - axis_at))
    return level


def centred(rng, shape, width, reach, pieces=(), dtype=jnp.bfloat16):
    factor_of = steps_of(rng, shape, pieces, -0.22, 0.18) if pieces else 1.0
    drawn = jax.random.normal(rng, shape, jnp.float32) * width * factor_of
    return jnp.minimum(jnp.maximum(drawn, -reach), reach).astype(dtype)


def noise_with(stream_key, dims, width, most, shards, heavy, kind=jnp.bfloat16):
    entries = width * jax.random.normal(stream_key, dims, jnp.float32)
    if shards:
        entries = entries * steps_of(stream_key, dims, shards, -0.22, 0.18)
    return jnp.clip(with_spikes(entries, jax.random.fold_in(stream_key, 3), *heavy), -most, most).astype(kind)


def setup_inputs(seed: int = 0) -> dict:
    keys = jax.random.split(jax.random.key(seed), 6)
    activations = centred(keys[0], (MB, NB, NB, C), 1.0, 6.0, ((0, 2), (1, 16), (2, 16)))
    cotangent = noise_with(keys[1], (MB, NB, NB, C), 1.0, 6.0, ((0, 2), (1, 16), (2, 16)), (1, 3, 16, 2.0))
    conv_weight = centred(keys[2], (2, 9, C, K), (9 * C) ** -0.5, 0.1875, ((0, 2),))
    conv_bias = centred(keys[3], (2, K), 0.5, 3.0, ((0, 2),))
    out_weight = centred(keys[4], (2, K, C), K ** -0.5, 0.75, ((0, 2),))
    return {"activations": activations, "cotangent": cotangent, "conv_weight": conv_weight, "conv_bias": conv_bias, "out_weight": out_weight}


def tap_window(padded, dilation, row_offset_tap, col_tap, side):
    row_start = dilation * (1 + row_offset_tap)
    col_start = dilation * (1 + col_tap)
    return padded[row_start:row_start + side, col_start:col_start + side]

def forward_section(inputs, conv, bias, projection, dilation):
    side = inputs.shape[0]
    channels = inputs.shape[2]
    hidden = jnp.maximum(inputs, 0)
    padded = jnp.pad(hidden, ((dilation, dilation), (dilation, dilation), (0, 0)))
    summed = jnp.zeros((side * side, conv.shape[2]), jnp.float32)
    for tap_index in range(9):
        window = tap_window(padded, dilation, tap_index // 3 - 1, tap_index % 3 - 1, side)
        summed = summed + jnp.dot(window.reshape(-1, channels), conv[tap_index], preferred_element_type=jnp.float32)
    pre_act = summed + bias.astype(jnp.float32)
    bottle = jnp.maximum(pre_act, 0.0).astype(jnp.bfloat16)
    branch_sum = (inputs.reshape(-1, channels).astype(jnp.float32) + jnp.dot(bottle, projection, preferred_element_type=jnp.float32)).astype(jnp.bfloat16).reshape(side, side, channels)
    sym = ((branch_sum.astype(jnp.float32) + jnp.swapaxes(branch_sum, 0, 1).astype(jnp.float32)) * 0.5).astype(jnp.bfloat16)
    return (sym, (inputs, padded, pre_act, bottle))

def backward_section(upstream, stored, conv, projection, dilation):
    inputs, padded, pre_act, bottle = stored
    side = inputs.shape[0]
    channels = inputs.shape[2]
    grad_branch = ((upstream.astype(jnp.float32) + jnp.swapaxes(upstream, 0, 1).astype(jnp.float32)) * 0.5).astype(jnp.bfloat16).reshape(-1, channels)
    grad_bottle = lax.dot_general(grad_branch, projection, (((1,), (1,)), ((), ())), preferred_element_type=jnp.float32)
    grad_pre = jnp.where(pre_act > 0, grad_bottle, 0.0).astype(jnp.bfloat16)
    grad_proj = lax.dot_general(bottle, grad_branch, (((0,), (0,)), ((), ())), preferred_element_type=jnp.float32)
    grad_bias = lax.optimization_barrier(jnp.sum(grad_pre.astype(jnp.float32), axis=0))
    conv_terms = []
    for tap_index in range(9):
        window = tap_window(padded, dilation, tap_index // 3 - 1, tap_index % 3 - 1, side)
        conv_terms.append(lax.dot_general(window.reshape(-1, channels), grad_pre, (((0,), (0,)), ((), ())), preferred_element_type=jnp.float32))
    grad_conv = jnp.stack(conv_terms)
    grad_square = grad_pre.reshape(side, side, -1)
    grad_padded = jnp.pad(grad_square, ((dilation, dilation), (dilation, dilation), (0, 0)))
    summed = jnp.zeros((side * side, channels), jnp.float32)
    for tap_index in range(9):
        window = tap_window(grad_padded, dilation, 1 - tap_index // 3, 1 - tap_index % 3, side)
        summed = summed + lax.dot_general(window.reshape(-1, window.shape[2]), conv[tap_index], (((1,), (1,)), ((), ())), preferred_element_type=jnp.float32)
    masked = jnp.where(inputs.reshape(-1, channels) > 0, summed, 0.0)
    grad_inputs = (grad_branch.astype(jnp.float32) + masked).astype(jnp.bfloat16).reshape(side, side, channels)
    return (grad_inputs, (grad_conv, grad_bias, grad_proj))

def reference(activations, cotangent, conv_weight, conv_bias, out_weight):
    dilation_list = (FIRST_DILATION, SECOND_DILATION)
    conv_total = jnp.zeros(conv_weight.shape, jnp.float32)
    bias_total = jnp.zeros(conv_bias.shape, jnp.float32)
    proj_total = jnp.zeros(out_weight.shape, jnp.float32)
    results = []
    for batch_index in range(activations.shape[0]):
        current = activations[batch_index]
        stored_list = []
        for section in range(2):
            current, stored = forward_section(current, conv_weight[section], conv_bias[section], out_weight[section], dilation_list[section])
            stored_list.append(stored)
        upstream = cotangent[batch_index]
        for section in (1, 0):
            upstream, section_grads = backward_section(upstream, stored_list[section], conv_weight[section], out_weight[section], dilation_list[section])
            conv_total = conv_total.at[section].add(section_grads[0])
            bias_total = bias_total.at[section].add(section_grads[1])
            proj_total = proj_total.at[section].add(section_grads[2])
        results.append(upstream)
    factor = 1.0 / jnp.sqrt(jnp.float32(activations.shape[0] * activations.shape[1] * activations.shape[2]))
    return (jnp.stack(results), conv_total * factor, bias_total * factor, proj_total * factor)
```

```python
import functools

import numpy as np

import jax
import jax.numpy as jnp
from jax import lax
from jax.experimental import pallas as pl
from jax.experimental.pallas import tpu as pltpu
from jax.sharding import PartitionSpec as P

MESH = pl.DeviceIdType.MESH
F32 = jnp.float32
BF16 = jnp.bfloat16

SIDE = 24
AREA = SIDE * SIDE
C = 128
K = 64
D0 = 2
D1 = 8
WIDE = 40
CONV_ROWS = 9 * C
PROJ_ROW = CONV_ROWS
BIAS_ROW = CONV_ROWS + K
PACK_ROWS = CONV_ROWS + K + 16
GRAD_BLOCKS = 12
GRAD_ROWS = GRAD_BLOCKS * K
DIRECTIONS = ((-1, 0), (1, 0), (0, -1), (0, 1), (-1, -1), (-1, 1), (1, -1), (1, 1))
OPPOSITE = (1, 0, 3, 2, 7, 6, 5, 4)
NT = (((1,), (1,)), ((), ()))
TN = (((0,), (0,)), ((), ()))


def dot(a, b, dims=(((1,), (0,)), ((), ()))):
    return lax.dot_general(a, b, dims, preferred_element_type=F32)


def kernel(
    n,
    factor,
    act,
    cot,
    conv_w,
    bias_w,
    proj_w,
    out_grad,
    out_conv,
    out_bias,
    out_proj,
    weights,
    rolled,
    w0t,
    w1cat,
    back1,
    back0,
    proj_diag,
    proj_twice,
    own_f,
    turned_f,
    stage_f,
    act_t,
    cot_t,
    act_m,
    cot_m,
    send_e0,
    send_c0,
    recv_e0,
    recv_c0,
    hidden1,
    hid_e,
    hid_c,
    recv_e1,
    recv_c1,
    gp1,
    gp1_e,
    gp1_c,
    recv_e2,
    recv_c2,
    gp0,
    gp0_e,
    gp0_c,
    recv_e3,
    recv_c3,
    pad_a,
    pad_b,
    pad_8,
    cols_a,
    cols_b,
    cols_8,
    cols_g,
    pre0,
    bottle0,
    grad_bot,
    bottle1,
    branch1,
    branch0,
    grads,
    grads_send,
    grads_recv,
    acc_send,
    plane_recv,
    line_recv,
    total_recv,
    halo_send,
    halo_recv,
    pair_send,
    pair_recv,
    plane_send_sem,
    plane_recv_sem,
    line_send_sem,
    line_recv_sem,
    all_send_sem,
    all_recv_sem,
):
    seg = lax.axis_index("segment")
    row = lax.axis_index("row")
    col = lax.axis_index("col")
    part = int(round(n**0.5))
    piece = GRAD_ROWS // n
    row_hi, row_lo = row // part, row % part
    col_hi, col_lo = col // part, col % part
    plane_me = row_lo * part + col_lo
    line_me = row_hi * part + col_hi
    off_diagonal = row != col

    def plane_peer(index):
        return (seg, row_hi * part + index // part, col_hi * part + index % part)

    def line_peer(index):
        return (seg, (index // part) * part + row_lo, (index % part) * part + col_lo)

    def neighbour(k):
        dr, dc = DIRECTIONS[k]
        r, c = row + dr, col + dc
        exists = None
        if dr:
            exists = (r >= 0) if dr < 0 else (r < n)
        if dc:
            side = (c >= 0) if dc < 0 else (c < n)
            exists = side if exists is None else jnp.logical_and(exists, side)
        return exists, (seg, r, c)

    for ref in (recv_e0, recv_c0, recv_e1, recv_c1, recv_e2, recv_c2, recv_e3, recv_c3):
        ref[...] = jnp.zeros_like(ref)

    barrier = pltpu.get_barrier_semaphore()

    def signal(device):
        pl.semaphore_signal(barrier, inc=1, device_id=device, device_id_type=MESH)

    greeted = jnp.int32(1 + 2 * (n - 1))
    for k in range(8):
        exists, device = neighbour(k)
        pl.when(exists)(functools.partial(signal, device))
        greeted = greeted + exists.astype(jnp.int32)
    mirror = (seg, col, row)
    pl.when(off_diagonal)(functools.partial(signal, mirror))
    greeted = greeted + off_diagonal.astype(jnp.int32)
    sibling = (1 - seg, row, col)
    signal(sibling)

    @pl.loop(1, n)
    def _(step):
        signal(plane_peer((plane_me + step) % n))
        signal(line_peer((line_me + step) % n))

    weights[seg] = jnp.zeros((PACK_ROWS, 128), BF16)
    weights[seg, 0:CONV_ROWS, 0:K] = conv_w[...]
    weights[seg, PROJ_ROW : PROJ_ROW + K] = proj_w[...]
    bias_row = bias_w[...].astype(F32)
    weights[seg, BIAS_ROW : BIAS_ROW + 16] = jnp.broadcast_to(
        jnp.concatenate([bias_row, bias_row], axis=1), (16, 2 * K)
    ).astype(BF16)

    def turn(flat, out):
        @pl.loop(0, SIDE // 2)
        def _(i):
            two = jnp.concatenate(
                [flat[pl.ds(2 * i, SIDE, stride=SIDE), :], flat[pl.ds(2 * i + 1, SIDE, stride=SIDE), :]], axis=0
            )
            out[pl.ds(pl.multiple_of(i * 2 * SIDE, 16), 2 * SIDE), :] = two.astype(BF16)

    own_f[...] = cot[...].astype(F32)
    turn(own_f, cot_t)
    own_f[...] = act[...].astype(F32)
    turn(own_f, act_t)

    pl.semaphore_wait(barrier, greeted)

    def mirror_copy(src, dst, index):
        return pltpu.make_async_remote_copy(
            src_ref=src,
            dst_ref=dst,
            send_sem=pair_send.at[index],
            recv_sem=pair_recv.at[index],
            device_id=mirror,
            device_id_type=MESH,
        )

    def mirror_start(src, dst, index):
        @pl.when(off_diagonal)
        def _():
            mirror_copy(src, dst, index).start()

        @pl.when(jnp.logical_not(off_diagonal))
        def _():
            dst[...] = src[...]

    def mirror_wait(src, dst, index):
        @pl.when(off_diagonal)
        def _():
            mirror_copy(src, dst, index).wait_recv()

    def sibling_copy(src, dst, index):
        return pltpu.make_async_remote_copy(
            src_ref=src,
            dst_ref=dst,
            send_sem=pair_send.at[index],
            recv_sem=pair_recv.at[index],
            device_id=sibling,
            device_id_type=MESH,
        )

    mirror_start(act_t, act_m, 0)
    weights_copy = sibling_copy(weights.at[seg], weights.at[seg], 2)
    weights_copy.start()

    def halo_copy(phase, k, sources, edges, corners):
        opposite = OPPOSITE[k]
        target = edges.at[opposite] if k < 4 else corners.at[opposite - 4]
        return pltpu.make_async_remote_copy(
            src_ref=sources[k],
            dst_ref=target,
            send_sem=halo_send.at[phase, k],
            recv_sem=halo_recv.at[phase, opposite],
            device_id=neighbour(k)[1],
            device_id_type=MESH,
        )

    def halo_arrival(phase, k, sources, edges, corners):
        target = edges.at[k] if k < 4 else corners.at[k - 4]
        return pltpu.make_async_remote_copy(
            src_ref=target,
            dst_ref=target,
            send_sem=halo_send.at[phase, k],
            recv_sem=halo_recv.at[phase, k],
            device_id=neighbour(k)[1],
            device_id_type=MESH,
        )

    def halo_start(phase, sources, edges, corners):
        for k in (7, 6, 5, 4, 3, 2, 1, 0):
            pl.when(neighbour(k)[0])(
                lambda k=k: halo_copy(phase, k, sources, edges, corners).start()
            )

    def halo_wait(phase, sources, edges, corners):
        for k in range(8):
            pl.when(neighbour(k)[0])(
                lambda k=k: halo_arrival(phase, k, sources, edges, corners).wait_recv()
            )

    def halo_sent(phase, sources, edges, corners):
        for k in range(8):
            pl.when(neighbour(k)[0])(
                lambda k=k: halo_copy(phase, k, sources, edges, corners).wait_send()
            )

    def pack_narrow(tiles, edges, corners):
        strip = D0 * SIDE
        for t, tile in enumerate(tiles):
            at = slice(t * strip, (t + 1) * strip)
            edges[0, at] = tile[0:strip].astype(BF16)
            edges[1, at] = tile[AREA - strip : AREA].astype(BF16)
            for k, first in ((2, 0), (3, SIDE - D0)):
                columns = [tile[pl.ds(first + j, SIDE, stride=SIDE), :] for j in range(D0)]
                edges[k, at] = jnp.concatenate(columns, axis=0).astype(BF16)
        for k, (r, c) in enumerate(((0, 0), (0, SIDE - D0), (SIDE - D0, 0), (SIDE - D0, SIDE - D0))):
            stage_f[0:16] = jnp.zeros((16, C), F32)
            for t, tile in enumerate(tiles):
                for i in range(D0):
                    start = (r + i) * SIDE + c
                    stage_f[t * 4 + i * D0 : t * 4 + (i + 1) * D0] = tile[start : start + D0]
            corners[k] = stage_f[0:16].astype(BF16)

    def unpack_narrow(t, edges, corners, pad, change):
        strip = D0 * SIDE
        at = slice(t * strip, (t + 1) * strip)
        north = change(edges[0, at].astype(F32))
        south = change(edges[1, at].astype(F32))
        west = change(edges[2, at].astype(F32))
        east = change(edges[3, at].astype(F32))
        for i in range(D0):
            lines = slice(i * SIDE, (i + 1) * SIDE)
            pad[i * WIDE + 8 : i * WIDE + 8 + SIDE] = north[lines]
            low = (D0 + SIDE + i) * WIDE + 8
            pad[low : low + SIDE] = south[lines]
            pad[pl.ds(D0 * WIDE + 8 - D0 + i, SIDE, stride=WIDE), :] = west[lines]
            pad[pl.ds(D0 * WIDE + 8 + SIDE + i, SIDE, stride=WIDE), :] = east[lines]
        for k, (r, c) in enumerate(((0, 8 - D0), (0, 8 + SIDE), (D0 + SIDE, 8 - D0), (D0 + SIDE, 8 + SIDE))):
            stage_f[0:16] = change(corners[k].astype(F32))
            for i in range(D0):
                start = (r + i) * WIDE + c
                pad[start : start + D0] = stage_f[t * 4 + i * D0 : t * 4 + (i + 1) * D0]

    def fill_centre(tile, pad, dilation, change):
        for i in range(SIDE):
            start = (dilation + i) * WIDE + 8
            pad[start : start + SIDE] = change(tile[i * SIDE : (i + 1) * SIDE])

    def pack_wide(tile, edges, corners):
        for k, first in ((0, 0), (1, SIDE - D1)):
            edges[k] = jnp.concatenate(
                [tile[i * SIDE + first : i * SIDE + first + D1] for i in range(SIDE)], axis=0
            ).astype(BF16)
        for k, (r, c) in enumerate(((0, 0), (0, SIDE - D1), (SIDE - D1, 0), (SIDE - D1, SIDE - D1))):
            corners[k] = jnp.concatenate(
                [tile[(r + i) * SIDE + c : (r + i) * SIDE + c + D1] for i in range(D1)], axis=0
            ).astype(BF16)

    def wide_sources(flat, edges, corners):
        strip = D1 * SIDE
        return (
            flat.at[0:strip],
            flat.at[AREA - strip : AREA],
            edges.at[0],
            edges.at[1],
        ) + tuple(corners.at[k] for k in range(4))

    def unpack_wide(edges, corners, pad):
        north = edges[0].astype(F32)
        south = edges[1].astype(F32)
        west = edges[2].astype(F32)
        east = edges[3].astype(F32)
        for i in range(D1):
            lines = slice(i * SIDE, (i + 1) * SIDE)
            pad[i * WIDE + D1 : i * WIDE + D1 + SIDE] = north[lines]
            low = (D1 + SIDE + i) * WIDE + D1
            pad[low : low + SIDE] = south[lines]
        for i in range(SIDE):
            lines = slice(i * D1, (i + 1) * D1)
            start = (D1 + i) * WIDE
            pad[start : start + D1] = west[lines]
            pad[start + D1 + SIDE : start + WIDE] = east[lines]
        for k, (r, c) in enumerate(((0, 0), (0, D1 + SIDE), (D1 + SIDE, 0), (D1 + SIDE, D1 + SIDE))):
            corner = corners[k].astype(F32)
            for i in range(D1):
                start = (r + i) * WIDE + c
                pad[start : start + D1] = corner[i * D1 : (i + 1) * D1]

    def spread(pad, cols, dilation):
        for b in range(3):
            first = 8 + (b - 1) * dilation
            for i in range(0, SIDE + 2 * dilation, 2):
                two = jnp.concatenate(
                    [pad[(i + h) * WIDE + first : (i + h) * WIDE + first + SIDE] for h in range(2)], axis=0
                )
                cols[i * SIDE : (i + 2) * SIDE, b * C : (b + 1) * C] = two.astype(BF16)

    same = lambda x: x
    relu = lambda x: jnp.maximum(x, 0.0)

    fill_centre(own_f, pad_a, D0, relu)
    weights_copy.wait_recv()
    for s in range(2):
        rolled[s] = pltpu.roll(weights[s, 0:CONV_ROWS].astype(F32), K, 1).astype(BF16)
    proj_diag[...] = jnp.zeros_like(proj_diag)
    proj_diag[0:K, 0:C] = weights[0, PROJ_ROW : PROJ_ROW + K]
    proj_diag[K : 2 * K, C : 2 * C] = weights[0, PROJ_ROW : PROJ_ROW + K]
    for s in range(2):
        for h in range(2):
            proj_twice[s, h * K : (h + 1) * K] = weights[s, PROJ_ROW : PROJ_ROW + K]
    tap = lambda a, b: slice((3 * a + b) * C, (3 * a + b + 1) * C)
    for a in range(3):
        for b in range(3):
            w0t[tap(a, b)] = rolled[0, tap(b, a)]
            w1cat[tap(a, b)] = weights[1, tap(a, b)] + rolled[1, tap(b, a)]
            lanes = slice(b * C, (b + 1) * C)
            back0[a, :, lanes] = weights[0, tap(2 - a, 2 - b)]
            back1[a, 0:C, lanes] = weights[1, tap(2 - a, 2 - b)]
            back1[a, C : 2 * C, lanes] = rolled[1, tap(2 - b, 2 - a)]

    mirror_wait(act_t, act_m, 0)
    turned_f[...] = act_m[...].astype(F32)
    pack_narrow((own_f, turned_f), send_e0, send_c0)
    sources0 = tuple(send_e0.at[k] for k in range(4)) + tuple(send_c0.at[k] for k in range(4))
    halo0 = (0, sources0, recv_e0, recv_c0)
    halo_start(*halo0)
    mirror_start(cot_t, cot_m, 1)
    fill_centre(turned_f, pad_b, D0, relu)
    halo_wait(*halo0)
    unpack_narrow(0, recv_e0, recv_c0, pad_a, relu)
    unpack_narrow(1, recv_e0, recv_c0, pad_b, relu)
    spread(pad_a, cols_a, D0)
    spread(pad_b, cols_b, D0)

    chunk = 192
    shift0 = D0 * SIDE
    shift1 = D1 * SIDE
    wide = 3 * C

    def rows_at(base, extra=0):
        return pl.ds(pl.multiple_of(base + extra, 16), chunk)

    bias0 = weights[0, BIAS_ROW : BIAS_ROW + 16].astype(F32)[0:1]
    bias1 = weights[1, BIAS_ROW : BIAS_ROW + 16].astype(F32)[0:1]

    @pl.loop(0, AREA // chunk)
    def _(i):
        base = i * chunk
        total = bias0
        for a in range(3):
            total = total + dot(cols_a[rows_at(base, a * shift0), :], weights[0, a * wide : (a + 1) * wide])
        for a in range(3):
            total = total + dot(cols_b[rows_at(base, a * shift0), :], w0t[a * wide : (a + 1) * wide])
        pre0[rows_at(base), :] = total
        bottle = jnp.maximum(total, 0.0).astype(BF16)
        bottle0[rows_at(base), :] = bottle
        both = dot(bottle, proj_diag[...])
        own = (own_f[rows_at(base), :] + both[:, 0:C]).astype(BF16).astype(F32)
        turned = (turned_f[rows_at(base), :] + both[:, C : 2 * C]).astype(BF16).astype(F32)
        sym = ((own + turned) * 0.5).astype(BF16)
        hidden1[rows_at(base), :] = jnp.maximum(sym, jnp.zeros_like(sym))

    turned_f[...] = hidden1[...].astype(F32)
    pack_wide(turned_f, hid_e, hid_c)
    halo1 = (1, wide_sources(hidden1, hid_e, hid_c), recv_e1, recv_c1)
    halo_start(*halo1)
    fill_centre(turned_f, pad_8, D1, same)
    mirror_wait(cot_t, cot_m, 1)

    @pl.loop(0, AREA // chunk)
    def _(i):
        at = rows_at(i * chunk)
        branch = ((cot[at, :].astype(F32) + cot_m[at, :].astype(F32)) * 0.5).astype(BF16)
        branch1[at, :] = branch
        grad_bot[at, :] = dot(branch, proj_twice[1], NT)

    halo_wait(*halo1)
    unpack_wide(recv_e1, recv_c1, pad_8)
    spread(pad_8, cols_8, D1)

    @pl.loop(0, AREA // chunk)
    def _(i):
        base = i * chunk
        total = bias1
        for a in range(3):
            total = total + dot(cols_8[rows_at(base, a * shift1), :], w1cat[a * wide : (a + 1) * wide])
        bottle1[rows_at(base), :] = jnp.maximum(total, 0.0).astype(BF16)
        grad = jnp.where(total > 0, grad_bot[rows_at(base), :], 0.0)
        turned_f[rows_at(base), :] = grad
        gp1[rows_at(base), :] = grad.astype(BF16)

    pack_wide(turned_f, gp1_e, gp1_c)
    halo2 = (2, wide_sources(gp1, gp1_e, gp1_c), recv_e2, recv_c2)
    halo_start(*halo2)
    fill_centre(turned_f, pad_8, D1, lambda x: x)

    ones = jnp.ones((AREA, C), BF16)

    def weight_gradients(s, grad_pre, cols, shift, bottle, branch):
        for a in range(3):
            product = dot(grad_pre[...], cols[a * shift : a * shift + AREA, :], TN)
            for b in range(3):
                at = (3 * a + b) * K
                grads[s, at : at + K] = product[0:K, b * C : (b + 1) * C].astype(BF16)
        grads[s, 9 * K : 10 * K] = dot(bottle[...], branch[...], TN)[0:K].astype(BF16)
        grads[s, 10 * K : 11 * K] = dot(grad_pre[...], ones, TN)[0:K].astype(BF16)
        grads[s, 11 * K : 12 * K] = jnp.zeros((K, C), BF16)

    weight_gradients(1, gp1, cols_8, shift1, bottle1, branch1)
    halo_wait(*halo2)
    unpack_wide(recv_e2, recv_c2, pad_8)
    spread(pad_8, cols_g, D1)

    @pl.loop(0, AREA // chunk)
    def _(i):
        base = i * chunk
        total = None
        for a in range(3):
            term = dot(cols_g[rows_at(base, a * shift1), :], back1[a], NT)
            total = term if total is None else total + term
        branch = branch1[rows_at(base), :].astype(F32)
        live = hidden1[rows_at(base), :].astype(F32) > 0
        own = (branch + jnp.where(live, total[:, 0:C], 0.0)).astype(BF16).astype(F32)
        turned = (branch + jnp.where(live, total[:, C : 2 * C], 0.0)).astype(BF16).astype(F32)
        mean = ((own + turned) * 0.5).astype(BF16)
        branch0[rows_at(base), :] = mean
        grad = jnp.where(pre0[rows_at(base), :] > 0, dot(mean, proj_twice[0], NT), 0.0)
        turned_f[rows_at(base), :] = grad
        gp0[rows_at(base), :] = grad.astype(BF16)

    pack_narrow((turned_f,), gp0_e, gp0_c)
    sources3 = tuple(gp0_e.at[k] for k in range(4)) + tuple(gp0_c.at[k] for k in range(4))
    halo3 = (3, sources3, recv_e3, recv_c3)
    halo_start(*halo3)
    weight_gradients(0, gp0, cols_a, shift0, bottle0, branch0)

    grads_copy = sibling_copy(grads.at[1 - seg], grads_recv, 3)
    grads_copy.start()
    fill_centre(turned_f, pad_a, D0, same)
    grads_copy.wait_recv()
    acc_send[...] = (grads[seg].astype(F32) + grads_recv[...].astype(F32)).astype(BF16)

    def piece_at(index):
        return pl.ds(pl.multiple_of(index * piece, 16), piece)

    def group_copy(step, me, peer, src, dst, send_sem, recv_sem, index):
        return pltpu.make_async_remote_copy(
            src_ref=src,
            dst_ref=dst.at[index],
            send_sem=send_sem.at[step],
            recv_sem=recv_sem.at[index],
            device_id=peer,
            device_id_type=MESH,
        )

    def plane_copy(step):
        to = (plane_me + step) % n
        return group_copy(
            step, plane_me, plane_peer(to), acc_send.at[piece_at(to)], plane_recv, plane_send_sem, plane_recv_sem, plane_me
        )

    def line_copy(step):
        to = (line_me + step) % n
        return group_copy(
            step, line_me, line_peer(to), line_recv.at[line_me], line_recv, line_send_sem, line_recv_sem, line_me
        )

    def all_copy(step):
        to = (plane_me + step) % n
        return group_copy(
            step, plane_me, plane_peer(to), total_recv.at[plane_me], total_recv, all_send_sem, all_recv_sem, plane_me
        )

    def arrivals(me, peer, dst, send_sem, recv_sem):
        @pl.loop(1, n)
        def _(step):
            index = (me + step) % n
            group_copy(step, me, peer(index), dst.at[index], dst, send_sem, recv_sem, index).wait_recv()

    def add_up(buffer):
        total = buffer[0].astype(F32)
        for i in range(1, n):
            total = total + buffer[i].astype(F32)
        return total

    pl.loop(1, n)(lambda step: plane_copy(step).start())
    plane_recv[plane_me] = acc_send[piece_at(plane_me), :]

    halo_wait(*halo3)
    unpack_narrow(0, recv_e3, recv_c3, pad_a, same)
    spread(pad_a, cols_b, D0)

    @pl.loop(0, AREA // chunk)
    def _(i):
        base = i * chunk
        total = None
        for a in range(3):
            term = dot(cols_b[rows_at(base, a * shift0), :], back0[a], NT)
            total = term if total is None else total + term
        branch = branch0[rows_at(base), :].astype(F32)
        live = own_f[rows_at(base), :] > 0
        out_grad[rows_at(base), :] = (branch + jnp.where(live, total, 0.0)).astype(BF16)

    arrivals(plane_me, plane_peer, plane_recv, plane_send_sem, plane_recv_sem)
    line_recv[line_me] = add_up(plane_recv).astype(BF16)
    pl.loop(1, n)(lambda step: line_copy(step).start())
    arrivals(line_me, line_peer, line_recv, line_send_sem, line_recv_sem)
    total_recv[plane_me] = add_up(line_recv).astype(BF16)
    pl.loop(1, n)(lambda step: all_copy(step).start())

    pl.when(off_diagonal)(lambda: mirror_copy(act_t, act_m, 0).wait_send())
    pl.when(off_diagonal)(lambda: mirror_copy(cot_t, cot_m, 1).wait_send())
    weights_copy.wait_send()
    grads_copy.wait_send()
    for halo in (halo0, halo1, halo2, halo3):
        halo_sent(*halo)
    pl.loop(1, n)(lambda step: plane_copy(step).wait_send())
    pl.loop(1, n)(lambda step: line_copy(step).wait_send())

    arrivals(plane_me, plane_peer, total_recv, all_send_sem, all_recv_sem)
    for i in range(n):
        stage_f[i * piece : (i + 1) * piece] = total_recv[i].astype(F32) * factor
    for t in range(9):
        out_conv[t * C : (t + 1) * C] = stage_f[t * K : (t + 1) * K].T
    out_proj[...] = stage_f[9 * K : 10 * K]
    out_bias[...] = stage_f[10 * K : 11 * K].T[0:8]
    pl.loop(1, n)(lambda step: all_copy(step).wait_send())


def solution(mesh):
    n = mesh.shape["row"]
    cells = mesh.shape["segment"] * (SIDE * n) * (SIDE * n)
    factor = float(np.float32(1.0) / np.sqrt(np.float32(cells)))
    piece = GRAD_ROWS // n
    vmem = pltpu.VMEM
    scratch = [
        vmem((2, PACK_ROWS, 128), BF16),
        vmem((2, CONV_ROWS, 128), BF16),
        vmem((CONV_ROWS, 128), BF16),
        vmem((CONV_ROWS, 128), BF16),
        vmem((3, 2 * C, 3 * C), BF16),
        vmem((3, C, 3 * C), BF16),
        vmem((2 * K, 2 * C), BF16),
        vmem((2, 2 * K, C), BF16),
        vmem((AREA, C), F32),
        vmem((AREA, C), F32),
        vmem((GRAD_ROWS, C), F32),
        vmem((AREA, C), BF16),
        vmem((AREA, C), BF16),
        vmem((AREA, C), BF16),
        vmem((AREA, C), BF16),
        vmem((4, 2 * D0 * SIDE, C), BF16),
        vmem((4, 16, C), BF16),
        vmem((4, 2 * D0 * SIDE, C), BF16),
        vmem((4, 16, C), BF16),
        vmem((AREA, C), BF16),
        vmem((2, D1 * SIDE, C), BF16),
        vmem((4, D1 * D1, C), BF16),
        vmem((4, D1 * SIDE, C), BF16),
        vmem((4, D1 * D1, C), BF16),
        vmem((AREA, C), BF16),
        vmem((2, D1 * SIDE, C), BF16),
        vmem((4, D1 * D1, C), BF16),
        vmem((4, D1 * SIDE, C), BF16),
        vmem((4, D1 * D1, C), BF16),
        vmem((AREA, C), BF16),
        vmem((4, D0 * SIDE, C), BF16),
        vmem((4, 16, C), BF16),
        vmem((4, D0 * SIDE, C), BF16),
        vmem((4, 16, C), BF16),
        vmem(((SIDE + 2 * D0) * WIDE, C), F32),
        vmem(((SIDE + 2 * D0) * WIDE, C), F32),
        vmem(((SIDE + 2 * D1) * WIDE, C), F32),
        vmem(((SIDE + 2 * D0) * SIDE, 3 * C), BF16),
        vmem(((SIDE + 2 * D0) * SIDE, 3 * C), BF16),
        vmem(((SIDE + 2 * D1) * SIDE, 3 * C), BF16),
        vmem(((SIDE + 2 * D1) * SIDE, 3 * C), BF16),
        vmem((AREA, C), F32),
        vmem((AREA, C), BF16),
        vmem((AREA, C), F32),
        vmem((AREA, C), BF16),
        vmem((AREA, C), BF16),
        vmem((AREA, C), BF16),
        vmem((2, GRAD_ROWS, C), BF16),
        vmem((16, C), BF16),
        vmem((GRAD_ROWS, C), BF16),
        vmem((GRAD_ROWS, C), BF16),
        vmem((n, piece, C), BF16),
        vmem((n, piece, C), BF16),
        vmem((n, piece, C), BF16),
        pltpu.SemaphoreType.DMA((4, 8)),
        pltpu.SemaphoreType.DMA((4, 8)),
        pltpu.SemaphoreType.DMA((4,)),
        pltpu.SemaphoreType.DMA((4,)),
    ] + [pltpu.SemaphoreType.DMA((n,))] * 6

    call = pl.pallas_call(
        functools.partial(kernel, n, factor),
        out_shape=(
            jax.ShapeDtypeStruct((AREA, C), BF16),
            jax.ShapeDtypeStruct((CONV_ROWS, K), F32),
            jax.ShapeDtypeStruct((8, K), F32),
            jax.ShapeDtypeStruct((K, C), F32),
        ),
        in_specs=[pl.BlockSpec(memory_space=pltpu.VMEM)] * 5,
        out_specs=[pl.BlockSpec(memory_space=pltpu.VMEM)] * 4,
        scratch_shapes=scratch,
        compiler_params=pltpu.CompilerParams(
            collective_id=0, has_side_effects=True, vmem_limit_bytes=40 * 1024 * 1024
        ),
        name="trunk",
    )

    def local(activations, cotangent, conv_weight, conv_bias, out_weight):
        grad, conv, bias, proj = call(
            activations.reshape(AREA, C),
            cotangent.reshape(AREA, C),
            conv_weight.reshape(CONV_ROWS, K),
            conv_bias,
            out_weight.reshape(K, C),
        )
        return (
            grad.reshape(1, SIDE, SIDE, C),
            conv.reshape(1, 9, C, K),
            bias[0:1],
            proj.reshape(1, K, C),
        )

    in_specs = (
        P("segment", "row", "col", None),
        P("segment", "row", "col", None),
        P("segment", None, None, None),
        P("segment", None),
        P("segment", None, None),
    )
    out_specs = (
        P("segment", "row", "col", None),
        P("segment", None, None, None),
        P("segment", None),
        P("segment", None, None),
    )
    return jax.shard_map(local, mesh=mesh, in_specs=in_specs, out_specs=out_specs, check_vma=False)
```

```python
import functools

import numpy as np

import jax
import jax.numpy as jnp
from jax import lax
from jax.experimental import pallas as pl
from jax.experimental.pallas import tpu as pltpu
from jax.sharding import PartitionSpec as P

MESH = pl.DeviceIdType.MESH
F32 = jnp.float32
BF16 = jnp.bfloat16

SIDE = 24
AREA = SIDE * SIDE
C = 128
K = 64
D0 = 2
D1 = 8
WIDE = 40
CONV_ROWS = 9 * K
PROJ_ROW = CONV_ROWS
BIAS_ROW = CONV_ROWS + K
PACK_ROWS = CONV_ROWS + K + 16
GRAD_BLOCKS = 12
GRAD_ROWS = GRAD_BLOCKS * K
DIRECTIONS = ((-1, 0), (1, 0), (0, -1), (0, 1), (-1, -1), (-1, 1), (1, -1), (1, 1))
OPPOSITE = (1, 0, 3, 2, 7, 6, 5, 4)
NT = (((1,), (1,)), ((), ()))
TN = (((0,), (0,)), ((), ()))


def dot(a, b, dims=(((1,), (0,)), ((), ()))):
    return lax.dot_general(a, b, dims, preferred_element_type=F32)


def kernel(
    n,
    factor,
    act_in,
    cot_in,
    conv_in,
    bias_in,
    proj_in,
    out_grad,
    out_conv,
    out_bias,
    out_proj,
    act,
    cot,
    bias_w,
    weights,
    first,
    second,
    back1,
    back0,
    proj_pad,
    proj_twice,
    own_f,
    work_f,
    stage_f,
    sum_t,
    cot_t,
    sum_m,
    cot_m,
    send_e0,
    send_c0,
    recv_e0,
    recv_c0,
    hidden1,
    hid_e,
    hid_c,
    recv_e1,
    recv_c1,
    gp1,
    gp1_e,
    gp1_c,
    recv_e2,
    recv_c2,
    gp0,
    gp0_e,
    gp0_c,
    recv_e3,
    recv_c3,
    pad_a,
    pad_8,
    pad_9,
    cols_a,
    cols_b,
    cols_8,
    cols_g,
    pre0,
    bottle0,
    grad_bot,
    bottle1,
    branch1,
    branch0,
    grads,
    plane_recv,
    line_recv,
    total_recv,
    halo_send,
    halo_recv,
    pair_send,
    pair_recv,
    plane_send_sem,
    plane_recv_sem,
    line_send_sem,
    line_recv_sem,
    all_send_sem,
    all_recv_sem,
    greeting,
    partner,
    input_sem,
):
    seg = lax.axis_index("segment")
    row = lax.axis_index("row")
    col = lax.axis_index("col")
    part = int(round(n**0.5))
    piece = GRAD_ROWS // n
    row_hi, row_lo = row // part, row % part
    col_hi, col_lo = col // part, col % part
    plane_me = row_lo * part + col_lo
    line_me = row_hi * part + col_hi
    off_diagonal = row != col
    mirror = (seg, col, row)
    sibling = (1 - seg, row, col)

    def plane_peer(section, index):
        return (section, row_hi * part + index // part, col_hi * part + index % part)

    def line_peer(index):
        return (seg, (index // part) * part + row_lo, (index % part) * part + col_lo)

    def row_peer(step):
        return (seg, ((row_hi + step) % part) * part + row_lo, col)

    def col_peer(step):
        return (seg, row, ((col_hi + step) % part) * part + col_lo)

    def there(k):
        dr, dc = DIRECTIONS[k]
        r, c = row + dr, col + dc
        exists = None
        if dr:
            exists = (r >= 0) if dr < 0 else (r < n)
        if dc:
            side = (c >= 0) if dc < 0 else (c < n)
            exists = side if exists is None else jnp.logical_and(exists, side)
        return exists

    def neighbour(k):
        dr, dc = DIRECTIONS[k]
        return (seg, row + dr, col + dc)

    inputs = [
        pltpu.make_async_copy(src, dst, input_sem.at[i])
        for i, (src, dst) in enumerate(
            (
                (act_in, act),
                (cot_in, cot),
                (conv_in, weights.at[seg, 0:CONV_ROWS]),
                (proj_in, weights.at[seg, PROJ_ROW : PROJ_ROW + K]),
                (bias_in, bias_w),
            )
        )
    ]
    for copy in inputs:
        copy.start()
    barrier = pltpu.get_barrier_semaphore()

    def signal(device):
        pl.semaphore_signal(barrier, inc=1, device_id=device, device_id_type=MESH)

    greeted = jnp.int32(1 + 2 * (part - 1))
    pl.when(off_diagonal)(functools.partial(signal, mirror))
    greeted = greeted + off_diagonal.astype(jnp.int32)
    for step in range(1, part):
        signal(col_peer(step))
        signal(row_peer(step))
    for k in range(7, -1, -1):
        pl.when(there(k))(functools.partial(signal, neighbour(k)))
        greeted = greeted + there(k).astype(jnp.int32)
    signal(sibling)

    def turn(flat, out):
        @pl.loop(0, SIDE // 2)
        def _(i):
            two = jnp.concatenate(
                [flat[pl.ds(2 * i, SIDE, stride=SIDE), :], flat[pl.ds(2 * i + 1, SIDE, stride=SIDE), :]], axis=0
            )
            out[pl.ds(pl.multiple_of(i * 2 * SIDE, 16), 2 * SIDE), :] = two.astype(BF16)

    strip = D0 * SIDE
    corners_of_tile = ((0, 0), (0, SIDE - D0), (SIDE - D0, 0), (SIDE - D0, SIDE - D0))

    def pack_corners(tile, corners):
        for k, (r, c) in enumerate(corners_of_tile):
            stage_f[...] = jnp.zeros((16, C), F32)
            for i in range(D0):
                start = (r + i) * SIDE + c
                stage_f[i * D0 : (i + 1) * D0] = tile[start : start + D0]
            corners[k] = stage_f[...].astype(BF16)

    def pack_narrow(tile, edges, corners):
        edges[0] = tile[0:strip].astype(BF16)
        edges[1] = tile[AREA - strip : AREA].astype(BF16)
        for k, first_column in ((2, 0), (3, SIDE - D0)):
            columns = [tile[pl.ds(first_column + j, SIDE, stride=SIDE), :] for j in range(D0)]
            edges[k] = jnp.concatenate(columns, axis=0).astype(BF16)
        pack_corners(tile, corners)

    for copy in inputs:
        copy.wait()
    own_f[...] = act[...].astype(F32)
    pack_narrow(own_f, send_e0, send_c0)
    bias_row = bias_w[...].astype(F32)
    weights[seg, BIAS_ROW : BIAS_ROW + 16] = jnp.broadcast_to(
        jnp.concatenate([bias_row, bias_row], axis=1), (16, 2 * K)
    ).astype(BF16)
    work_f[...] = cot[...].astype(F32)
    turn(work_f, cot_t)

    pl.semaphore_wait(barrier, greeted)

    def pair_copy(src, dst, index, device):
        return pltpu.make_async_remote_copy(
            src_ref=src,
            dst_ref=dst,
            send_sem=pair_send.at[index],
            recv_sem=pair_recv.at[index],
            device_id=device,
            device_id_type=MESH,
        )

    def mirror_copy(src, dst, index):
        return pair_copy(src, dst, index, mirror)

    def mirror_start(src, dst, index):
        @pl.when(off_diagonal)
        def _():
            mirror_copy(src, dst, index).start()

        @pl.when(jnp.logical_not(off_diagonal))
        def _():
            dst[...] = src[...]

    def mirror_wait(src, dst, index):
        pl.when(off_diagonal)(lambda: mirror_copy(src, dst, index).wait_recv())

    def halo_to(phase, k, slot, device, sources, edges, corners):
        return pltpu.make_async_remote_copy(
            src_ref=sources[k],
            dst_ref=edges.at[slot] if slot < 4 else corners.at[slot - 4],
            send_sem=halo_send.at[phase, k],
            recv_sem=halo_recv.at[phase, slot],
            device_id=device,
            device_id_type=MESH,
        )

    def halo_copy(phase, k, sources, edges, corners):
        return halo_to(phase, k, OPPOSITE[k], neighbour(k), sources, edges, corners)

    def halo_start(*halo):
        for k in range(7, -1, -1):
            pl.when(there(k))(lambda k=k: halo_copy(halo[0], k, *halo[1:]).start())

    def halo_clear(phase, sources, edges, corners):
        for k in range(8):

            @pl.when(jnp.logical_not(there(k)))
            def _():
                ref = edges.at[k] if k < 4 else corners.at[k - 4]
                ref[...] = jnp.zeros_like(ref)

    def arrived(phase, k, edges, corners):
        target = edges.at[k] if k < 4 else corners.at[k - 4]
        return pltpu.make_async_remote_copy(
            src_ref=target,
            dst_ref=target,
            send_sem=halo_send.at[phase, k],
            recv_sem=halo_recv.at[phase, k],
            device_id=neighbour(k),
            device_id_type=MESH,
        )

    def halo_wait(phase, sources, edges, corners):
        for k in range(8):
            pl.when(there(k))(lambda k=k: arrived(phase, k, edges, corners).wait_recv())

    def halo_sent(*halo):
        for k in range(8):
            pl.when(there(k))(lambda k=k: halo_copy(halo[0], k, *halo[1:]).wait_send())

    sources0 = tuple(send_e0.at[k] for k in range(4)) + tuple(send_c0.at[k] for k in range(4))
    halo0 = (0, sources0, recv_e0, recv_c0)
    halo_start(*halo0)
    weights_copy = pair_copy(weights.at[seg], weights.at[seg], 2, sibling)
    weights_copy.start()
    mirror_start(cot_t, cot_m, 1)
    for step in range(1, part):
        pl.semaphore_signal(greeting, inc=1, device_id=row_peer(step), device_id_type=MESH)

    halo_clear(*halo0)
    halo_clear(1, None, recv_e1, recv_c1)
    halo_clear(2, None, recv_e2, recv_c2)
    halo_clear(3, None, recv_e3, recv_c3)

    def unpack_narrow(edges, corners, pad, change):
        north = change(edges[0].astype(F32))
        south = change(edges[1].astype(F32))
        west = change(edges[2].astype(F32))
        east = change(edges[3].astype(F32))
        for i in range(D0):
            lines = slice(i * SIDE, (i + 1) * SIDE)
            pad[i * WIDE + 8 : i * WIDE + 8 + SIDE] = north[lines]
            low = (D0 + SIDE + i) * WIDE + 8
            pad[low : low + SIDE] = south[lines]
            pad[pl.ds(D0 * WIDE + 8 - D0 + i, SIDE, stride=WIDE), :] = west[lines]
            pad[pl.ds(D0 * WIDE + 8 + SIDE + i, SIDE, stride=WIDE), :] = east[lines]
        for k, (r, c) in enumerate(((0, 8 - D0), (0, 8 + SIDE), (D0 + SIDE, 8 - D0), (D0 + SIDE, 8 + SIDE))):
            stage_f[...] = change(corners[k].astype(F32))
            for i in range(D0):
                start = (r + i) * WIDE + c
                pad[start : start + D0] = stage_f[i * D0 : (i + 1) * D0]

    def fill_centre(tile, pad, dilation, change):
        for i in range(SIDE):
            start = (dilation + i) * WIDE + 8
            pad[start : start + SIDE] = change(tile[i * SIDE : (i + 1) * SIDE])

    def pack_wide(tile, edges, corners):
        for k, first in ((0, 0), (1, SIDE - D1)):
            edges[k] = jnp.concatenate(
                [tile[i * SIDE + first : i * SIDE + first + D1] for i in range(SIDE)], axis=0
            ).astype(BF16)
        for k, (r, c) in enumerate(((0, 0), (0, SIDE - D1), (SIDE - D1, 0), (SIDE - D1, SIDE - D1))):
            corners[k] = jnp.concatenate(
                [tile[(r + i) * SIDE + c : (r + i) * SIDE + c + D1] for i in range(D1)], axis=0
            ).astype(BF16)

    def wide_sources(flat, edges, corners):
        lines = D1 * SIDE
        return (
            flat.at[0:lines],
            flat.at[AREA - lines : AREA],
            edges.at[0],
            edges.at[1],
        ) + tuple(corners.at[k] for k in range(4))

    def unpack_wide(edges, corners, pad):
        north = edges[0].astype(F32)
        south = edges[1].astype(F32)
        west = edges[2].astype(F32)
        east = edges[3].astype(F32)
        for i in range(D1):
            lines = slice(i * SIDE, (i + 1) * SIDE)
            pad[i * WIDE + D1 : i * WIDE + D1 + SIDE] = north[lines]
            low = (D1 + SIDE + i) * WIDE + D1
            pad[low : low + SIDE] = south[lines]
        for i in range(SIDE):
            lines = slice(i * D1, (i + 1) * D1)
            start = (D1 + i) * WIDE
            pad[start : start + D1] = west[lines]
            pad[start + D1 + SIDE : start + WIDE] = east[lines]
        for k, (r, c) in enumerate(((0, 0), (0, D1 + SIDE), (D1 + SIDE, 0), (D1 + SIDE, D1 + SIDE))):
            corner = corners[k].astype(F32)
            for i in range(D1):
                start = (r + i) * WIDE + c
                pad[start : start + D1] = corner[i * D1 : (i + 1) * D1]

    def spread(pad, cols, dilation):
        for b in range(3):
            first = 8 + (b - 1) * dilation
            for i in range(0, SIDE + 2 * dilation, 2):
                two = jnp.concatenate(
                    [pad[(i + h) * WIDE + first : (i + h) * WIDE + first + SIDE] for h in range(2)], axis=0
                )
                cols[i * SIDE : (i + 2) * SIDE, b * C : (b + 1) * C] = two.astype(BF16)

    same = lambda x: x
    relu = lambda x: jnp.maximum(x, 0.0)

    fill_centre(own_f, pad_a, D0, relu)
    for ref in (first, back1, back0, proj_pad):
        ref[...] = jnp.zeros_like(ref)
    weights_copy.wait_recv()

    proj_pad[0:K] = weights[0, PROJ_ROW : PROJ_ROW + K]
    for s in range(2):
        for h in range(2):
            proj_twice[s, h * K : (h + 1) * K] = weights[s, PROJ_ROW : PROJ_ROW + K]
    tap = lambda a, b: slice((3 * a + b) * K, (3 * a + b + 1) * K)
    for a in range(3):
        for b in range(3):
            lanes = slice(b * C, (b + 1) * C)
            own, turned = slice(b * C, b * C + K), slice(b * C + K, (b + 1) * C)
            first[a, 0:K, lanes] = weights[0, tap(a, b)]
            second[a, 0:K, lanes] = weights[1, tap(a, b)]
            second[a, K : 2 * K, lanes] = weights[1, tap(b, a)]
            back0[a, own] = weights[0, tap(2 - a, 2 - b)]
            back1[a, own, 0:C] = weights[1, tap(2 - a, 2 - b)]
            back1[a, turned, C : 2 * C] = weights[1, tap(2 - b, 2 - a)]

    halo_wait(*halo0)
    unpack_narrow(recv_e0, recv_c0, pad_a, relu)
    spread(pad_a, cols_a, D0)

    chunk = 192
    shift0 = D0 * SIDE
    shift1 = D1 * SIDE

    def rows_at(base, extra=0):
        return pl.ds(pl.multiple_of(base + extra, 16), chunk)

    bias0 = weights[0, BIAS_ROW : BIAS_ROW + 16].astype(F32)[0:1]
    bias1 = weights[1, BIAS_ROW : BIAS_ROW + 16].astype(F32)[0:1]

    @pl.loop(0, AREA // chunk)
    def _(i):
        base = i * chunk
        total = bias0
        for a in range(3):
            total = total + dot(cols_a[rows_at(base, a * shift0), :], first[a], NT)
        pre0[rows_at(base), :] = total
        bottle = jnp.maximum(total, 0.0).astype(BF16)
        bottle0[rows_at(base), :] = bottle
        branch_sum = (own_f[rows_at(base), :] + dot(bottle, proj_pad[...])).astype(BF16)
        work_f[rows_at(base), :] = branch_sum.astype(F32)

    turn(work_f, sum_t)
    mirror_start(sum_t, sum_m, 0)

    mirror_wait(cot_t, cot_m, 1)

    @pl.loop(0, AREA // chunk)
    def _(i):
        at = rows_at(i * chunk)
        branch = ((cot[at, :].astype(F32) + cot_m[at, :].astype(F32)) * 0.5).astype(BF16)
        branch1[at, :] = branch
        grad_bot[at, :] = dot(branch, proj_twice[1], NT)

    mirror_wait(sum_t, sum_m, 0)

    @pl.loop(0, AREA // chunk)
    def _(i):
        at = rows_at(i * chunk)
        sym = ((work_f[at, :] + sum_m[at, :].astype(F32)) * 0.5).astype(BF16)
        live = jnp.maximum(sym, jnp.zeros_like(sym))
        hidden1[at, :] = live
        work_f[at, :] = live.astype(F32)

    pack_wide(work_f, hid_e, hid_c)
    halo1 = (1, wide_sources(hidden1, hid_e, hid_c), recv_e1, recv_c1)
    halo_start(*halo1)
    fill_centre(work_f, pad_8, D1, same)

    halo_wait(*halo1)

    pl.semaphore_signal(partner, inc=1, device_id=sibling, device_id_type=MESH)

    unpack_wide(recv_e1, recv_c1, pad_8)
    spread(pad_8, cols_8, D1)

    @pl.loop(0, AREA // chunk)
    def _(i):
        base = i * chunk
        total = bias1
        for a in range(3):
            total = total + dot(cols_8[rows_at(base, a * shift1), :], second[a], NT)
        bottle1[rows_at(base), :] = jnp.maximum(total, 0.0).astype(BF16)
        grad = jnp.where(total > 0, grad_bot[rows_at(base), :], 0.0)
        work_f[rows_at(base), :] = grad
        gp1[rows_at(base), :] = grad.astype(BF16)

    pack_wide(work_f, gp1_e, gp1_c)
    halo2 = (2, wide_sources(gp1, gp1_e, gp1_c), recv_e2, recv_c2)
    halo_start(*halo2)

    ones = jnp.ones((AREA, C), BF16)

    def weight_gradients(s, grad_pre, cols, shift, bottle, branch):
        turned_grad = grad_pre[...].T[0:K]
        for a in range(3):
            product = dot(turned_grad, cols[a * shift : a * shift + AREA, :])
            for b in range(3):
                at = (3 * a + b) * K
                grads[s, at : at + K] = product[:, b * C : (b + 1) * C].astype(BF16)
        grads[s, 9 * K : 10 * K] = dot(bottle[...].T[0:K], branch[...]).astype(BF16)
        grads[s, 10 * K : 11 * K] = dot(turned_grad, ones).astype(BF16)
        grads[s, 11 * K : 12 * K] = jnp.zeros((K, C), BF16)

    def piece_at(index):
        return pl.ds(pl.multiple_of(index * piece, 16), piece)

    slot_me = seg * n + plane_me

    def group_copy(src, dst, send_sem, recv_sem, device):
        return pltpu.make_async_remote_copy(
            src_ref=src, dst_ref=dst, send_sem=send_sem, recv_sem=recv_sem, device_id=device, device_id_type=MESH
        )

    def plane_copy(s, step):
        to = (plane_me + step) % n
        return group_copy(
            grads.at[s, piece_at(to)],
            plane_recv.at[slot_me],
            plane_send_sem.at[s, step],
            plane_recv_sem.at[slot_me],
            plane_peer(s, to),
        )

    def plane_start(s):
        @pl.when(seg != s)
        def _():
            plane_copy(s, 0).start()

        pl.loop(1, n)(lambda step: plane_copy(s, step).start())

        @pl.when(seg == s)
        def _():
            plane_recv[slot_me] = grads[s, piece_at(plane_me), :]

    def plane_sent(s):
        @pl.when(seg != s)
        def _():
            plane_copy(s, 0).wait_send()

        pl.loop(1, n)(lambda step: plane_copy(s, step).wait_send())

    def plane_wait():
        @pl.loop(1, 2 * n)
        def _(step):
            slot = (slot_me + step) % (2 * n)
            group_copy(
                plane_recv.at[slot], plane_recv.at[slot], plane_send_sem.at[0, 0], plane_recv_sem.at[slot], sibling
            ).wait_recv()

    def line_copy(step):
        to = (line_me + step) % n
        return group_copy(
            line_recv.at[line_me], line_recv.at[line_me], line_send_sem.at[step], line_recv_sem.at[line_me], line_peer(to)
        )

    def all_copy(step):
        to = (plane_me + step) % n
        return group_copy(
            total_recv.at[plane_me],
            total_recv.at[plane_me],
            all_send_sem.at[step],
            all_recv_sem.at[plane_me],
            plane_peer(seg, to),
        )

    def arrivals(me, dst, send_sem, recv_sem):
        @pl.loop(1, n)
        def _(step):
            index = (me + step) % n
            group_copy(dst.at[index], dst.at[index], send_sem.at[step], recv_sem.at[index], sibling).wait_recv()

    def add_up(buffer, count):
        total = buffer[0].astype(F32)
        for i in range(1, count):
            total = total + buffer[i].astype(F32)
        return total

    def line_start():
        plane_wait()
        line_recv[line_me] = add_up(plane_recv, 2 * n).astype(BF16)
        pl.loop(1, n)(lambda step: line_copy(step).start())

    weight_gradients(1, gp1, cols_8, shift1, bottle1, branch1)
    pl.semaphore_wait(partner, 1)
    plane_start(1)
    fill_centre(work_f, pad_9, D1, same)
    pl.semaphore_wait(greeting, part - 1)

    halo_wait(*halo2)

    unpack_wide(recv_e2, recv_c2, pad_9)
    spread(pad_9, cols_g, D1)

    @pl.loop(0, AREA // chunk)
    def _(i):
        base = i * chunk
        total = None
        for a in range(3):
            term = dot(cols_g[rows_at(base, a * shift1), :], back1[a])
            total = term if total is None else total + term
        branch = branch1[rows_at(base), :].astype(F32)
        live = hidden1[rows_at(base), :].astype(F32) > 0
        own = (branch + jnp.where(live, total[:, 0:C], 0.0)).astype(BF16).astype(F32)
        turned = (branch + jnp.where(live, total[:, C : 2 * C], 0.0)).astype(BF16).astype(F32)
        mean = ((own + turned) * 0.5).astype(BF16)
        branch0[rows_at(base), :] = mean
        grad = jnp.where(pre0[rows_at(base), :] > 0, dot(mean, proj_twice[0], NT), 0.0)
        work_f[rows_at(base), :] = grad
        gp0[rows_at(base), :] = grad.astype(BF16)

    weight_gradients(0, gp0, cols_a, shift0, bottle0, branch0)

    plane_start(0)

    pack_narrow(work_f, gp0_e, gp0_c)
    sources3 = tuple(gp0_e.at[k] for k in range(4)) + tuple(gp0_c.at[k] for k in range(4))
    halo3 = (3, sources3, recv_e3, recv_c3)
    halo_start(*halo3)
    fill_centre(work_f, pad_a, D0, same)

    line_start()

    halo_wait(*halo3)

    unpack_narrow(recv_e3, recv_c3, pad_a, same)
    spread(pad_a, cols_b, D0)

    @pl.loop(0, AREA // chunk)
    def _(i):
        base = i * chunk
        total = None
        for a in range(3):
            term = dot(cols_b[rows_at(base, a * shift0), :], back0[a])
            total = term if total is None else total + term
        branch = branch0[rows_at(base), :].astype(F32)
        live = own_f[rows_at(base), :] > 0
        out_grad[rows_at(base), :] = (branch + jnp.where(live, total, 0.0)).astype(BF16)

    pl.when(off_diagonal)(lambda: mirror_copy(sum_t, sum_m, 0).wait_send())
    pl.when(off_diagonal)(lambda: mirror_copy(cot_t, cot_m, 1).wait_send())
    weights_copy.wait_send()
    for halo in (halo0, halo1, halo2, halo3):
        halo_sent(*halo)
    plane_sent(0)
    plane_sent(1)

    arrivals(line_me, line_recv, line_send_sem, line_recv_sem)

    total_recv[plane_me] = add_up(line_recv, n).astype(BF16)
    pl.loop(1, n)(lambda step: all_copy(step).start())
    pl.loop(1, n)(lambda step: line_copy(step).wait_send())

    arrivals(plane_me, total_recv, all_send_sem, all_recv_sem)

    for i in range(n):
        values = total_recv[i].astype(F32) * factor
        if piece <= K and (i + 1) * piece <= CONV_ROWS:
            out_conv[i * piece : (i + 1) * piece] = values
        else:
            for first, last, out in ((0, CONV_ROWS, out_conv), (9 * K, 10 * K, out_proj), (10 * K, 11 * K, None)):
                low, high = max(first, i * piece), min(last, (i + 1) * piece)
                if low < high:
                    block = values[low - i * piece : high - i * piece]
                    if out is None:
                        work_f[low - first : high - first] = block
                    else:
                        out[low - first : high - first] = block
    out_bias[...] = work_f[0:K].T[0:1]
    pl.loop(1, n)(lambda step: all_copy(step).wait_send())


def solution(mesh):
    n = mesh.shape["row"]
    cells = mesh.shape["segment"] * (SIDE * n) * (SIDE * n)
    factor = float(np.float32(1.0) / np.sqrt(np.float32(cells)))
    piece = GRAD_ROWS // n
    vmem = pltpu.VMEM
    scratch = [
        vmem((AREA, C), BF16),
        vmem((AREA, C), BF16),
        vmem((1, K), BF16),
        vmem((2, PACK_ROWS, C), BF16),
        vmem((3, 2 * K, 3 * C), BF16),
        vmem((3, 2 * K, 3 * C), BF16),
        vmem((3, 3 * C, 2 * C), BF16),
        vmem((3, 3 * C, C), BF16),
        vmem((2 * K, C), BF16),
        vmem((2, 2 * K, C), BF16),
        vmem((AREA, C), F32),
        vmem((AREA, C), F32),
        vmem((16, C), F32),
        vmem((AREA, C), BF16),
        vmem((AREA, C), BF16),
        vmem((AREA, C), BF16),
        vmem((AREA, C), BF16),
        vmem((4, D0 * SIDE, C), BF16),
        vmem((4, 16, C), BF16),
        vmem((4, D0 * SIDE, C), BF16),
        vmem((4, 16, C), BF16),
        vmem((AREA, C), BF16),
        vmem((2, D1 * SIDE, C), BF16),
        vmem((4, D1 * D1, C), BF16),
        vmem((4, D1 * SIDE, C), BF16),
        vmem((4, D1 * D1, C), BF16),
        vmem((AREA, C), BF16),
        vmem((2, D1 * SIDE, C), BF16),
        vmem((4, D1 * D1, C), BF16),
        vmem((4, D1 * SIDE, C), BF16),
        vmem((4, D1 * D1, C), BF16),
        vmem((AREA, C), BF16),
        vmem((4, D0 * SIDE, C), BF16),
        vmem((4, 16, C), BF16),
        vmem((4, D0 * SIDE, C), BF16),
        vmem((4, 16, C), BF16),
        vmem(((SIDE + 2 * D0) * WIDE, C), F32),
        vmem(((SIDE + 2 * D1) * WIDE, C), F32),
        vmem(((SIDE + 2 * D1) * WIDE, C), F32),
        vmem(((SIDE + 2 * D0) * SIDE, 3 * C), BF16),
        vmem(((SIDE + 2 * D0) * SIDE, 3 * C), BF16),
        vmem(((SIDE + 2 * D1) * SIDE, 3 * C), BF16),
        vmem(((SIDE + 2 * D1) * SIDE, 3 * C), BF16),
        vmem((AREA, C), F32),
        vmem((AREA, C), BF16),
        vmem((AREA, C), F32),
        vmem((AREA, C), BF16),
        vmem((AREA, C), BF16),
        vmem((AREA, C), BF16),
        vmem((2, GRAD_ROWS, C), BF16),
        vmem((2 * n, piece, C), BF16),
        vmem((n, piece, C), BF16),
        vmem((n, piece, C), BF16),
        pltpu.SemaphoreType.DMA((4, 8)),
        pltpu.SemaphoreType.DMA((4, 8)),
        pltpu.SemaphoreType.DMA((4,)),
        pltpu.SemaphoreType.DMA((4,)),
        pltpu.SemaphoreType.DMA((2, n)),
        pltpu.SemaphoreType.DMA((2 * n,)),
    ] + [pltpu.SemaphoreType.DMA((n,))] * 4 + [pltpu.SemaphoreType.REGULAR] * 2 + [pltpu.SemaphoreType.DMA((5,))]

    call = pl.pallas_call(
        functools.partial(kernel, n, factor),
        out_shape=(
            jax.ShapeDtypeStruct((AREA, C), BF16),
            jax.ShapeDtypeStruct((CONV_ROWS, C), F32),
            jax.ShapeDtypeStruct((1, K), F32),
            jax.ShapeDtypeStruct((K, C), F32),
        ),
        in_specs=[pl.BlockSpec(memory_space=pltpu.HBM)] * 5,
        out_specs=[pl.BlockSpec(memory_space=pltpu.VMEM)] * 4,
        scratch_shapes=scratch,
        compiler_params=pltpu.CompilerParams(
            collective_id=0, has_side_effects=True, vmem_limit_bytes=58 * 1024 * 1024
        ),
        name="trunk",
    )

    def local(activations, cotangent, conv_weight, conv_bias, out_weight):
        grad, conv, bias, proj = call(
            activations.reshape(AREA, C),
            cotangent.reshape(AREA, C),
            jnp.swapaxes(conv_weight, 2, 3).reshape(CONV_ROWS, C),
            conv_bias,
            out_weight.reshape(K, C),
        )
        return (
            grad.reshape(1, SIDE, SIDE, C),
            jnp.swapaxes(conv.reshape(1, 9, K, C), 2, 3),
            bias,
            proj.reshape(1, K, C),
        )

    in_specs = (
        P("segment", "row", "col", None),
        P("segment", "row", "col", None),
        P("segment", None, None, None),
        P("segment", None),
        P("segment", None, None),
    )
    out_specs = (
        P("segment", "row", "col", None),
        P("segment", None, None, None),
        P("segment", None),
        P("segment", None, None),
    )
    return jax.shard_map(local, mesh=mesh, in_specs=in_specs, out_specs=out_specs, check_vma=False)
```

```python
import functools

import numpy as np

import jax
import jax.numpy as jnp
from jax import lax
from jax.experimental import pallas as pl
from jax.experimental.pallas import tpu as pltpu
from jax.sharding import PartitionSpec as P

MESH = pl.DeviceIdType.MESH
F32 = jnp.float32
BF16 = jnp.bfloat16

SIDE = 24
AREA = SIDE * SIDE
C = 128
K = 64
D0 = 2
D1 = 8
WIDE = 40
CONV_ROWS = 9 * K
PROJ_ROW = CONV_ROWS
BIAS_ROW = CONV_ROWS + K
PACK_ROWS = CONV_ROWS + K + 16
GRAD_BLOCKS = 12
GRAD_ROWS = GRAD_BLOCKS * K
DIRECTIONS = ((-1, 0), (1, 0), (0, -1), (0, 1), (-1, -1), (-1, 1), (1, -1), (1, 1))
OPPOSITE = (1, 0, 3, 2, 7, 6, 5, 4)
NT = (((1,), (1,)), ((), ()))
TN = (((0,), (0,)), ((), ()))


def dot(a, b, dims=(((1,), (0,)), ((), ()))):
    return lax.dot_general(a, b, dims, preferred_element_type=F32)


def kernel(
    n,
    factor,
    act_in,
    cot_in,
    conv_in,
    bias_in,
    proj_in,
    out_grad,
    out_conv,
    out_bias,
    out_proj,
    act,
    cot,
    bias_w,
    weights,
    first,
    second,
    back1,
    back0,
    proj_pad,
    proj_twice,
    own_f,
    work_f,
    stage_f,
    sum_t,
    cot_t,
    sum_m,
    cot_m,
    send_e0,
    send_c0,
    recv_e0,
    recv_c0,
    hidden1,
    hid_e,
    hid_c,
    recv_e1,
    recv_c1,
    gp1,
    gp1_e,
    gp1_c,
    recv_e2,
    recv_c2,
    gp0,
    gp0_e,
    gp0_c,
    recv_e3,
    recv_c3,
    pad_a,
    pad_8,
    pad_9,
    cols_a,
    cols_b,
    cols_8,
    cols_g,
    pre0,
    bottle0,
    grad_bot,
    bottle1,
    branch1,
    branch0,
    grads,
    plane_recv,
    near_recv,
    far_recv,
    total_recv,
    halo_send,
    halo_recv,
    pair_send,
    pair_recv,
    plane_send_sem,
    plane_recv_sem,
    near_send_sem,
    near_recv_sem,
    far_send_sem,
    far_recv_sem,
    all_send_sem,
    all_recv_sem,
    partner,
    input_sem,
):
    seg = lax.axis_index("segment")
    row = lax.axis_index("row")
    col = lax.axis_index("col")
    part = int(round(n**0.5))
    piece = GRAD_ROWS // n
    row_hi, row_lo = row // part, row % part
    col_hi, col_lo = col // part, col % part
    plane_me = row_lo * part + col_lo
    off_diagonal = row != col
    mirror = (seg, col, row)
    sibling = (1 - seg, row, col)

    def hops(step):
        return sum(min(d, part - d) for d in divmod(step, part))

    plane_steps = sorted(range(1, n), key=hops, reverse=True)

    def plane_peer(section, step):
        return (
            section,
            row_hi * part + (row_lo + step // part) % part,
            col_hi * part + (col_lo + step % part) % part,
        )

    def plane_index(step):
        return (row_lo + step // part) % part * part + (col_lo + step % part) % part

    def near_peer(step):
        return (seg, (row_hi + step) % part * part + row_lo, col)

    def far_peer(step):
        return (seg, row, (col_hi + step) % part * part + col_lo)

    def there(k):
        dr, dc = DIRECTIONS[k]
        r, c = row + dr, col + dc
        exists = None
        if dr:
            exists = (r >= 0) if dr < 0 else (r < n)
        if dc:
            side = (c >= 0) if dc < 0 else (c < n)
            exists = side if exists is None else jnp.logical_and(exists, side)
        return exists

    def neighbour(k):
        dr, dc = DIRECTIONS[k]
        return (seg, row + dr, col + dc)

    inputs = [
        pltpu.make_async_copy(src, dst, input_sem.at[i])
        for i, (src, dst) in enumerate(
            (
                (act_in, act),
                (cot_in, cot),
                (conv_in, weights.at[seg, 0:CONV_ROWS]),
                (proj_in, weights.at[seg, PROJ_ROW : PROJ_ROW + K]),
                (bias_in, bias_w),
            )
        )
    ]
    for copy in inputs:
        copy.start()
    barrier = pltpu.get_barrier_semaphore()

    def signal(device):
        pl.semaphore_signal(barrier, inc=1, device_id=device, device_id_type=MESH)

    greeted = jnp.int32(1 + 2 * (part - 1))
    pl.when(off_diagonal)(functools.partial(signal, mirror))
    greeted = greeted + off_diagonal.astype(jnp.int32)
    for step in range(1, part):
        signal(far_peer(step))
        signal(near_peer(step))
    for k in range(7, -1, -1):
        pl.when(there(k))(functools.partial(signal, neighbour(k)))
        greeted = greeted + there(k).astype(jnp.int32)
    signal(sibling)

    strip = D0 * SIDE
    corners_of_tile = ((0, 0), (0, SIDE - D0), (SIDE - D0, 0), (SIDE - D0, SIDE - D0))

    def pack_corners(tile, corners):
        for k, (r, c) in enumerate(corners_of_tile):
            stage_f[...] = jnp.zeros((16, C), F32)
            for i in range(D0):
                start = (r + i) * SIDE + c
                stage_f[i * D0 : (i + 1) * D0] = tile[start : start + D0]
            corners[k] = stage_f[...].astype(BF16)

    def pack_narrow(tile, edges, corners):
        edges[0] = tile[0:strip].astype(BF16)
        edges[1] = tile[AREA - strip : AREA].astype(BF16)
        for k, first_column in ((2, 0), (3, SIDE - D0)):
            columns = [tile[pl.ds(first_column + j, SIDE, stride=SIDE), :] for j in range(D0)]
            edges[k] = jnp.concatenate(columns, axis=0).astype(BF16)
        pack_corners(tile, corners)

    inputs[0].wait()
    own_f[...] = act[...].astype(F32)
    pack_narrow(own_f, send_e0, send_c0)

    pl.semaphore_wait(barrier, greeted)

    def pair_copy(src, dst, index, device):
        return pltpu.make_async_remote_copy(
            src_ref=src,
            dst_ref=dst,
            send_sem=pair_send.at[index],
            recv_sem=pair_recv.at[index],
            device_id=device,
            device_id_type=MESH,
        )

    def mirror_copy(src, dst, index):
        return pair_copy(src, dst, index, mirror)

    def mirror_start(src, dst, index):
        @pl.when(off_diagonal)
        def _():
            mirror_copy(src, dst, index).start()

        @pl.when(jnp.logical_not(off_diagonal))
        def _():
            dst[...] = src[...]

    def mirror_wait(src, dst, index):
        pl.when(off_diagonal)(lambda: mirror_copy(src, dst, index).wait_recv())

    def halo_to(phase, k, slot, device, sources, edges, corners):
        return pltpu.make_async_remote_copy(
            src_ref=sources[k],
            dst_ref=edges.at[slot] if slot < 4 else corners.at[slot - 4],
            send_sem=halo_send.at[phase, k],
            recv_sem=halo_recv.at[phase, slot],
            device_id=device,
            device_id_type=MESH,
        )

    def halo_copy(phase, k, sources, edges, corners):
        return halo_to(phase, k, OPPOSITE[k], neighbour(k), sources, edges, corners)

    def halo_start(*halo):
        for k in range(7, -1, -1):
            pl.when(there(k))(lambda k=k: halo_copy(halo[0], k, *halo[1:]).start())

    def halo_clear(phase, sources, edges, corners):
        for k in range(8):

            @pl.when(jnp.logical_not(there(k)))
            def _():
                ref = edges.at[k] if k < 4 else corners.at[k - 4]
                ref[...] = jnp.zeros_like(ref)

    def arrived(phase, k, edges, corners):
        target = edges.at[k] if k < 4 else corners.at[k - 4]
        return pltpu.make_async_remote_copy(
            src_ref=target,
            dst_ref=target,
            send_sem=halo_send.at[phase, k],
            recv_sem=halo_recv.at[phase, k],
            device_id=neighbour(k),
            device_id_type=MESH,
        )

    def halo_wait(phase, sources, edges, corners):
        for k in range(8):
            pl.when(there(k))(lambda k=k: arrived(phase, k, edges, corners).wait_recv())

    def halo_sent(*halo):
        for k in range(8):
            pl.when(there(k))(lambda k=k: halo_copy(halo[0], k, *halo[1:]).wait_send())

    sources0 = tuple(send_e0.at[k] for k in range(4)) + tuple(send_c0.at[k] for k in range(4))
    halo0 = (0, sources0, recv_e0, recv_c0)
    halo_start(*halo0)

    def turn(flat, out):
        @pl.loop(0, SIDE // 2)
        def _(i):
            two = jnp.concatenate(
                [flat[pl.ds(2 * i, SIDE, stride=SIDE), :], flat[pl.ds(2 * i + 1, SIDE, stride=SIDE), :]], axis=0
            )
            out[pl.ds(pl.multiple_of(i * 2 * SIDE, 16), 2 * SIDE), :] = two.astype(BF16)

    inputs[1].wait()
    work_f[...] = cot[...].astype(F32)
    turn(work_f, cot_t)
    mirror_start(cot_t, cot_m, 1)

    for copy in inputs[2:]:
        copy.wait()
    bias_row = bias_w[...].astype(F32)
    weights[seg, BIAS_ROW : BIAS_ROW + 16] = jnp.broadcast_to(
        jnp.concatenate([bias_row, bias_row], axis=1), (16, 2 * K)
    ).astype(BF16)
    weights_copy = pair_copy(weights.at[seg], weights.at[seg], 2, sibling)
    weights_copy.start()
    halo_clear(*halo0)
    halo_clear(1, None, recv_e1, recv_c1)
    halo_clear(2, None, recv_e2, recv_c2)
    halo_clear(3, None, recv_e3, recv_c3)

    def unpack_narrow(edges, corners, pad, change):
        north = change(edges[0].astype(F32))
        south = change(edges[1].astype(F32))
        west = change(edges[2].astype(F32))
        east = change(edges[3].astype(F32))
        for i in range(D0):
            lines = slice(i * SIDE, (i + 1) * SIDE)
            pad[i * WIDE + 8 : i * WIDE + 8 + SIDE] = north[lines]
            low = (D0 + SIDE + i) * WIDE + 8
            pad[low : low + SIDE] = south[lines]
            pad[pl.ds(D0 * WIDE + 8 - D0 + i, SIDE, stride=WIDE), :] = west[lines]
            pad[pl.ds(D0 * WIDE + 8 + SIDE + i, SIDE, stride=WIDE), :] = east[lines]
        for k, (r, c) in enumerate(((0, 8 - D0), (0, 8 + SIDE), (D0 + SIDE, 8 - D0), (D0 + SIDE, 8 + SIDE))):
            stage_f[...] = change(corners[k].astype(F32))
            for i in range(D0):
                start = (r + i) * WIDE + c
                pad[start : start + D0] = stage_f[i * D0 : (i + 1) * D0]

    def fill_centre(tile, pad, dilation, change):
        for i in range(SIDE):
            start = (dilation + i) * WIDE + 8
            pad[start : start + SIDE] = change(tile[i * SIDE : (i + 1) * SIDE])

    def pack_wide(tile, edges, corners):
        for k, first in ((0, 0), (1, SIDE - D1)):
            edges[k] = jnp.concatenate(
                [tile[i * SIDE + first : i * SIDE + first + D1] for i in range(SIDE)], axis=0
            ).astype(BF16)
        for k, (r, c) in enumerate(((0, 0), (0, SIDE - D1), (SIDE - D1, 0), (SIDE - D1, SIDE - D1))):
            corners[k] = jnp.concatenate(
                [tile[(r + i) * SIDE + c : (r + i) * SIDE + c + D1] for i in range(D1)], axis=0
            ).astype(BF16)

    def wide_sources(flat, edges, corners):
        lines = D1 * SIDE
        return (
            flat.at[0:lines],
            flat.at[AREA - lines : AREA],
            edges.at[0],
            edges.at[1],
        ) + tuple(corners.at[k] for k in range(4))

    def unpack_wide(edges, corners, pad):
        north = edges[0].astype(F32)
        south = edges[1].astype(F32)
        west = edges[2].astype(F32)
        east = edges[3].astype(F32)
        for i in range(D1):
            lines = slice(i * SIDE, (i + 1) * SIDE)
            pad[i * WIDE + D1 : i * WIDE + D1 + SIDE] = north[lines]
            low = (D1 + SIDE + i) * WIDE + D1
            pad[low : low + SIDE] = south[lines]
        for i in range(SIDE):
            lines = slice(i * D1, (i + 1) * D1)
            start = (D1 + i) * WIDE
            pad[start : start + D1] = west[lines]
            pad[start + D1 + SIDE : start + WIDE] = east[lines]
        for k, (r, c) in enumerate(((0, 0), (0, D1 + SIDE), (D1 + SIDE, 0), (D1 + SIDE, D1 + SIDE))):
            corner = corners[k].astype(F32)
            for i in range(D1):
                start = (r + i) * WIDE + c
                pad[start : start + D1] = corner[i * D1 : (i + 1) * D1]

    def spread(pad, cols, dilation):
        for b in range(3):
            first = 8 + (b - 1) * dilation
            for i in range(0, SIDE + 2 * dilation, 2):
                two = jnp.concatenate(
                    [pad[(i + h) * WIDE + first : (i + h) * WIDE + first + SIDE] for h in range(2)], axis=0
                )
                cols[i * SIDE : (i + 2) * SIDE, b * C : (b + 1) * C] = two.astype(BF16)

    same = lambda x: x
    relu = lambda x: jnp.maximum(x, 0.0)

    fill_centre(own_f, pad_a, D0, relu)
    for ref in (first, back1, back0, proj_pad):
        ref[...] = jnp.zeros_like(ref)
    weights_copy.wait_recv()

    proj_pad[0:K] = weights[0, PROJ_ROW : PROJ_ROW + K]
    for s in range(2):
        for h in range(2):
            proj_twice[s, h * K : (h + 1) * K] = weights[s, PROJ_ROW : PROJ_ROW + K]
    tap = lambda a, b: slice((3 * a + b) * K, (3 * a + b + 1) * K)
    for a in range(3):
        for b in range(3):
            lanes = slice(b * C, (b + 1) * C)
            own, turned = slice(b * C, b * C + K), slice(b * C + K, (b + 1) * C)
            first[a, 0:K, lanes] = weights[0, tap(a, b)]
            second[a, 0:K, lanes] = weights[1, tap(a, b)]
            second[a, K : 2 * K, lanes] = weights[1, tap(b, a)]
            back0[a, own] = weights[0, tap(2 - a, 2 - b)]
            back1[a, own, 0:C] = weights[1, tap(2 - a, 2 - b)]
            back1[a, turned, C : 2 * C] = weights[1, tap(2 - b, 2 - a)]

    halo_wait(*halo0)
    unpack_narrow(recv_e0, recv_c0, pad_a, relu)
    spread(pad_a, cols_a, D0)

    chunk = 192
    shift0 = D0 * SIDE
    shift1 = D1 * SIDE

    def rows_at(base, extra=0):
        return pl.ds(pl.multiple_of(base + extra, 16), chunk)

    bias0 = weights[0, BIAS_ROW : BIAS_ROW + 16].astype(F32)[0:1]
    bias1 = weights[1, BIAS_ROW : BIAS_ROW + 16].astype(F32)[0:1]

    @pl.loop(0, AREA // chunk)
    def _(i):
        base = i * chunk
        total = bias0
        for a in range(3):
            total = total + dot(cols_a[rows_at(base, a * shift0), :], first[a], NT)
        pre0[rows_at(base), :] = total
        bottle = jnp.maximum(total, 0.0).astype(BF16)
        bottle0[rows_at(base), :] = bottle
        branch_sum = (own_f[rows_at(base), :] + dot(bottle, proj_pad[...])).astype(BF16)
        work_f[rows_at(base), :] = branch_sum.astype(F32)

    turn(work_f, sum_t)
    mirror_start(sum_t, sum_m, 0)

    mirror_wait(cot_t, cot_m, 1)

    @pl.loop(0, AREA // chunk)
    def _(i):
        at = rows_at(i * chunk)
        branch = ((cot[at, :].astype(F32) + cot_m[at, :].astype(F32)) * 0.5).astype(BF16)
        branch1[at, :] = branch
        grad_bot[at, :] = dot(branch, proj_twice[1], NT)

    mirror_wait(sum_t, sum_m, 0)

    @pl.loop(0, AREA // chunk)
    def _(i):
        at = rows_at(i * chunk)
        sym = ((work_f[at, :] + sum_m[at, :].astype(F32)) * 0.5).astype(BF16)
        live = jnp.maximum(sym, jnp.zeros_like(sym))
        hidden1[at, :] = live
        work_f[at, :] = live.astype(F32)

    pack_wide(work_f, hid_e, hid_c)
    halo1 = (1, wide_sources(hidden1, hid_e, hid_c), recv_e1, recv_c1)
    halo_start(*halo1)
    fill_centre(work_f, pad_8, D1, same)

    halo_wait(*halo1)

    pl.semaphore_signal(partner, inc=1, device_id=sibling, device_id_type=MESH)

    unpack_wide(recv_e1, recv_c1, pad_8)
    spread(pad_8, cols_8, D1)

    @pl.loop(0, AREA // chunk)
    def _(i):
        base = i * chunk
        total = bias1
        for a in range(3):
            total = total + dot(cols_8[rows_at(base, a * shift1), :], second[a], NT)
        bottle1[rows_at(base), :] = jnp.maximum(total, 0.0).astype(BF16)
        grad = jnp.where(total > 0, grad_bot[rows_at(base), :], 0.0)
        work_f[rows_at(base), :] = grad
        gp1[rows_at(base), :] = grad.astype(BF16)

    pack_wide(work_f, gp1_e, gp1_c)
    halo2 = (2, wide_sources(gp1, gp1_e, gp1_c), recv_e2, recv_c2)
    halo_start(*halo2)

    ones = jnp.ones((AREA, C), BF16)

    def weight_gradients(s, grad_pre, cols, shift, bottle, branch):
        turned_grad = grad_pre[...].T[0:K]
        for a in range(3):
            product = dot(turned_grad, cols[a * shift : a * shift + AREA, :])
            for b in range(3):
                at = (3 * a + b) * K
                grads[s, at : at + K] = product[:, b * C : (b + 1) * C].astype(BF16)
        grads[s, 9 * K : 10 * K] = dot(bottle[...].T[0:K], branch[...]).astype(BF16)
        grads[s, 10 * K : 11 * K] = dot(turned_grad, ones).astype(BF16)
        grads[s, 11 * K : 12 * K] = jnp.zeros((K, C), BF16)

    def piece_at(index):
        return pl.ds(pl.multiple_of(index * piece, 16), piece)

    slot_me = seg * n + plane_me

    def group_copy(src, dst, send_sem, recv_sem, device):
        return pltpu.make_async_remote_copy(
            src_ref=src, dst_ref=dst, send_sem=send_sem, recv_sem=recv_sem, device_id=device, device_id_type=MESH
        )

    def plane_copy(s, step):
        return group_copy(
            grads.at[s, piece_at(plane_index(step))],
            plane_recv.at[slot_me],
            plane_send_sem.at[s, step],
            plane_recv_sem.at[slot_me],
            plane_peer(s, step),
        )

    def plane_start(s):
        for step in plane_steps:
            plane_copy(s, step).start()

        @pl.when(seg != s)
        def _():
            plane_copy(s, 0).start()

        @pl.when(seg == s)
        def _():
            plane_recv[slot_me] = grads[s, piece_at(plane_me), :]

    def plane_sent(s):
        for step in plane_steps:
            plane_copy(s, step).wait_send()

        @pl.when(seg != s)
        def _():
            plane_copy(s, 0).wait_send()

    def arrive(dst, send_sem, recv_sem, index):
        group_copy(dst.at[index], dst.at[index], send_sem, recv_sem.at[index], sibling).wait_recv()

    def plane_wait():
        @pl.loop(1, 2 * n)
        def _(step):
            arrive(plane_recv, plane_send_sem.at[0, 0], plane_recv_sem, (slot_me + step) % (2 * n))

    def near_copy(step):
        mine = near_recv.at[row_hi]
        return group_copy(mine, mine, near_send_sem.at[step], near_recv_sem.at[row_hi], near_peer(step))

    def far_copy(step):
        mine = far_recv.at[col_hi]
        return group_copy(mine, mine, far_send_sem.at[step], far_recv_sem.at[col_hi], far_peer(step))

    def all_copy(step):
        mine = total_recv.at[plane_me]
        return group_copy(mine, mine, all_send_sem.at[step], all_recv_sem.at[plane_me], plane_peer(seg, step))

    def add_up(buffer, count):
        total = buffer[0].astype(F32)
        for i in range(1, count):
            total = total + buffer[i].astype(F32)
        return total

    def near_start():
        plane_wait()
        near_recv[row_hi] = add_up(plane_recv, 2 * n).astype(BF16)
        for step in range(1, part):
            near_copy(step).start()

    def far_start():
        for step in range(1, part):
            arrive(near_recv, near_send_sem.at[step], near_recv_sem, (row_hi + step) % part)
        far_recv[col_hi] = add_up(near_recv, part).astype(BF16)
        for step in range(1, part):
            far_copy(step).start()

    weight_gradients(1, gp1, cols_8, shift1, bottle1, branch1)
    pl.semaphore_wait(partner, 1)
    plane_start(1)
    fill_centre(work_f, pad_9, D1, same)

    halo_wait(*halo2)

    unpack_wide(recv_e2, recv_c2, pad_9)
    spread(pad_9, cols_g, D1)

    @pl.loop(0, AREA // chunk)
    def _(i):
        base = i * chunk
        total = None
        for a in range(3):
            term = dot(cols_g[rows_at(base, a * shift1), :], back1[a])
            total = term if total is None else total + term
        branch = branch1[rows_at(base), :].astype(F32)
        live = hidden1[rows_at(base), :].astype(F32) > 0
        own = (branch + jnp.where(live, total[:, 0:C], 0.0)).astype(BF16).astype(F32)
        turned = (branch + jnp.where(live, total[:, C : 2 * C], 0.0)).astype(BF16).astype(F32)
        mean = ((own + turned) * 0.5).astype(BF16)
        branch0[rows_at(base), :] = mean
        grad = jnp.where(pre0[rows_at(base), :] > 0, dot(mean, proj_twice[0], NT), 0.0)
        work_f[rows_at(base), :] = grad
        gp0[rows_at(base), :] = grad.astype(BF16)

    weight_gradients(0, gp0, cols_a, shift0, bottle0, branch0)

    plane_start(0)

    pack_narrow(work_f, gp0_e, gp0_c)
    sources3 = tuple(gp0_e.at[k] for k in range(4)) + tuple(gp0_c.at[k] for k in range(4))
    halo3 = (3, sources3, recv_e3, recv_c3)
    halo_start(*halo3)
    fill_centre(work_f, pad_a, D0, same)

    near_start()

    far_start()

    halo_wait(*halo3)

    unpack_narrow(recv_e3, recv_c3, pad_a, same)
    spread(pad_a, cols_b, D0)

    @pl.loop(0, AREA // chunk)
    def _(i):
        base = i * chunk
        total = None
        for a in range(3):
            term = dot(cols_b[rows_at(base, a * shift0), :], back0[a])
            total = term if total is None else total + term
        branch = branch0[rows_at(base), :].astype(F32)
        live = own_f[rows_at(base), :] > 0
        out_grad[rows_at(base), :] = (branch + jnp.where(live, total, 0.0)).astype(BF16)

    pl.when(off_diagonal)(lambda: mirror_copy(sum_t, sum_m, 0).wait_send())
    pl.when(off_diagonal)(lambda: mirror_copy(cot_t, cot_m, 1).wait_send())
    weights_copy.wait_send()
    for halo in (halo0, halo1, halo2, halo3):
        halo_sent(*halo)
    plane_sent(0)
    plane_sent(1)

    for step in range(1, part):
        arrive(far_recv, far_send_sem.at[step], far_recv_sem, (col_hi + step) % part)

    total_recv[plane_me] = add_up(far_recv, part).astype(BF16)
    for step in plane_steps:
        all_copy(step).start()
    for step in range(1, part):
        near_copy(step).wait_send()
        far_copy(step).wait_send()

    @pl.loop(1, n)
    def _(step):
        arrive(total_recv, all_send_sem.at[step], all_recv_sem, (plane_me + step) % n)

    for i in range(n):
        values = total_recv[i].astype(F32) * factor
        if piece <= K and (i + 1) * piece <= CONV_ROWS:
            out_conv[i * piece : (i + 1) * piece] = values
        else:
            for first, last, out in ((0, CONV_ROWS, out_conv), (9 * K, 10 * K, out_proj), (10 * K, 11 * K, None)):
                low, high = max(first, i * piece), min(last, (i + 1) * piece)
                if low < high:
                    block = values[low - i * piece : high - i * piece]
                    if out is None:
                        work_f[low - first : high - first] = block
                    else:
                        out[low - first : high - first] = block
    out_bias[...] = work_f[0:K].T[0:1]
    for step in plane_steps:
        all_copy(step).wait_send()


def solution(mesh):
    n = mesh.shape["row"]
    cells = mesh.shape["segment"] * (SIDE * n) * (SIDE * n)
    factor = float(np.float32(1.0) / np.sqrt(np.float32(cells)))
    piece = GRAD_ROWS // n
    part = int(round(n**0.5))
    vmem = pltpu.VMEM
    scratch = [
        vmem((AREA, C), BF16),
        vmem((AREA, C), BF16),
        vmem((1, K), BF16),
        vmem((2, PACK_ROWS, C), BF16),
        vmem((3, 2 * K, 3 * C), BF16),
        vmem((3, 2 * K, 3 * C), BF16),
        vmem((3, 3 * C, 2 * C), BF16),
        vmem((3, 3 * C, C), BF16),
        vmem((2 * K, C), BF16),
        vmem((2, 2 * K, C), BF16),
        vmem((AREA, C), F32),
        vmem((AREA, C), F32),
        vmem((16, C), F32),
        vmem((AREA, C), BF16),
        vmem((AREA, C), BF16),
        vmem((AREA, C), BF16),
        vmem((AREA, C), BF16),
        vmem((4, D0 * SIDE, C), BF16),
        vmem((4, 16, C), BF16),
        vmem((4, D0 * SIDE, C), BF16),
        vmem((4, 16, C), BF16),
        vmem((AREA, C), BF16),
        vmem((2, D1 * SIDE, C), BF16),
        vmem((4, D1 * D1, C), BF16),
        vmem((4, D1 * SIDE, C), BF16),
        vmem((4, D1 * D1, C), BF16),
        vmem((AREA, C), BF16),
        vmem((2, D1 * SIDE, C), BF16),
        vmem((4, D1 * D1, C), BF16),
        vmem((4, D1 * SIDE, C), BF16),
        vmem((4, D1 * D1, C), BF16),
        vmem((AREA, C), BF16),
        vmem((4, D0 * SIDE, C), BF16),
        vmem((4, 16, C), BF16),
        vmem((4, D0 * SIDE, C), BF16),
        vmem((4, 16, C), BF16),
        vmem(((SIDE + 2 * D0) * WIDE, C), F32),
        vmem(((SIDE + 2 * D1) * WIDE, C), F32),
        vmem(((SIDE + 2 * D1) * WIDE, C), F32),
        vmem(((SIDE + 2 * D0) * SIDE, 3 * C), BF16),
        vmem(((SIDE + 2 * D0) * SIDE, 3 * C), BF16),
        vmem(((SIDE + 2 * D1) * SIDE, 3 * C), BF16),
        vmem(((SIDE + 2 * D1) * SIDE, 3 * C), BF16),
        vmem((AREA, C), F32),
        vmem((AREA, C), BF16),
        vmem((AREA, C), F32),
        vmem((AREA, C), BF16),
        vmem((AREA, C), BF16),
        vmem((AREA, C), BF16),
        vmem((2, GRAD_ROWS, C), BF16),
        vmem((2 * n, piece, C), BF16),
        vmem((part, piece, C), BF16),
        vmem((part, piece, C), BF16),
        vmem((n, piece, C), BF16),
        pltpu.SemaphoreType.DMA((4, 8)),
        pltpu.SemaphoreType.DMA((4, 8)),
        pltpu.SemaphoreType.DMA((4,)),
        pltpu.SemaphoreType.DMA((4,)),
        pltpu.SemaphoreType.DMA((2, n)),
        pltpu.SemaphoreType.DMA((2 * n,)),
    ] + [pltpu.SemaphoreType.DMA((part,))] * 4 + [pltpu.SemaphoreType.DMA((n,))] * 2
    scratch += [pltpu.SemaphoreType.REGULAR, pltpu.SemaphoreType.DMA((5,))]

    call = pl.pallas_call(
        functools.partial(kernel, n, factor),
        out_shape=(
            jax.ShapeDtypeStruct((AREA, C), BF16),
            jax.ShapeDtypeStruct((CONV_ROWS, C), F32),
            jax.ShapeDtypeStruct((1, K), F32),
            jax.ShapeDtypeStruct((K, C), F32),
        ),
        in_specs=[pl.BlockSpec(memory_space=pltpu.HBM)] * 5,
        out_specs=[pl.BlockSpec(memory_space=pltpu.VMEM)] * 4,
        scratch_shapes=scratch,
        compiler_params=pltpu.CompilerParams(
            collective_id=0, has_side_effects=True, vmem_limit_bytes=58 * 1024 * 1024
        ),
        name="trunk",
    )

    def local(activations, cotangent, conv_weight, conv_bias, out_weight):
        grad, conv, bias, proj = call(
            activations.reshape(AREA, C),
            cotangent.reshape(AREA, C),
            jnp.swapaxes(conv_weight, 2, 3).reshape(CONV_ROWS, C),
            conv_bias,
            out_weight.reshape(K, C),
        )
        return (
            grad.reshape(1, SIDE, SIDE, C),
            jnp.swapaxes(conv.reshape(1, 9, K, C), 2, 3),
            bias,
            proj.reshape(1, K, C),
        )

    in_specs = (
        P("segment", "row", "col", None),
        P("segment", "row", "col", None),
        P("segment", None, None, None),
        P("segment", None),
        P("segment", None, None),
    )
    out_specs = (
        P("segment", "row", "col", None),
        P("segment", None, None, None),
        P("segment", None),
        P("segment", None, None),
    )
    return jax.shard_map(local, mesh=mesh, in_specs=in_specs, out_specs=out_specs, check_vma=False)
```

```python
import functools

import numpy as np

import jax
import jax.numpy as jnp
from jax import lax
from jax.experimental import pallas as pl
from jax.experimental.pallas import tpu as pltpu
from jax.sharding import PartitionSpec as P

MESH = pl.DeviceIdType.MESH
F32 = jnp.float32
BF16 = jnp.bfloat16

SIDE = 24
AREA = SIDE * SIDE
C = 128
K = 64
D0 = 2
D1 = 8
WIDE = 40
CONV_ROWS = 9 * K
PROJ_ROW = CONV_ROWS
BIAS_ROW = CONV_ROWS + K
PACK_ROWS = CONV_ROWS + K + 16
GRAD_BLOCKS = 12
GRAD_ROWS = GRAD_BLOCKS * K
DIRECTIONS = ((-1, 0), (1, 0), (0, -1), (0, 1), (-1, -1), (-1, 1), (1, -1), (1, 1))
OPPOSITE = (1, 0, 3, 2, 7, 6, 5, 4)
NT = (((1,), (1,)), ((), ()))
TN = (((0,), (0,)), ((), ()))


def dot(a, b, dims=(((1,), (0,)), ((), ()))):
    return lax.dot_general(a, b, dims, preferred_element_type=F32)


def kernel(
    n,
    act_in,
    cot_in,
    conv_in,
    bias_in,
    proj_in,
    out_grad,
    total_recv,
    act,
    cot,
    bias_w,
    weights,
    first,
    second,
    back1,
    back0,
    proj_pad,
    proj_twice,
    own_f,
    work_f,
    stage_f,
    sum_t,
    cot_t,
    sum_m,
    cot_m,
    send_e0,
    send_c0,
    recv_e0,
    recv_c0,
    hidden1,
    hid_e,
    hid_c,
    recv_e1,
    recv_c1,
    gp1,
    gp1_e,
    gp1_c,
    recv_e2,
    recv_c2,
    gp0,
    gp0_e,
    gp0_c,
    recv_e3,
    recv_c3,
    pad_a,
    pad_8,
    pad_9,
    cols_a,
    cols_b,
    cols_8,
    cols_g,
    pre0,
    bottle0,
    grad_bot,
    bottle1,
    branch1,
    branch0,
    grads,
    plane_recv,
    near_recv,
    far_recv,
    halo_send,
    halo_recv,
    pair_send,
    pair_recv,
    plane_send_sem,
    plane_recv_sem,
    near_send_sem,
    near_recv_sem,
    far_send_sem,
    far_recv_sem,
    all_send_sem,
    all_recv_sem,
    partner,
    input_sem,
):
    seg = lax.axis_index("segment")
    row = lax.axis_index("row")
    col = lax.axis_index("col")
    part = int(round(n**0.5))
    piece = GRAD_ROWS // n
    row_hi, row_lo = row // part, row % part
    col_hi, col_lo = col // part, col % part
    plane_me = row_lo * part + col_lo
    off_diagonal = row != col
    mirror = (seg, col, row)
    sibling = (1 - seg, row, col)

    def hops(step):
        return sum(min(d, part - d) for d in divmod(step, part))

    plane_steps = sorted(range(1, n), key=hops, reverse=True)

    def plane_peer(section, step):
        return (
            section,
            row_hi * part + (row_lo + step // part) % part,
            col_hi * part + (col_lo + step % part) % part,
        )

    def plane_index(step):
        return (row_lo + step // part) % part * part + (col_lo + step % part) % part

    def near_peer(step):
        return (seg, (row_hi + step) % part * part + row_lo, col)

    def far_peer(step):
        return (seg, row, (col_hi + step) % part * part + col_lo)

    def there(k):
        dr, dc = DIRECTIONS[k]
        r, c = row + dr, col + dc
        exists = None
        if dr:
            exists = (r >= 0) if dr < 0 else (r < n)
        if dc:
            side = (c >= 0) if dc < 0 else (c < n)
            exists = side if exists is None else jnp.logical_and(exists, side)
        return exists

    def neighbour(k):
        dr, dc = DIRECTIONS[k]
        return (seg, row + dr, col + dc)

    inputs = [
        pltpu.make_async_copy(src, dst, input_sem.at[i])
        for i, (src, dst) in enumerate(
            (
                (act_in, act),
                (cot_in, cot),
                (conv_in, weights.at[seg, 0:CONV_ROWS]),
                (proj_in, weights.at[seg, PROJ_ROW : PROJ_ROW + K]),
                (bias_in, bias_w),
            )
        )
    ]
    for copy in inputs:
        copy.start()
    barrier = pltpu.get_barrier_semaphore()

    def signal(device):
        pl.semaphore_signal(barrier, inc=1, device_id=device, device_id_type=MESH)

    greeted = jnp.int32(1 + 2 * (part - 1))
    pl.when(off_diagonal)(functools.partial(signal, mirror))
    greeted = greeted + off_diagonal.astype(jnp.int32)
    for step in range(1, part):
        signal(far_peer(step))
        signal(near_peer(step))
    for k in range(7, -1, -1):
        pl.when(there(k))(functools.partial(signal, neighbour(k)))
        greeted = greeted + there(k).astype(jnp.int32)
    signal(sibling)

    strip = D0 * SIDE
    corners_of_tile = ((0, 0), (0, SIDE - D0), (SIDE - D0, 0), (SIDE - D0, SIDE - D0))

    def pack_corners(tile, corners):
        for k, (r, c) in enumerate(corners_of_tile):
            stage_f[...] = jnp.zeros((16, C), F32)
            for i in range(D0):
                start = (r + i) * SIDE + c
                stage_f[i * D0 : (i + 1) * D0] = tile[start : start + D0]
            corners[k] = stage_f[...].astype(BF16)

    def pack_narrow(tile, edges, corners):
        edges[0] = tile[0:strip].astype(BF16)
        edges[1] = tile[AREA - strip : AREA].astype(BF16)
        for k, first_column in ((2, 0), (3, SIDE - D0)):
            columns = [tile[pl.ds(first_column + j, SIDE, stride=SIDE), :] for j in range(D0)]
            edges[k] = jnp.concatenate(columns, axis=0).astype(BF16)
        pack_corners(tile, corners)

    inputs[0].wait()
    own_f[...] = act[...].astype(F32)
    pack_narrow(own_f, send_e0, send_c0)

    pl.semaphore_wait(barrier, greeted)

    def pair_copy(src, dst, index, device):
        return pltpu.make_async_remote_copy(
            src_ref=src,
            dst_ref=dst,
            send_sem=pair_send.at[index],
            recv_sem=pair_recv.at[index],
            device_id=device,
            device_id_type=MESH,
        )

    def mirror_copy(src, dst, index):
        return pair_copy(src, dst, index, mirror)

    def mirror_start(src, dst, index):
        @pl.when(off_diagonal)
        def _():
            mirror_copy(src, dst, index).start()

        @pl.when(jnp.logical_not(off_diagonal))
        def _():
            dst[...] = src[...]

    def mirror_wait(src, dst, index):
        pl.when(off_diagonal)(lambda: mirror_copy(src, dst, index).wait_recv())

    def halo_to(phase, k, slot, device, sources, edges, corners):
        return pltpu.make_async_remote_copy(
            src_ref=sources[k],
            dst_ref=edges.at[slot] if slot < 4 else corners.at[slot - 4],
            send_sem=halo_send.at[phase, k],
            recv_sem=halo_recv.at[phase, slot],
            device_id=device,
            device_id_type=MESH,
        )

    def halo_copy(phase, k, sources, edges, corners):
        return halo_to(phase, k, OPPOSITE[k], neighbour(k), sources, edges, corners)

    def halo_start(*halo):
        for k in range(7, -1, -1):
            pl.when(there(k))(lambda k=k: halo_copy(halo[0], k, *halo[1:]).start())

    def halo_clear(phase, sources, edges, corners):
        for k in range(8):

            @pl.when(jnp.logical_not(there(k)))
            def _():
                ref = edges.at[k] if k < 4 else corners.at[k - 4]
                ref[...] = jnp.zeros_like(ref)

    def arrived(phase, k, edges, corners):
        target = edges.at[k] if k < 4 else corners.at[k - 4]
        return pltpu.make_async_remote_copy(
            src_ref=target,
            dst_ref=target,
            send_sem=halo_send.at[phase, k],
            recv_sem=halo_recv.at[phase, k],
            device_id=neighbour(k),
            device_id_type=MESH,
        )

    def halo_wait(phase, sources, edges, corners):
        for k in range(8):
            pl.when(there(k))(lambda k=k: arrived(phase, k, edges, corners).wait_recv())

    def halo_sent(*halo):
        for k in range(8):
            pl.when(there(k))(lambda k=k: halo_copy(halo[0], k, *halo[1:]).wait_send())

    sources0 = tuple(send_e0.at[k] for k in range(4)) + tuple(send_c0.at[k] for k in range(4))
    halo0 = (0, sources0, recv_e0, recv_c0)
    halo_start(*halo0)

    def turn(flat, out):
        @pl.loop(0, SIDE // 2)
        def _(i):
            two = jnp.concatenate(
                [flat[pl.ds(2 * i, SIDE, stride=SIDE), :], flat[pl.ds(2 * i + 1, SIDE, stride=SIDE), :]], axis=0
            )
            out[pl.ds(pl.multiple_of(i * 2 * SIDE, 16), 2 * SIDE), :] = two.astype(BF16)

    inputs[1].wait()
    work_f[...] = cot[...].astype(F32)
    turn(work_f, cot_t)
    mirror_start(cot_t, cot_m, 1)

    for copy in inputs[2:]:
        copy.wait()
    bias_row = bias_w[...].astype(F32)
    weights[seg, BIAS_ROW : BIAS_ROW + 16] = jnp.broadcast_to(
        jnp.concatenate([bias_row, bias_row], axis=1), (16, 2 * K)
    ).astype(BF16)
    weights_copy = pair_copy(weights.at[seg], weights.at[seg], 2, sibling)
    weights_copy.start()
    halo_clear(*halo0)
    halo_clear(1, None, recv_e1, recv_c1)
    halo_clear(2, None, recv_e2, recv_c2)
    halo_clear(3, None, recv_e3, recv_c3)

    def unpack_narrow(edges, corners, pad, change):
        north = change(edges[0].astype(F32))
        south = change(edges[1].astype(F32))
        west = change(edges[2].astype(F32))
        east = change(edges[3].astype(F32))
        for i in range(D0):
            lines = slice(i * SIDE, (i + 1) * SIDE)
            pad[i * WIDE + 8 : i * WIDE + 8 + SIDE] = north[lines]
            low = (D0 + SIDE + i) * WIDE + 8
            pad[low : low + SIDE] = south[lines]
            pad[pl.ds(D0 * WIDE + 8 - D0 + i, SIDE, stride=WIDE), :] = west[lines]
            pad[pl.ds(D0 * WIDE + 8 + SIDE + i, SIDE, stride=WIDE), :] = east[lines]
        for k, (r, c) in enumerate(((0, 8 - D0), (0, 8 + SIDE), (D0 + SIDE, 8 - D0), (D0 + SIDE, 8 + SIDE))):
            stage_f[...] = change(corners[k].astype(F32))
            for i in range(D0):
                start = (r + i) * WIDE + c
                pad[start : start + D0] = stage_f[i * D0 : (i + 1) * D0]

    def fill_centre(tile, pad, dilation, change):
        for i in range(SIDE):
            start = (dilation + i) * WIDE + 8
            pad[start : start + SIDE] = change(tile[i * SIDE : (i + 1) * SIDE])

    def pack_wide(tile, edges, corners):
        for k, first in ((0, 0), (1, SIDE - D1)):
            edges[k] = jnp.concatenate(
                [tile[i * SIDE + first : i * SIDE + first + D1] for i in range(SIDE)], axis=0
            ).astype(BF16)
        for k, (r, c) in enumerate(((0, 0), (0, SIDE - D1), (SIDE - D1, 0), (SIDE - D1, SIDE - D1))):
            corners[k] = jnp.concatenate(
                [tile[(r + i) * SIDE + c : (r + i) * SIDE + c + D1] for i in range(D1)], axis=0
            ).astype(BF16)

    def wide_sources(flat, edges, corners):
        lines = D1 * SIDE
        return (
            flat.at[0:lines],
            flat.at[AREA - lines : AREA],
            edges.at[0],
            edges.at[1],
        ) + tuple(corners.at[k] for k in range(4))

    def unpack_wide(edges, corners, pad):
        north = edges[0].astype(F32)
        south = edges[1].astype(F32)
        west = edges[2].astype(F32)
        east = edges[3].astype(F32)
        for i in range(D1):
            lines = slice(i * SIDE, (i + 1) * SIDE)
            pad[i * WIDE + D1 : i * WIDE + D1 + SIDE] = north[lines]
            low = (D1 + SIDE + i) * WIDE + D1
            pad[low : low + SIDE] = south[lines]
        for i in range(SIDE):
            lines = slice(i * D1, (i + 1) * D1)
            start = (D1 + i) * WIDE
            pad[start : start + D1] = west[lines]
            pad[start + D1 + SIDE : start + WIDE] = east[lines]
        for k, (r, c) in enumerate(((0, 0), (0, D1 + SIDE), (D1 + SIDE, 0), (D1 + SIDE, D1 + SIDE))):
            corner = corners[k].astype(F32)
            for i in range(D1):
                start = (r + i) * WIDE + c
                pad[start : start + D1] = corner[i * D1 : (i + 1) * D1]

    def spread(pad, cols, dilation):
        for b in range(3):
            first = 8 + (b - 1) * dilation
            for i in range(0, SIDE + 2 * dilation, 2):
                two = jnp.concatenate(
                    [pad[(i + h) * WIDE + first : (i + h) * WIDE + first + SIDE] for h in range(2)], axis=0
                )
                cols[i * SIDE : (i + 2) * SIDE, b * C : (b + 1) * C] = two.astype(BF16)

    same = lambda x: x
    relu = lambda x: jnp.maximum(x, 0.0)

    fill_centre(own_f, pad_a, D0, relu)
    for ref in (first, back1, back0, proj_pad):
        ref[...] = jnp.zeros_like(ref)
    weights_copy.wait_recv()

    proj_pad[0:K] = weights[0, PROJ_ROW : PROJ_ROW + K]
    for s in range(2):
        for h in range(2):
            proj_twice[s, h * K : (h + 1) * K] = weights[s, PROJ_ROW : PROJ_ROW + K]
    tap = lambda a, b: slice((3 * a + b) * K, (3 * a + b + 1) * K)
    for a in range(3):
        for b in range(3):
            lanes = slice(b * C, (b + 1) * C)
            own, turned = slice(b * C, b * C + K), slice(b * C + K, (b + 1) * C)
            first[a, 0:K, lanes] = weights[0, tap(a, b)]
            second[a, 0:K, lanes] = weights[1, tap(a, b)]
            second[a, K : 2 * K, lanes] = weights[1, tap(b, a)]
            back0[a, own] = weights[0, tap(2 - a, 2 - b)]
            back1[a, own, 0:C] = weights[1, tap(2 - a, 2 - b)]
            back1[a, turned, C : 2 * C] = weights[1, tap(2 - b, 2 - a)]

    halo_wait(*halo0)
    unpack_narrow(recv_e0, recv_c0, pad_a, relu)
    spread(pad_a, cols_a, D0)

    chunk = 192
    shift0 = D0 * SIDE
    shift1 = D1 * SIDE

    def rows_at(base, extra=0):
        return pl.ds(pl.multiple_of(base + extra, 16), chunk)

    bias0 = weights[0, BIAS_ROW : BIAS_ROW + 16].astype(F32)[0:1]
    bias1 = weights[1, BIAS_ROW : BIAS_ROW + 16].astype(F32)[0:1]

    @pl.loop(0, AREA // chunk)
    def _(i):
        base = i * chunk
        total = bias0
        for a in range(3):
            total = total + dot(cols_a[rows_at(base, a * shift0), :], first[a], NT)
        pre0[rows_at(base), :] = total
        bottle = jnp.maximum(total, 0.0).astype(BF16)
        bottle0[rows_at(base), :] = bottle
        branch_sum = (own_f[rows_at(base), :] + dot(bottle, proj_pad[...])).astype(BF16)
        work_f[rows_at(base), :] = branch_sum.astype(F32)

    turn(work_f, sum_t)
    mirror_start(sum_t, sum_m, 0)

    mirror_wait(cot_t, cot_m, 1)

    @pl.loop(0, AREA // chunk)
    def _(i):
        at = rows_at(i * chunk)
        branch = ((cot[at, :].astype(F32) + cot_m[at, :].astype(F32)) * 0.5).astype(BF16)
        branch1[at, :] = branch
        grad_bot[at, :] = dot(branch, proj_twice[1], NT)

    mirror_wait(sum_t, sum_m, 0)

    @pl.loop(0, AREA // chunk)
    def _(i):
        at = rows_at(i * chunk)
        sym = ((work_f[at, :] + sum_m[at, :].astype(F32)) * 0.5).astype(BF16)
        live = jnp.maximum(sym, jnp.zeros_like(sym))
        hidden1[at, :] = live
        work_f[at, :] = live.astype(F32)

    pack_wide(work_f, hid_e, hid_c)
    halo1 = (1, wide_sources(hidden1, hid_e, hid_c), recv_e1, recv_c1)
    halo_start(*halo1)
    fill_centre(work_f, pad_8, D1, same)

    halo_wait(*halo1)

    pl.semaphore_signal(partner, inc=1, device_id=sibling, device_id_type=MESH)

    unpack_wide(recv_e1, recv_c1, pad_8)
    spread(pad_8, cols_8, D1)

    @pl.loop(0, AREA // chunk)
    def _(i):
        base = i * chunk
        total = bias1
        for a in range(3):
            total = total + dot(cols_8[rows_at(base, a * shift1), :], second[a], NT)
        bottle1[rows_at(base), :] = jnp.maximum(total, 0.0).astype(BF16)
        grad = jnp.where(total > 0, grad_bot[rows_at(base), :], 0.0)
        work_f[rows_at(base), :] = grad
        gp1[rows_at(base), :] = grad.astype(BF16)

    pack_wide(work_f, gp1_e, gp1_c)
    halo2 = (2, wide_sources(gp1, gp1_e, gp1_c), recv_e2, recv_c2)
    halo_start(*halo2)

    ones = jnp.ones((AREA, C), BF16)

    def weight_gradients(s, grad_pre, cols, shift, bottle, branch):
        turned_grad = grad_pre[...].T[0:K]
        for a in range(3):
            product = dot(turned_grad, cols[a * shift : a * shift + AREA, :])
            for b in range(3):
                at = (3 * a + b) * K
                grads[s, at : at + K] = product[:, b * C : (b + 1) * C].astype(BF16)
        grads[s, 9 * K : 10 * K] = dot(bottle[...].T[0:K], branch[...]).astype(BF16)
        grads[s, 10 * K : 11 * K] = dot(turned_grad, ones).astype(BF16)
        grads[s, 11 * K : 12 * K] = jnp.zeros((K, C), BF16)

    def piece_at(index):
        return pl.ds(pl.multiple_of(index * piece, 16), piece)

    slot_me = seg * n + plane_me

    def group_copy(src, dst, send_sem, recv_sem, device):
        return pltpu.make_async_remote_copy(
            src_ref=src, dst_ref=dst, send_sem=send_sem, recv_sem=recv_sem, device_id=device, device_id_type=MESH
        )

    def plane_copy(s, step):
        return group_copy(
            grads.at[s, piece_at(plane_index(step))],
            plane_recv.at[slot_me],
            plane_send_sem.at[s, step],
            plane_recv_sem.at[slot_me],
            plane_peer(s, step),
        )

    def plane_start(s):
        for step in plane_steps:
            plane_copy(s, step).start()

        @pl.when(seg != s)
        def _():
            plane_copy(s, 0).start()

        @pl.when(seg == s)
        def _():
            plane_recv[slot_me] = grads[s, piece_at(plane_me), :]

    def plane_sent(s):
        for step in plane_steps:
            plane_copy(s, step).wait_send()

        @pl.when(seg != s)
        def _():
            plane_copy(s, 0).wait_send()

    def arrive(dst, send_sem, recv_sem, index):
        group_copy(dst.at[index], dst.at[index], send_sem, recv_sem.at[index], sibling).wait_recv()

    def plane_wait():
        @pl.loop(1, 2 * n)
        def _(step):
            arrive(plane_recv, plane_send_sem.at[0, 0], plane_recv_sem, (slot_me + step) % (2 * n))

    def near_copy(step):
        mine = near_recv.at[row_hi]
        return group_copy(mine, mine, near_send_sem.at[step], near_recv_sem.at[row_hi], near_peer(step))

    def far_copy(step):
        mine = far_recv.at[col_hi]
        return group_copy(mine, mine, far_send_sem.at[step], far_recv_sem.at[col_hi], far_peer(step))

    def all_copy(step):
        mine = total_recv.at[plane_me]
        return group_copy(mine, mine, all_send_sem.at[step], all_recv_sem.at[plane_me], plane_peer(seg, step))

    def add_up(buffer, count):
        total = buffer[0].astype(F32)
        for i in range(1, count):
            total = total + buffer[i].astype(F32)
        return total

    def near_start():
        plane_wait()
        near_recv[row_hi] = add_up(plane_recv, 2 * n).astype(BF16)
        for step in range(1, part):
            near_copy(step).start()

    def far_start():
        for step in range(1, part):
            arrive(near_recv, near_send_sem.at[step], near_recv_sem, (row_hi + step) % part)
        far_recv[col_hi] = add_up(near_recv, part).astype(BF16)
        for step in range(1, part):
            far_copy(step).start()

    weight_gradients(1, gp1, cols_8, shift1, bottle1, branch1)
    pl.semaphore_wait(partner, 1)
    plane_start(1)
    fill_centre(work_f, pad_9, D1, same)

    halo_wait(*halo2)

    unpack_wide(recv_e2, recv_c2, pad_9)
    spread(pad_9, cols_g, D1)

    @pl.loop(0, AREA // chunk)
    def _(i):
        base = i * chunk
        total = None
        for a in range(3):
            term = dot(cols_g[rows_at(base, a * shift1), :], back1[a])
            total = term if total is None else total + term
        branch = branch1[rows_at(base), :].astype(F32)
        live = hidden1[rows_at(base), :].astype(F32) > 0
        own = (branch + jnp.where(live, total[:, 0:C], 0.0)).astype(BF16).astype(F32)
        turned = (branch + jnp.where(live, total[:, C : 2 * C], 0.0)).astype(BF16).astype(F32)
        mean = ((own + turned) * 0.5).astype(BF16)
        branch0[rows_at(base), :] = mean
        grad = jnp.where(pre0[rows_at(base), :] > 0, dot(mean, proj_twice[0], NT), 0.0)
        work_f[rows_at(base), :] = grad
        gp0[rows_at(base), :] = grad.astype(BF16)

    weight_gradients(0, gp0, cols_a, shift0, bottle0, branch0)

    plane_start(0)

    pack_narrow(work_f, gp0_e, gp0_c)
    sources3 = tuple(gp0_e.at[k] for k in range(4)) + tuple(gp0_c.at[k] for k in range(4))
    halo3 = (3, sources3, recv_e3, recv_c3)
    halo_start(*halo3)
    fill_centre(work_f, pad_a, D0, same)

    near_start()

    far_start()

    halo_wait(*halo3)

    unpack_narrow(recv_e3, recv_c3, pad_a, same)
    spread(pad_a, cols_b, D0)

    @pl.loop(0, AREA // chunk)
    def _(i):
        base = i * chunk
        total = None
        for a in range(3):
            term = dot(cols_b[rows_at(base, a * shift0), :], back0[a])
            total = term if total is None else total + term
        branch = branch0[rows_at(base), :].astype(F32)
        live = own_f[rows_at(base), :] > 0
        out_grad[rows_at(base), :] = (branch + jnp.where(live, total, 0.0)).astype(BF16)

    pl.when(off_diagonal)(lambda: mirror_copy(sum_t, sum_m, 0).wait_send())
    pl.when(off_diagonal)(lambda: mirror_copy(cot_t, cot_m, 1).wait_send())
    weights_copy.wait_send()
    for halo in (halo0, halo1, halo2, halo3):
        halo_sent(*halo)
    plane_sent(0)
    plane_sent(1)

    for step in range(1, part):
        arrive(far_recv, far_send_sem.at[step], far_recv_sem, (col_hi + step) % part)

    total_recv[plane_me] = add_up(far_recv, part).astype(BF16)
    for step in plane_steps:
        all_copy(step).start()
    for step in range(1, part):
        near_copy(step).wait_send()
        far_copy(step).wait_send()

    @pl.loop(1, n)
    def _(step):
        arrive(total_recv, all_send_sem.at[step], all_recv_sem, (plane_me + step) % n)

    for step in plane_steps:
        all_copy(step).wait_send()


def write(factor, grad, total, out_grad, out_conv, out_bias, out_proj, sums, bias, sems):
    first = pltpu.make_async_copy(grad, out_grad, sems.at[0])
    first.start()
    pieces, piece = total.shape[0], total.shape[1]
    for i in range(pieces):
        sums[i * piece : (i + 1) * piece] = total[i].astype(F32) * factor
    bias[...] = sums[10 * K : 11 * K].T[0:1]
    copies = [
        pltpu.make_async_copy(sums.at[0:CONV_ROWS], out_conv, sems.at[1]),
        pltpu.make_async_copy(bias, out_bias, sems.at[2]),
        pltpu.make_async_copy(sums.at[9 * K : 10 * K], out_proj, sems.at[3]),
    ]
    for copy in copies:
        copy.start()
    for copy in [first] + copies:
        copy.wait()


def solution(mesh):
    n = mesh.shape["row"]
    cells = mesh.shape["segment"] * (SIDE * n) * (SIDE * n)
    factor = float(np.float32(1.0) / np.sqrt(np.float32(cells)))
    piece = GRAD_ROWS // n
    part = int(round(n**0.5))
    vmem = pltpu.VMEM
    scratch = [
        vmem((AREA, C), BF16),
        vmem((AREA, C), BF16),
        vmem((1, K), BF16),
        vmem((2, PACK_ROWS, C), BF16),
        vmem((3, 2 * K, 3 * C), BF16),
        vmem((3, 2 * K, 3 * C), BF16),
        vmem((3, 3 * C, 2 * C), BF16),
        vmem((3, 3 * C, C), BF16),
        vmem((2 * K, C), BF16),
        vmem((2, 2 * K, C), BF16),
        vmem((AREA, C), F32),
        vmem((AREA, C), F32),
        vmem((16, C), F32),
        vmem((AREA, C), BF16),
        vmem((AREA, C), BF16),
        vmem((AREA, C), BF16),
        vmem((AREA, C), BF16),
        vmem((4, D0 * SIDE, C), BF16),
        vmem((4, 16, C), BF16),
        vmem((4, D0 * SIDE, C), BF16),
        vmem((4, 16, C), BF16),
        vmem((AREA, C), BF16),
        vmem((2, D1 * SIDE, C), BF16),
        vmem((4, D1 * D1, C), BF16),
        vmem((4, D1 * SIDE, C), BF16),
        vmem((4, D1 * D1, C), BF16),
        vmem((AREA, C), BF16),
        vmem((2, D1 * SIDE, C), BF16),
        vmem((4, D1 * D1, C), BF16),
        vmem((4, D1 * SIDE, C), BF16),
        vmem((4, D1 * D1, C), BF16),
        vmem((AREA, C), BF16),
        vmem((4, D0 * SIDE, C), BF16),
        vmem((4, 16, C), BF16),
        vmem((4, D0 * SIDE, C), BF16),
        vmem((4, 16, C), BF16),
        vmem(((SIDE + 2 * D0) * WIDE, C), F32),
        vmem(((SIDE + 2 * D1) * WIDE, C), F32),
        vmem(((SIDE + 2 * D1) * WIDE, C), F32),
        vmem(((SIDE + 2 * D0) * SIDE, 3 * C), BF16),
        vmem(((SIDE + 2 * D0) * SIDE, 3 * C), BF16),
        vmem(((SIDE + 2 * D1) * SIDE, 3 * C), BF16),
        vmem(((SIDE + 2 * D1) * SIDE, 3 * C), BF16),
        vmem((AREA, C), F32),
        vmem((AREA, C), BF16),
        vmem((AREA, C), F32),
        vmem((AREA, C), BF16),
        vmem((AREA, C), BF16),
        vmem((AREA, C), BF16),
        vmem((2, GRAD_ROWS, C), BF16),
        vmem((2 * n, piece, C), BF16),
        vmem((part, piece, C), BF16),
        vmem((part, piece, C), BF16),
        pltpu.SemaphoreType.DMA((4, 8)),
        pltpu.SemaphoreType.DMA((4, 8)),
        pltpu.SemaphoreType.DMA((4,)),
        pltpu.SemaphoreType.DMA((4,)),
        pltpu.SemaphoreType.DMA((2, n)),
        pltpu.SemaphoreType.DMA((2 * n,)),
    ] + [pltpu.SemaphoreType.DMA((part,))] * 4 + [pltpu.SemaphoreType.DMA((n,))] * 2
    scratch += [pltpu.SemaphoreType.REGULAR, pltpu.SemaphoreType.DMA((5,))]

    call = pl.pallas_call(
        functools.partial(kernel, n),
        out_shape=(
            jax.ShapeDtypeStruct((AREA, C), BF16),
            jax.ShapeDtypeStruct((n, piece, C), BF16),
        ),
        in_specs=[pl.BlockSpec(memory_space=pltpu.HBM)] * 5,
        out_specs=[pl.BlockSpec(memory_space=pltpu.VMEM)] * 2,
        scratch_shapes=scratch,
        compiler_params=pltpu.CompilerParams(
            collective_id=0, has_side_effects=True, vmem_limit_bytes=40 * 1024 * 1024
        ),
        name="trunk",
    )

    finish = pl.pallas_call(
        functools.partial(write, factor),
        out_shape=(
            jax.ShapeDtypeStruct((AREA, C), BF16),
            jax.ShapeDtypeStruct((CONV_ROWS, C), F32),
            jax.ShapeDtypeStruct((1, K), F32),
            jax.ShapeDtypeStruct((K, C), F32),
        ),
        in_specs=[pl.BlockSpec(memory_space=pltpu.VMEM)] * 2,
        out_specs=[pl.BlockSpec(memory_space=pltpu.HBM)] * 4,
        scratch_shapes=[vmem((GRAD_ROWS, C), F32), vmem((1, K), F32), pltpu.SemaphoreType.DMA((4,))],
        compiler_params=pltpu.CompilerParams(vmem_limit_bytes=8 * 1024 * 1024),
        name="outputs",
    )

    def local(activations, cotangent, conv_weight, conv_bias, out_weight):
        held = [
            pltpu.with_memory_space_constraint(x, pltpu.HBM)
            for x in (
                activations.reshape(AREA, C),
                cotangent.reshape(AREA, C),
                jnp.swapaxes(conv_weight, 2, 3).reshape(CONV_ROWS, C),
                conv_bias,
                out_weight.reshape(K, C),
            )
        ]
        grad, conv, bias, proj = finish(*call(*held))
        return (
            grad.reshape(1, SIDE, SIDE, C),
            jnp.swapaxes(conv.reshape(1, 9, K, C), 2, 3),
            bias,
            proj.reshape(1, K, C),
        )

    in_specs = (
        P("segment", "row", "col", None),
        P("segment", "row", "col", None),
        P("segment", None, None, None),
        P("segment", None),
        P("segment", None, None),
    )
    out_specs = (
        P("segment", "row", "col", None),
        P("segment", None, None, None),
        P("segment", None),
        P("segment", None, None),
    )
    return jax.shard_map(local, mesh=mesh, in_specs=in_specs, out_specs=out_specs, check_vma=False)
```

```python
import functools

import numpy as np

import jax
import jax.numpy as jnp
from jax import lax
from jax.experimental import pallas as pl
from jax.experimental.pallas import tpu as pltpu
from jax.sharding import PartitionSpec as P

MESH = pl.DeviceIdType.MESH
F32 = jnp.float32
BF16 = jnp.bfloat16

SIDE = 24
AREA = SIDE * SIDE
C = 128
K = 64
D0 = 2
D1 = 8
WIDE = 40
CONV_ROWS = 9 * K
PROJ_ROW = CONV_ROWS
BIAS_ROW = CONV_ROWS + K
PACK_ROWS = CONV_ROWS + K + 16
GRAD_BLOCKS = 12
GRAD_ROWS = GRAD_BLOCKS * K
DIRECTIONS = ((-1, 0), (1, 0), (0, -1), (0, 1), (-1, -1), (-1, 1), (1, -1), (1, 1))
OPPOSITE = (1, 0, 3, 2, 7, 6, 5, 4)
NT = (((1,), (1,)), ((), ()))
TN = (((0,), (0,)), ((), ()))


def dot(a, b, dims=(((1,), (0,)), ((), ()))):
    return lax.dot_general(a, b, dims, preferred_element_type=F32)


def kernel(
    n,
    act_in,
    cot_in,
    conv_in,
    bias_in,
    proj_in,
    out_grad,
    total_recv,
    act,
    cot,
    bias_w,
    weights,
    first,
    second,
    back1,
    back0,
    proj_pad,
    proj_twice,
    own_f,
    work_f,
    stage_f,
    sum_t,
    cot_t,
    sum_m,
    cot_m,
    send_e0,
    send_c0,
    recv_e0,
    recv_c0,
    hidden1,
    hid_e,
    hid_c,
    recv_e1,
    recv_c1,
    gp1,
    gp1_e,
    gp1_c,
    recv_e2,
    recv_c2,
    gp0,
    gp0_e,
    gp0_c,
    recv_e3,
    recv_c3,
    pad_a,
    pad_8,
    pad_9,
    cols_a,
    cols_b,
    cols_8,
    cols_g,
    pre0,
    bottle0,
    grad_bot,
    bottle1,
    branch1,
    branch0,
    grads,
    plane_recv,
    near_recv,
    far_recv,
    halo_send,
    halo_recv,
    pair_send,
    pair_recv,
    plane_send_sem,
    plane_recv_sem,
    near_send_sem,
    near_recv_sem,
    far_send_sem,
    far_recv_sem,
    all_send_sem,
    all_recv_sem,
    partner,
    input_sem,
):
    seg = lax.axis_index("segment")
    row = lax.axis_index("row")
    col = lax.axis_index("col")
    part = int(round(n**0.5))
    piece = GRAD_ROWS // n
    row_hi, row_lo = row // part, row % part
    col_hi, col_lo = col // part, col % part
    plane_me = row_lo * part + col_lo
    off_diagonal = row != col
    mirror = (seg, col, row)
    sibling = (1 - seg, row, col)

    def hops(step):
        return sum(min(d, part - d) for d in divmod(step, part))

    plane_steps = sorted(range(1, n), key=hops, reverse=True)

    def plane_peer(section, step):
        return (
            section,
            row_hi * part + (row_lo + step // part) % part,
            col_hi * part + (col_lo + step % part) % part,
        )

    def plane_index(step):
        return (row_lo + step // part) % part * part + (col_lo + step % part) % part

    def near_peer(step):
        return (seg, (row_hi + step) % part * part + row_lo, col)

    def far_peer(step):
        return (seg, row, (col_hi + step) % part * part + col_lo)

    def there(k):
        dr, dc = DIRECTIONS[k]
        r, c = row + dr, col + dc
        exists = None
        if dr:
            exists = (r >= 0) if dr < 0 else (r < n)
        if dc:
            side = (c >= 0) if dc < 0 else (c < n)
            exists = side if exists is None else jnp.logical_and(exists, side)
        return exists

    def neighbour(k):
        dr, dc = DIRECTIONS[k]
        return (seg, row + dr, col + dc)

    inputs = [
        pltpu.make_async_copy(src, dst, input_sem.at[i])
        for i, (src, dst) in enumerate(
            (
                (act_in, act),
                (cot_in, cot),
                (conv_in, weights.at[seg, 0:CONV_ROWS]),
                (proj_in, weights.at[seg, PROJ_ROW : PROJ_ROW + K]),
                (bias_in, bias_w),
            )
        )
    ]
    for copy in inputs:
        copy.start()
    barrier = pltpu.get_barrier_semaphore()

    def signal(device):
        pl.semaphore_signal(barrier, inc=1, device_id=device, device_id_type=MESH)

    greeted = jnp.int32(1 + 2 * (part - 1))
    pl.when(off_diagonal)(functools.partial(signal, mirror))
    greeted = greeted + off_diagonal.astype(jnp.int32)
    for step in range(1, part):
        signal(far_peer(step))
        signal(near_peer(step))
    for k in range(7, -1, -1):
        pl.when(there(k))(functools.partial(signal, neighbour(k)))
        greeted = greeted + there(k).astype(jnp.int32)
    signal(sibling)

    strip = D0 * SIDE
    corners_of_tile = ((0, 0), (0, SIDE - D0), (SIDE - D0, 0), (SIDE - D0, SIDE - D0))

    def pack_corners(tile, corners):
        for k, (r, c) in enumerate(corners_of_tile):
            stage_f[...] = jnp.zeros((16, C), F32)
            for i in range(D0):
                start = (r + i) * SIDE + c
                stage_f[i * D0 : (i + 1) * D0] = tile[start : start + D0]
            corners[k] = stage_f[...].astype(BF16)

    def pack_narrow(tile, edges, corners):
        edges[0] = tile[0:strip].astype(BF16)
        edges[1] = tile[AREA - strip : AREA].astype(BF16)
        for k, first_column in ((2, 0), (3, SIDE - D0)):
            columns = [tile[pl.ds(first_column + j, SIDE, stride=SIDE), :] for j in range(D0)]
            edges[k] = jnp.concatenate(columns, axis=0).astype(BF16)
        pack_corners(tile, corners)

    inputs[0].wait()
    own_f[...] = act[...].astype(F32)
    pack_narrow(own_f, send_e0, send_c0)

    pl.semaphore_wait(barrier, greeted)

    def pair_copy(src, dst, index, device):
        return pltpu.make_async_remote_copy(
            src_ref=src,
            dst_ref=dst,
            send_sem=pair_send.at[index],
            recv_sem=pair_recv.at[index],
            device_id=device,
            device_id_type=MESH,
        )

    def mirror_copy(src, dst, index):
        return pair_copy(src, dst, index, mirror)

    def mirror_start(src, dst, index):
        @pl.when(off_diagonal)
        def _():
            mirror_copy(src, dst, index).start()

        @pl.when(jnp.logical_not(off_diagonal))
        def _():
            dst[...] = src[...]

    def mirror_wait(src, dst, index):
        pl.when(off_diagonal)(lambda: mirror_copy(src, dst, index).wait_recv())

    def halo_to(phase, k, slot, device, sources, edges, corners):
        return pltpu.make_async_remote_copy(
            src_ref=sources[k],
            dst_ref=edges.at[slot] if slot < 4 else corners.at[slot - 4],
            send_sem=halo_send.at[phase, k],
            recv_sem=halo_recv.at[phase, slot],
            device_id=device,
            device_id_type=MESH,
        )

    def halo_copy(phase, k, sources, edges, corners):
        return halo_to(phase, k, OPPOSITE[k], neighbour(k), sources, edges, corners)

    def halo_start(*halo):
        for k in range(7, -1, -1):
            pl.when(there(k))(lambda k=k: halo_copy(halo[0], k, *halo[1:]).start())

    def halo_clear(phase, sources, edges, corners):
        for k in range(8):

            @pl.when(jnp.logical_not(there(k)))
            def _():
                ref = edges.at[k] if k < 4 else corners.at[k - 4]
                ref[...] = jnp.zeros_like(ref)

    def arrived(phase, k, edges, corners):
        target = edges.at[k] if k < 4 else corners.at[k - 4]
        return pltpu.make_async_remote_copy(
            src_ref=target,
            dst_ref=target,
            send_sem=halo_send.at[phase, k],
            recv_sem=halo_recv.at[phase, k],
            device_id=neighbour(k),
            device_id_type=MESH,
        )

    def halo_wait(phase, sources, edges, corners):
        for k in range(8):
            pl.when(there(k))(lambda k=k: arrived(phase, k, edges, corners).wait_recv())

    def halo_sent(*halo):
        for k in range(8):
            pl.when(there(k))(lambda k=k: halo_copy(halo[0], k, *halo[1:]).wait_send())

    sources0 = tuple(send_e0.at[k] for k in range(4)) + tuple(send_c0.at[k] for k in range(4))
    halo0 = (0, sources0, recv_e0, recv_c0)
    halo_start(*halo0)

    def turn(flat, out):
        @pl.loop(0, SIDE // 2)
        def _(i):
            two = jnp.concatenate(
                [flat[pl.ds(2 * i, SIDE, stride=SIDE), :], flat[pl.ds(2 * i + 1, SIDE, stride=SIDE), :]], axis=0
            )
            out[pl.ds(pl.multiple_of(i * 2 * SIDE, 16), 2 * SIDE), :] = two.astype(BF16)

    inputs[1].wait()
    work_f[...] = cot[...].astype(F32)
    turn(work_f, cot_t)
    mirror_start(cot_t.at[0:288], cot_m.at[0:288], 1)

    for copy in inputs[2:]:
        copy.wait()
    bias_row = bias_w[...].astype(F32)
    weights[seg, BIAS_ROW : BIAS_ROW + 16] = jnp.broadcast_to(
        jnp.concatenate([bias_row, bias_row], axis=1), (16, 2 * K)
    ).astype(BF16)
    weights_copy = pair_copy(weights.at[seg], weights.at[seg], 2, sibling)
    weights_copy.start()
    halo_clear(*halo0)
    halo_clear(1, None, recv_e1, recv_c1)
    halo_clear(2, None, recv_e2, recv_c2)
    halo_clear(3, None, recv_e3, recv_c3)

    def unpack_narrow(edges, corners, pad, change):
        north = change(edges[0].astype(F32))
        south = change(edges[1].astype(F32))
        west = change(edges[2].astype(F32))
        east = change(edges[3].astype(F32))
        for i in range(D0):
            lines = slice(i * SIDE, (i + 1) * SIDE)
            pad[i * WIDE + 8 : i * WIDE + 8 + SIDE] = north[lines]
            low = (D0 + SIDE + i) * WIDE + 8
            pad[low : low + SIDE] = south[lines]
            pad[pl.ds(D0 * WIDE + 8 - D0 + i, SIDE, stride=WIDE), :] = west[lines]
            pad[pl.ds(D0 * WIDE + 8 + SIDE + i, SIDE, stride=WIDE), :] = east[lines]
        for k, (r, c) in enumerate(((0, 8 - D0), (0, 8 + SIDE), (D0 + SIDE, 8 - D0), (D0 + SIDE, 8 + SIDE))):
            stage_f[...] = change(corners[k].astype(F32))
            for i in range(D0):
                start = (r + i) * WIDE + c
                pad[start : start + D0] = stage_f[i * D0 : (i + 1) * D0]

    def fill_centre(tile, pad, dilation, change):
        for i in range(SIDE):
            start = (dilation + i) * WIDE + 8
            pad[start : start + SIDE] = change(tile[i * SIDE : (i + 1) * SIDE])

    def pack_wide(tile, edges, corners):
        for k, first in ((0, 0), (1, SIDE - D1)):
            edges[k] = jnp.concatenate(
                [tile[i * SIDE + first : i * SIDE + first + D1] for i in range(SIDE)], axis=0
            ).astype(BF16)
        for k, (r, c) in enumerate(((0, 0), (0, SIDE - D1), (SIDE - D1, 0), (SIDE - D1, SIDE - D1))):
            corners[k] = jnp.concatenate(
                [tile[(r + i) * SIDE + c : (r + i) * SIDE + c + D1] for i in range(D1)], axis=0
            ).astype(BF16)

    def wide_sources(flat, edges, corners):
        lines = D1 * SIDE
        return (
            flat.at[0:lines],
            flat.at[AREA - lines : AREA],
            edges.at[0],
            edges.at[1],
        ) + tuple(corners.at[k] for k in range(4))

    def unpack_wide(edges, corners, pad):
        north = edges[0].astype(F32)
        south = edges[1].astype(F32)
        west = edges[2].astype(F32)
        east = edges[3].astype(F32)
        for i in range(D1):
            lines = slice(i * SIDE, (i + 1) * SIDE)
            pad[i * WIDE + D1 : i * WIDE + D1 + SIDE] = north[lines]
            low = (D1 + SIDE + i) * WIDE + D1
            pad[low : low + SIDE] = south[lines]
        for i in range(SIDE):
            lines = slice(i * D1, (i + 1) * D1)
            start = (D1 + i) * WIDE
            pad[start : start + D1] = west[lines]
            pad[start + D1 + SIDE : start + WIDE] = east[lines]
        for k, (r, c) in enumerate(((0, 0), (0, D1 + SIDE), (D1 + SIDE, 0), (D1 + SIDE, D1 + SIDE))):
            corner = corners[k].astype(F32)
            for i in range(D1):
                start = (r + i) * WIDE + c
                pad[start : start + D1] = corner[i * D1 : (i + 1) * D1]

    def spread(pad, cols, dilation):
        for b in range(3):
            first = 8 + (b - 1) * dilation
            for i in range(0, SIDE + 2 * dilation, 2):
                two = jnp.concatenate(
                    [pad[(i + h) * WIDE + first : (i + h) * WIDE + first + SIDE] for h in range(2)], axis=0
                )
                cols[i * SIDE : (i + 2) * SIDE, b * C : (b + 1) * C] = two.astype(BF16)

    same = lambda x: x
    relu = lambda x: jnp.maximum(x, 0.0)

    fill_centre(own_f, pad_a, D0, relu)
    for ref in (first, back1, back0, proj_pad):
        ref[...] = jnp.zeros_like(ref)
    weights_copy.wait_recv()

    proj_pad[0:K] = weights[0, PROJ_ROW : PROJ_ROW + K]
    for s in range(2):
        for h in range(2):
            proj_twice[s, h * K : (h + 1) * K] = weights[s, PROJ_ROW : PROJ_ROW + K]
    tap = lambda a, b: slice((3 * a + b) * K, (3 * a + b + 1) * K)
    for a in range(3):
        for b in range(3):
            lanes = slice(b * C, (b + 1) * C)
            own, turned = slice(b * C, b * C + K), slice(b * C + K, (b + 1) * C)
            first[a, 0:K, lanes] = weights[0, tap(a, b)]
            second[a, 0:K, lanes] = weights[1, tap(a, b)]
            second[a, K : 2 * K, lanes] = weights[1, tap(b, a)]
            back0[a, own] = weights[0, tap(2 - a, 2 - b)]
            back1[a, own, 0:C] = weights[1, tap(2 - a, 2 - b)]
            back1[a, turned, C : 2 * C] = weights[1, tap(2 - b, 2 - a)]

    halo_wait(*halo0)
    unpack_narrow(recv_e0, recv_c0, pad_a, relu)
    spread(pad_a, cols_a, D0)

    chunk = 192
    shift0 = D0 * SIDE
    shift1 = D1 * SIDE

    def rows_at(base, extra=0):
        return pl.ds(pl.multiple_of(base + extra, 16), chunk)

    bias0 = weights[0, BIAS_ROW : BIAS_ROW + 16].astype(F32)[0:1]
    bias1 = weights[1, BIAS_ROW : BIAS_ROW + 16].astype(F32)[0:1]

    @pl.loop(0, AREA // chunk)
    def _(i):
        base = i * chunk
        total = bias0
        for a in range(3):
            total = total + dot(cols_a[rows_at(base, a * shift0), :], first[a], NT)
        pre0[rows_at(base), :] = total
        bottle = jnp.maximum(total, 0.0).astype(BF16)
        bottle0[rows_at(base), :] = bottle
        branch_sum = (own_f[rows_at(base), :] + dot(bottle, proj_pad[...])).astype(BF16)
        work_f[rows_at(base), :] = branch_sum.astype(F32)

    turn(work_f, sum_t)
    mirror_start(sum_t, sum_m, 0)
    mirror_start(cot_t.at[288:AREA], cot_m.at[288:AREA], 3)

    mirror_wait(sum_t, sum_m, 0)

    @pl.loop(0, AREA // chunk)
    def _(i):
        at = rows_at(i * chunk)
        sym = ((work_f[at, :] + sum_m[at, :].astype(F32)) * 0.5).astype(BF16)
        live = jnp.maximum(sym, jnp.zeros_like(sym))
        hidden1[at, :] = live
        work_f[at, :] = live.astype(F32)

    pack_wide(work_f, hid_e, hid_c)
    halo1 = (1, wide_sources(hidden1, hid_e, hid_c), recv_e1, recv_c1)
    halo_start(*halo1)
    fill_centre(work_f, pad_8, D1, same)

    mirror_wait(cot_t.at[0:288], cot_m.at[0:288], 1)
    mirror_wait(cot_t.at[288:AREA], cot_m.at[288:AREA], 3)

    @pl.loop(0, AREA // chunk)
    def _(i):
        at = rows_at(i * chunk)
        branch = ((cot[at, :].astype(F32) + cot_m[at, :].astype(F32)) * 0.5).astype(BF16)
        branch1[at, :] = branch
        grad_bot[at, :] = dot(branch, proj_twice[1], NT)

    halo_wait(*halo1)

    pl.semaphore_signal(partner, inc=1, device_id=sibling, device_id_type=MESH)

    unpack_wide(recv_e1, recv_c1, pad_8)
    spread(pad_8, cols_8, D1)

    @pl.loop(0, AREA // chunk)
    def _(i):
        base = i * chunk
        total = bias1
        for a in range(3):
            total = total + dot(cols_8[rows_at(base, a * shift1), :], second[a], NT)
        bottle1[rows_at(base), :] = jnp.maximum(total, 0.0).astype(BF16)
        grad = jnp.where(total > 0, grad_bot[rows_at(base), :], 0.0)
        work_f[rows_at(base), :] = grad
        gp1[rows_at(base), :] = grad.astype(BF16)

    pack_wide(work_f, gp1_e, gp1_c)
    halo2 = (2, wide_sources(gp1, gp1_e, gp1_c), recv_e2, recv_c2)
    halo_start(*halo2)

    ones = jnp.ones((AREA, C), BF16)

    def weight_gradients(s, grad_pre, cols, shift, bottle, branch):
        turned_grad = grad_pre[...].T[0:K]
        for a in range(3):
            product = dot(turned_grad, cols[a * shift : a * shift + AREA, :])
            for b in range(3):
                at = (3 * a + b) * K
                grads[s, at : at + K] = product[:, b * C : (b + 1) * C].astype(BF16)
        grads[s, 9 * K : 10 * K] = dot(bottle[...].T[0:K], branch[...]).astype(BF16)
        grads[s, 10 * K : 11 * K] = dot(turned_grad, ones).astype(BF16)
        grads[s, 11 * K : 12 * K] = jnp.zeros((K, C), BF16)

    def piece_at(index):
        return pl.ds(pl.multiple_of(index * piece, 16), piece)

    slot_me = seg * n + plane_me

    def group_copy(src, dst, send_sem, recv_sem, device):
        return pltpu.make_async_remote_copy(
            src_ref=src, dst_ref=dst, send_sem=send_sem, recv_sem=recv_sem, device_id=device, device_id_type=MESH
        )

    def plane_copy(s, step):
        return group_copy(
            grads.at[s, piece_at(plane_index(step))],
            plane_recv.at[slot_me],
            plane_send_sem.at[s, step],
            plane_recv_sem.at[slot_me],
            plane_peer(s, step),
        )

    def plane_start(s):
        for step in plane_steps:
            plane_copy(s, step).start()

        @pl.when(seg != s)
        def _():
            plane_copy(s, 0).start()

        @pl.when(seg == s)
        def _():
            plane_recv[slot_me] = grads[s, piece_at(plane_me), :]

    def plane_sent(s):
        for step in plane_steps:
            plane_copy(s, step).wait_send()

        @pl.when(seg != s)
        def _():
            plane_copy(s, 0).wait_send()

    def arrive(dst, send_sem, recv_sem, index):
        group_copy(dst.at[index], dst.at[index], send_sem, recv_sem.at[index], sibling).wait_recv()

    def plane_wait():
        @pl.loop(1, 2 * n)
        def _(step):
            arrive(plane_recv, plane_send_sem.at[0, 0], plane_recv_sem, (slot_me + step) % (2 * n))

    def near_copy(step):
        mine = near_recv.at[row_hi]
        return group_copy(mine, mine, near_send_sem.at[step], near_recv_sem.at[row_hi], near_peer(step))

    def far_copy(step):
        mine = far_recv.at[col_hi]
        return group_copy(mine, mine, far_send_sem.at[step], far_recv_sem.at[col_hi], far_peer(step))

    def all_copy(step):
        mine = total_recv.at[plane_me]
        return group_copy(mine, mine, all_send_sem.at[step], all_recv_sem.at[plane_me], plane_peer(seg, step))

    def add_up(buffer, count):
        total = buffer[0].astype(F32)
        for i in range(1, count):
            total = total + buffer[i].astype(F32)
        return total

    def near_start():
        plane_wait()
        near_recv[row_hi] = add_up(plane_recv, 2 * n).astype(BF16)
        for step in range(1, part):
            near_copy(step).start()

    def far_start():
        for step in range(1, part):
            arrive(near_recv, near_send_sem.at[step], near_recv_sem, (row_hi + step) % part)
        far_recv[col_hi] = add_up(near_recv, part).astype(BF16)
        for step in range(1, part):
            far_copy(step).start()

    weight_gradients(1, gp1, cols_8, shift1, bottle1, branch1)
    pl.semaphore_wait(partner, 1)
    plane_start(1)
    fill_centre(work_f, pad_9, D1, same)

    halo_wait(*halo2)

    unpack_wide(recv_e2, recv_c2, pad_9)
    spread(pad_9, cols_g, D1)

    @pl.loop(0, AREA // chunk)
    def _(i):
        base = i * chunk
        total = None
        for a in range(3):
            term = dot(cols_g[rows_at(base, a * shift1), :], back1[a])
            total = term if total is None else total + term
        branch = branch1[rows_at(base), :].astype(F32)
        live = hidden1[rows_at(base), :].astype(F32) > 0
        own = (branch + jnp.where(live, total[:, 0:C], 0.0)).astype(BF16).astype(F32)
        turned = (branch + jnp.where(live, total[:, C : 2 * C], 0.0)).astype(BF16).astype(F32)
        mean = ((own + turned) * 0.5).astype(BF16)
        branch0[rows_at(base), :] = mean
        grad = jnp.where(pre0[rows_at(base), :] > 0, dot(mean, proj_twice[0], NT), 0.0)
        work_f[rows_at(base), :] = grad
        gp0[rows_at(base), :] = grad.astype(BF16)

    weight_gradients(0, gp0, cols_a, shift0, bottle0, branch0)

    plane_start(0)

    pack_narrow(work_f, gp0_e, gp0_c)
    sources3 = tuple(gp0_e.at[k] for k in range(4)) + tuple(gp0_c.at[k] for k in range(4))
    halo3 = (3, sources3, recv_e3, recv_c3)
    halo_start(*halo3)
    fill_centre(work_f, pad_a, D0, same)

    near_start()

    far_start()

    halo_wait(*halo3)

    unpack_narrow(recv_e3, recv_c3, pad_a, same)
    spread(pad_a, cols_b, D0)

    @pl.loop(0, AREA // chunk)
    def _(i):
        base = i * chunk
        total = None
        for a in range(3):
            term = dot(cols_b[rows_at(base, a * shift0), :], back0[a])
            total = term if total is None else total + term
        branch = branch0[rows_at(base), :].astype(F32)
        live = own_f[rows_at(base), :] > 0
        out_grad[rows_at(base), :] = (branch + jnp.where(live, total, 0.0)).astype(BF16)

    pl.when(off_diagonal)(lambda: mirror_copy(sum_t, sum_m, 0).wait_send())
    pl.when(off_diagonal)(lambda: mirror_copy(cot_t.at[0:288], cot_m.at[0:288], 1).wait_send())
    pl.when(off_diagonal)(lambda: mirror_copy(cot_t.at[288:AREA], cot_m.at[288:AREA], 3).wait_send())
    weights_copy.wait_send()
    for halo in (halo0, halo1, halo2, halo3):
        halo_sent(*halo)
    plane_sent(0)
    plane_sent(1)

    for step in range(1, part):
        arrive(far_recv, far_send_sem.at[step], far_recv_sem, (col_hi + step) % part)

    total_recv[plane_me] = add_up(far_recv, part).astype(BF16)
    for step in plane_steps:
        all_copy(step).start()
    for step in range(1, part):
        near_copy(step).wait_send()
        far_copy(step).wait_send()

    @pl.loop(1, n)
    def _(step):
        arrive(total_recv, all_send_sem.at[step], all_recv_sem, (plane_me + step) % n)

    for step in plane_steps:
        all_copy(step).wait_send()


def write(factor, grad, total, out_grad, out_conv, out_bias, out_proj, sums, bias, sems):
    first = pltpu.make_async_copy(grad, out_grad, sems.at[0])
    first.start()
    pieces, piece = total.shape[0], total.shape[1]
    for i in range(pieces):
        sums[i * piece : (i + 1) * piece] = total[i].astype(F32) * factor
    bias[...] = sums[10 * K : 11 * K].T[0:1]
    copies = [
        pltpu.make_async_copy(sums.at[0:CONV_ROWS], out_conv, sems.at[1]),
        pltpu.make_async_copy(bias, out_bias, sems.at[2]),
        pltpu.make_async_copy(sums.at[9 * K : 10 * K], out_proj, sems.at[3]),
    ]
    for copy in copies:
        copy.start()
    for copy in [first] + copies:
        copy.wait()


def solution(mesh):
    n = mesh.shape["row"]
    cells = mesh.shape["segment"] * (SIDE * n) * (SIDE * n)
    factor = float(np.float32(1.0) / np.sqrt(np.float32(cells)))
    piece = GRAD_ROWS // n
    part = int(round(n**0.5))
    vmem = pltpu.VMEM
    scratch = [
        vmem((AREA, C), BF16),
        vmem((AREA, C), BF16),
        vmem((1, K), BF16),
        vmem((2, PACK_ROWS, C), BF16),
        vmem((3, 2 * K, 3 * C), BF16),
        vmem((3, 2 * K, 3 * C), BF16),
        vmem((3, 3 * C, 2 * C), BF16),
        vmem((3, 3 * C, C), BF16),
        vmem((2 * K, C), BF16),
        vmem((2, 2 * K, C), BF16),
        vmem((AREA, C), F32),
        vmem((AREA, C), F32),
        vmem((16, C), F32),
        vmem((AREA, C), BF16),
        vmem((AREA, C), BF16),
        vmem((AREA, C), BF16),
        vmem((AREA, C), BF16),
        vmem((4, D0 * SIDE, C), BF16),
        vmem((4, 16, C), BF16),
        vmem((4, D0 * SIDE, C), BF16),
        vmem((4, 16, C), BF16),
        vmem((AREA, C), BF16),
        vmem((2, D1 * SIDE, C), BF16),
        vmem((4, D1 * D1, C), BF16),
        vmem((4, D1 * SIDE, C), BF16),
        vmem((4, D1 * D1, C), BF16),
        vmem((AREA, C), BF16),
        vmem((2, D1 * SIDE, C), BF16),
        vmem((4, D1 * D1, C), BF16),
        vmem((4, D1 * SIDE, C), BF16),
        vmem((4, D1 * D1, C), BF16),
        vmem((AREA, C), BF16),
        vmem((4, D0 * SIDE, C), BF16),
        vmem((4, 16, C), BF16),
        vmem((4, D0 * SIDE, C), BF16),
        vmem((4, 16, C), BF16),
        vmem(((SIDE + 2 * D0) * WIDE, C), F32),
        vmem(((SIDE + 2 * D1) * WIDE, C), F32),
        vmem(((SIDE + 2 * D1) * WIDE, C), F32),
        vmem(((SIDE + 2 * D0) * SIDE, 3 * C), BF16),
        vmem(((SIDE + 2 * D0) * SIDE, 3 * C), BF16),
        vmem(((SIDE + 2 * D1) * SIDE, 3 * C), BF16),
        vmem(((SIDE + 2 * D1) * SIDE, 3 * C), BF16),
        vmem((AREA, C), F32),
        vmem((AREA, C), BF16),
        vmem((AREA, C), F32),
        vmem((AREA, C), BF16),
        vmem((AREA, C), BF16),
        vmem((AREA, C), BF16),
        vmem((2, GRAD_ROWS, C), BF16),
        vmem((2 * n, piece, C), BF16),
        vmem((part, piece, C), BF16),
        vmem((part, piece, C), BF16),
        pltpu.SemaphoreType.DMA((4, 8)),
        pltpu.SemaphoreType.DMA((4, 8)),
        pltpu.SemaphoreType.DMA((4,)),
        pltpu.SemaphoreType.DMA((4,)),
        pltpu.SemaphoreType.DMA((2, n)),
        pltpu.SemaphoreType.DMA((2 * n,)),
    ] + [pltpu.SemaphoreType.DMA((part,))] * 4 + [pltpu.SemaphoreType.DMA((n,))] * 2
    scratch += [pltpu.SemaphoreType.REGULAR, pltpu.SemaphoreType.DMA((5,))]

    call = pl.pallas_call(
        functools.partial(kernel, n),
        out_shape=(
            jax.ShapeDtypeStruct((AREA, C), BF16),
            jax.ShapeDtypeStruct((n, piece, C), BF16),
        ),
        in_specs=[pl.BlockSpec(memory_space=pltpu.HBM)] * 5,
        out_specs=[pl.BlockSpec(memory_space=pltpu.VMEM)] * 2,
        scratch_shapes=scratch,
        compiler_params=pltpu.CompilerParams(
            collective_id=0, has_side_effects=True, vmem_limit_bytes=40 * 1024 * 1024
        ),
        name="trunk",
    )

    finish = pl.pallas_call(
        functools.partial(write, factor),
        out_shape=(
            jax.ShapeDtypeStruct((AREA, C), BF16),
            jax.ShapeDtypeStruct((CONV_ROWS, C), F32),
            jax.ShapeDtypeStruct((1, K), F32),
            jax.ShapeDtypeStruct((K, C), F32),
        ),
        in_specs=[pl.BlockSpec(memory_space=pltpu.VMEM)] * 2,
        out_specs=[pl.BlockSpec(memory_space=pltpu.HBM)] * 4,
        scratch_shapes=[vmem((GRAD_ROWS, C), F32), vmem((1, K), F32), pltpu.SemaphoreType.DMA((4,))],
        compiler_params=pltpu.CompilerParams(vmem_limit_bytes=8 * 1024 * 1024),
        name="outputs",
    )

    def local(activations, cotangent, conv_weight, conv_bias, out_weight):
        held = [
            pltpu.with_memory_space_constraint(x, pltpu.HBM)
            for x in (
                activations.reshape(AREA, C),
                cotangent.reshape(AREA, C),
                jnp.swapaxes(conv_weight, 2, 3).reshape(CONV_ROWS, C),
                conv_bias,
                out_weight.reshape(K, C),
            )
        ]
        grad, conv, bias, proj = finish(*call(*held))
        return (
            grad.reshape(1, SIDE, SIDE, C),
            jnp.swapaxes(conv.reshape(1, 9, K, C), 2, 3),
            bias,
            proj.reshape(1, K, C),
        )

    in_specs = (
        P("segment", "row", "col", None),
        P("segment", "row", "col", None),
        P("segment", None, None, None),
        P("segment", None),
        P("segment", None, None),
    )
    out_specs = (
        P("segment", "row", "col", None),
        P("segment", None, None, None),
        P("segment", None),
        P("segment", None, None),
    )
    return jax.shard_map(local, mesh=mesh, in_specs=in_specs, out_specs=out_specs, check_vma=False)
```

```python
import functools

import numpy as np

import jax
import jax.numpy as jnp
from jax import lax
from jax.experimental import pallas as pl
from jax.experimental.pallas import tpu as pltpu
from jax.sharding import PartitionSpec as P

MESH = pl.DeviceIdType.MESH
F32 = jnp.float32
BF16 = jnp.bfloat16

SIDE = 24
AREA = SIDE * SIDE
C = 128
K = 64
D0 = 2
D1 = 8
WIDE = 40
CONV_ROWS = 9 * K
PROJ_ROW = CONV_ROWS
BIAS_ROW = CONV_ROWS + K
PACK_ROWS = CONV_ROWS + K + 16
GRAD_BLOCKS = 12
GRAD_ROWS = GRAD_BLOCKS * K
DIRECTIONS = ((-1, 0), (1, 0), (0, -1), (0, 1), (-1, -1), (-1, 1), (1, -1), (1, 1))
OPPOSITE = (1, 0, 3, 2, 7, 6, 5, 4)
NT = (((1,), (1,)), ((), ()))
TN = (((0,), (0,)), ((), ()))


def dot(a, b, dims=(((1,), (0,)), ((), ()))):
    return lax.dot_general(a, b, dims, preferred_element_type=F32)


def kernel(
    n,
    act_in,
    cot_in,
    conv_in,
    bias_in,
    proj_in,
    out_grad,
    total_recv,
    act,
    cot,
    bias_w,
    weights,
    first,
    second,
    back1,
    back0,
    proj_pad,
    proj_twice,
    own_f,
    work_f,
    stage_f,
    sum_t,
    cot_t,
    sum_m,
    cot_m,
    send_e0,
    send_c0,
    recv_e0,
    recv_c0,
    hidden1,
    hid_e,
    hid_c,
    recv_e1,
    recv_c1,
    gp1,
    gp1_e,
    gp1_c,
    recv_e2,
    recv_c2,
    gp0,
    gp0_e,
    gp0_c,
    recv_e3,
    recv_c3,
    pad_a,
    pad_8,
    pad_9,
    cols_a,
    cols_b,
    cols_8,
    cols_g,
    pre0,
    bottle0,
    grad_bot,
    bottle1,
    branch1,
    branch0,
    grads,
    plane_recv,
    near_recv,
    far_recv,
    halo_send,
    halo_recv,
    pair_send,
    pair_recv,
    plane_send_sem,
    plane_recv_sem,
    near_send_sem,
    near_recv_sem,
    far_send_sem,
    far_recv_sem,
    all_send_sem,
    all_recv_sem,
    partner,
    input_sem,
):
    seg = lax.axis_index("segment")
    row = lax.axis_index("row")
    col = lax.axis_index("col")
    part = int(round(n**0.5))
    piece = GRAD_ROWS // n
    row_hi, row_lo = row // part, row % part
    col_hi, col_lo = col // part, col % part
    plane_me = row_lo * part + col_lo
    off_diagonal = row != col
    short = jnp.logical_and(row_hi - col_hi <= 1, col_hi - row_hi <= 1)
    mirror = (seg, col, row)
    sibling = (1 - seg, row, col)

    def hops(step):
        return sum(min(d, part - d) for d in divmod(step, part))

    plane_steps = sorted(range(1, n), key=hops, reverse=True)

    def plane_peer(section, step):
        return (
            section,
            row_hi * part + (row_lo + step // part) % part,
            col_hi * part + (col_lo + step % part) % part,
        )

    def plane_index(step):
        return (row_lo + step // part) % part * part + (col_lo + step % part) % part

    def near_peer(step):
        return (seg, (row_hi + step) % part * part + row_lo, col)

    def far_peer(step):
        return (seg, row, (col_hi + step) % part * part + col_lo)

    def there(k):
        dr, dc = DIRECTIONS[k]
        r, c = row + dr, col + dc
        exists = None
        if dr:
            exists = (r >= 0) if dr < 0 else (r < n)
        if dc:
            side = (c >= 0) if dc < 0 else (c < n)
            exists = side if exists is None else jnp.logical_and(exists, side)
        return exists

    def neighbour(k):
        dr, dc = DIRECTIONS[k]
        return (seg, row + dr, col + dc)

    inputs = [
        pltpu.make_async_copy(src, dst, input_sem.at[i])
        for i, (src, dst) in enumerate(
            (
                (act_in, act),
                (cot_in, cot),
                (conv_in, weights.at[seg, 0:CONV_ROWS]),
                (proj_in, weights.at[seg, PROJ_ROW : PROJ_ROW + K]),
                (bias_in, bias_w),
            )
        )
    ]
    for copy in inputs:
        copy.start()
    barrier = pltpu.get_barrier_semaphore()

    def signal(device):
        pl.semaphore_signal(barrier, inc=1, device_id=device, device_id_type=MESH)

    greeted = jnp.int32(1 + 2 * (part - 1))
    pl.when(off_diagonal)(functools.partial(signal, mirror))
    greeted = greeted + off_diagonal.astype(jnp.int32)
    for step in range(1, part):
        signal(far_peer(step))
        signal(near_peer(step))
    for k in range(7, -1, -1):
        pl.when(there(k))(functools.partial(signal, neighbour(k)))
        greeted = greeted + there(k).astype(jnp.int32)
    signal(sibling)

    strip = D0 * SIDE
    corners_of_tile = ((0, 0), (0, SIDE - D0), (SIDE - D0, 0), (SIDE - D0, SIDE - D0))

    def pack_corners(tile, corners):
        for k, (r, c) in enumerate(corners_of_tile):
            stage_f[...] = jnp.zeros((16, C), F32)
            for i in range(D0):
                start = (r + i) * SIDE + c
                stage_f[i * D0 : (i + 1) * D0] = tile[start : start + D0]
            corners[k] = stage_f[...].astype(BF16)

    def pack_narrow(tile, edges, corners):
        edges[0] = tile[0:strip].astype(BF16)
        edges[1] = tile[AREA - strip : AREA].astype(BF16)
        for k, first_column in ((2, 0), (3, SIDE - D0)):
            columns = [tile[pl.ds(first_column + j, SIDE, stride=SIDE), :] for j in range(D0)]
            edges[k] = jnp.concatenate(columns, axis=0).astype(BF16)
        pack_corners(tile, corners)

    inputs[0].wait()
    own_f[...] = act[...].astype(F32)
    pack_narrow(own_f, send_e0, send_c0)

    pl.semaphore_wait(barrier, greeted)

    def pair_copy(src, dst, index, device):
        return pltpu.make_async_remote_copy(
            src_ref=src,
            dst_ref=dst,
            send_sem=pair_send.at[index],
            recv_sem=pair_recv.at[index],
            device_id=device,
            device_id_type=MESH,
        )

    def mirror_copy(src, dst, index):
        return pair_copy(src, dst, index, mirror)

    def mirror_start(src, dst, index):
        @pl.when(off_diagonal)
        def _():
            mirror_copy(src, dst, index).start()

        @pl.when(jnp.logical_not(off_diagonal))
        def _():
            dst[...] = src[...]

    def mirror_wait(src, dst, index):
        pl.when(off_diagonal)(lambda: mirror_copy(src, dst, index).wait_recv())

    def halo_to(phase, k, slot, device, sources, edges, corners):
        return pltpu.make_async_remote_copy(
            src_ref=sources[k],
            dst_ref=edges.at[slot] if slot < 4 else corners.at[slot - 4],
            send_sem=halo_send.at[phase, k],
            recv_sem=halo_recv.at[phase, slot],
            device_id=device,
            device_id_type=MESH,
        )

    def halo_copy(phase, k, sources, edges, corners):
        return halo_to(phase, k, OPPOSITE[k], neighbour(k), sources, edges, corners)

    def halo_start(*halo):
        for k in range(7, -1, -1):
            pl.when(there(k))(lambda k=k: halo_copy(halo[0], k, *halo[1:]).start())

    def halo_clear(phase, sources, edges, corners):
        for k in range(8):

            @pl.when(jnp.logical_not(there(k)))
            def _():
                ref = edges.at[k] if k < 4 else corners.at[k - 4]
                ref[...] = jnp.zeros_like(ref)

    def arrived(phase, k, edges, corners):
        target = edges.at[k] if k < 4 else corners.at[k - 4]
        return pltpu.make_async_remote_copy(
            src_ref=target,
            dst_ref=target,
            send_sem=halo_send.at[phase, k],
            recv_sem=halo_recv.at[phase, k],
            device_id=neighbour(k),
            device_id_type=MESH,
        )

    def halo_wait(phase, sources, edges, corners):
        for k in range(8):
            pl.when(there(k))(lambda k=k: arrived(phase, k, edges, corners).wait_recv())

    def halo_sent(*halo):
        for k in range(8):
            pl.when(there(k))(lambda k=k: halo_copy(halo[0], k, *halo[1:]).wait_send())

    sources0 = tuple(send_e0.at[k] for k in range(4)) + tuple(send_c0.at[k] for k in range(4))
    halo0 = (0, sources0, recv_e0, recv_c0)
    halo_start(*halo0)

    def turn(flat, out):
        @pl.loop(0, SIDE // 2)
        def _(i):
            two = jnp.concatenate(
                [flat[pl.ds(2 * i, SIDE, stride=SIDE), :], flat[pl.ds(2 * i + 1, SIDE, stride=SIDE), :]], axis=0
            )
            out[pl.ds(pl.multiple_of(i * 2 * SIDE, 16), 2 * SIDE), :] = two.astype(BF16)

    inputs[1].wait()
    work_f[...] = cot[...].astype(F32)
    turn(work_f, cot_t)
    pl.when(short)(lambda: mirror_start(cot_t.at[0:288], cot_m.at[0:288], 1))
    pl.when(short)(lambda: mirror_start(cot_t.at[288:AREA], cot_m.at[288:AREA], 3))

    for copy in inputs[2:]:
        copy.wait()
    bias_row = bias_w[...].astype(F32)
    weights[seg, BIAS_ROW : BIAS_ROW + 16] = jnp.broadcast_to(
        jnp.concatenate([bias_row, bias_row], axis=1), (16, 2 * K)
    ).astype(BF16)
    weights_copy = pair_copy(weights.at[seg], weights.at[seg], 2, sibling)
    weights_copy.start()
    halo_clear(*halo0)
    halo_clear(1, None, recv_e1, recv_c1)
    halo_clear(2, None, recv_e2, recv_c2)
    halo_clear(3, None, recv_e3, recv_c3)

    def unpack_narrow(edges, corners, pad, change):
        north = change(edges[0].astype(F32))
        south = change(edges[1].astype(F32))
        west = change(edges[2].astype(F32))
        east = change(edges[3].astype(F32))
        for i in range(D0):
            lines = slice(i * SIDE, (i + 1) * SIDE)
            pad[i * WIDE + 8 : i * WIDE + 8 + SIDE] = north[lines]
            low = (D0 + SIDE + i) * WIDE + 8
            pad[low : low + SIDE] = south[lines]
            pad[pl.ds(D0 * WIDE + 8 - D0 + i, SIDE, stride=WIDE), :] = west[lines]
            pad[pl.ds(D0 * WIDE + 8 + SIDE + i, SIDE, stride=WIDE), :] = east[lines]
        for k, (r, c) in enumerate(((0, 8 - D0), (0, 8 + SIDE), (D0 + SIDE, 8 - D0), (D0 + SIDE, 8 + SIDE))):
            stage_f[...] = change(corners[k].astype(F32))
            for i in range(D0):
                start = (r + i) * WIDE + c
                pad[start : start + D0] = stage_f[i * D0 : (i + 1) * D0]

    def fill_centre(tile, pad, dilation, change):
        for i in range(SIDE):
            start = (dilation + i) * WIDE + 8
            pad[start : start + SIDE] = change(tile[i * SIDE : (i + 1) * SIDE])

    def pack_wide(tile, edges, corners):
        for k, first in ((0, 0), (1, SIDE - D1)):
            edges[k] = jnp.concatenate(
                [tile[i * SIDE + first : i * SIDE + first + D1] for i in range(SIDE)], axis=0
            ).astype(BF16)
        for k, (r, c) in enumerate(((0, 0), (0, SIDE - D1), (SIDE - D1, 0), (SIDE - D1, SIDE - D1))):
            corners[k] = jnp.concatenate(
                [tile[(r + i) * SIDE + c : (r + i) * SIDE + c + D1] for i in range(D1)], axis=0
            ).astype(BF16)

    def wide_sources(flat, edges, corners):
        lines = D1 * SIDE
        return (
            flat.at[0:lines],
            flat.at[AREA - lines : AREA],
            edges.at[0],
            edges.at[1],
        ) + tuple(corners.at[k] for k in range(4))

    def unpack_wide(edges, corners, pad):
        north = edges[0].astype(F32)
        south = edges[1].astype(F32)
        west = edges[2].astype(F32)
        east = edges[3].astype(F32)
        for i in range(D1):
            lines = slice(i * SIDE, (i + 1) * SIDE)
            pad[i * WIDE + D1 : i * WIDE + D1 + SIDE] = north[lines]
            low = (D1 + SIDE + i) * WIDE + D1
            pad[low : low + SIDE] = south[lines]
        for i in range(SIDE):
            lines = slice(i * D1, (i + 1) * D1)
            start = (D1 + i) * WIDE
            pad[start : start + D1] = west[lines]
            pad[start + D1 + SIDE : start + WIDE] = east[lines]
        for k, (r, c) in enumerate(((0, 0), (0, D1 + SIDE), (D1 + SIDE, 0), (D1 + SIDE, D1 + SIDE))):
            corner = corners[k].astype(F32)
            for i in range(D1):
                start = (r + i) * WIDE + c
                pad[start : start + D1] = corner[i * D1 : (i + 1) * D1]

    def spread(pad, cols, dilation):
        for b in range(3):
            first = 8 + (b - 1) * dilation
            for i in range(0, SIDE + 2 * dilation, 2):
                two = jnp.concatenate(
                    [pad[(i + h) * WIDE + first : (i + h) * WIDE + first + SIDE] for h in range(2)], axis=0
                )
                cols[i * SIDE : (i + 2) * SIDE, b * C : (b + 1) * C] = two.astype(BF16)

    same = lambda x: x
    relu = lambda x: jnp.maximum(x, 0.0)

    fill_centre(own_f, pad_a, D0, relu)
    for ref in (first, back1, back0, proj_pad):
        ref[...] = jnp.zeros_like(ref)
    weights_copy.wait_recv()

    proj_pad[0:K] = weights[0, PROJ_ROW : PROJ_ROW + K]
    for s in range(2):
        for h in range(2):
            proj_twice[s, h * K : (h + 1) * K] = weights[s, PROJ_ROW : PROJ_ROW + K]
    tap = lambda a, b: slice((3 * a + b) * K, (3 * a + b + 1) * K)
    for a in range(3):
        for b in range(3):
            lanes = slice(b * C, (b + 1) * C)
            own, turned = slice(b * C, b * C + K), slice(b * C + K, (b + 1) * C)
            first[a, 0:K, lanes] = weights[0, tap(a, b)]
            second[a, 0:K, lanes] = weights[1, tap(a, b)]
            second[a, K : 2 * K, lanes] = weights[1, tap(b, a)]
            back0[a, own] = weights[0, tap(2 - a, 2 - b)]
            back1[a, own, 0:C] = weights[1, tap(2 - a, 2 - b)]
            back1[a, turned, C : 2 * C] = weights[1, tap(2 - b, 2 - a)]

    halo_wait(*halo0)
    unpack_narrow(recv_e0, recv_c0, pad_a, relu)
    spread(pad_a, cols_a, D0)

    chunk = 288
    shift0 = D0 * SIDE
    shift1 = D1 * SIDE

    def rows_at(base, extra=0):
        return pl.ds(pl.multiple_of(base + extra, 16), chunk)

    bias0 = weights[0, BIAS_ROW : BIAS_ROW + 16].astype(F32)[0:1]
    bias1 = weights[1, BIAS_ROW : BIAS_ROW + 16].astype(F32)[0:1]

    @pl.loop(0, AREA // chunk)
    def _(i):
        base = i * chunk
        total = bias0
        for a in range(3):
            total = total + dot(cols_a[rows_at(base, a * shift0), :], first[a], NT)
        pre0[rows_at(base), :] = total
        bottle = jnp.maximum(total, 0.0).astype(BF16)
        bottle0[rows_at(base), :] = bottle
        branch_sum = (own_f[rows_at(base), :] + dot(bottle, proj_pad[...])).astype(BF16)
        work_f[rows_at(base), :] = branch_sum.astype(F32)

    turn(work_f, sum_t)
    mirror_start(sum_t, sum_m, 0)
    pl.when(jnp.logical_not(short))(lambda: mirror_start(cot_t.at[0:288], cot_m.at[0:288], 1))
    pl.when(jnp.logical_not(short))(lambda: mirror_start(cot_t.at[288:AREA], cot_m.at[288:AREA], 3))

    mirror_wait(sum_t, sum_m, 0)

    @pl.loop(0, AREA // chunk)
    def _(i):
        at = rows_at(i * chunk)
        sym = ((work_f[at, :] + sum_m[at, :].astype(F32)) * 0.5).astype(BF16)
        live = jnp.maximum(sym, jnp.zeros_like(sym))
        hidden1[at, :] = live
        work_f[at, :] = live.astype(F32)

    pack_wide(work_f, hid_e, hid_c)
    halo1 = (1, wide_sources(hidden1, hid_e, hid_c), recv_e1, recv_c1)
    halo_start(*halo1)
    fill_centre(work_f, pad_8, D1, same)

    mirror_wait(cot_t.at[0:288], cot_m.at[0:288], 1)
    mirror_wait(cot_t.at[288:AREA], cot_m.at[288:AREA], 3)

    @pl.loop(0, AREA // chunk)
    def _(i):
        at = rows_at(i * chunk)
        branch = ((cot[at, :].astype(F32) + cot_m[at, :].astype(F32)) * 0.5).astype(BF16)
        branch1[at, :] = branch
        grad_bot[at, :] = dot(branch, proj_twice[1], NT)

    halo_wait(*halo1)

    pl.semaphore_signal(partner, inc=1, device_id=sibling, device_id_type=MESH)

    unpack_wide(recv_e1, recv_c1, pad_8)
    spread(pad_8, cols_8, D1)

    @pl.loop(0, AREA // chunk)
    def _(i):
        base = i * chunk
        total = bias1
        for a in range(3):
            total = total + dot(cols_8[rows_at(base, a * shift1), :], second[a], NT)
        bottle1[rows_at(base), :] = jnp.maximum(total, 0.0).astype(BF16)
        grad = jnp.where(total > 0, grad_bot[rows_at(base), :], 0.0)
        work_f[rows_at(base), :] = grad
        gp1[rows_at(base), :] = grad.astype(BF16)

    pack_wide(work_f, gp1_e, gp1_c)
    halo2 = (2, wide_sources(gp1, gp1_e, gp1_c), recv_e2, recv_c2)
    halo_start(*halo2)

    ones = jnp.ones((AREA, C), BF16)

    def weight_gradients(s, grad_pre, cols, shift, bottle, branch):
        turned_grad = grad_pre[...].T[0:K]
        for a in range(3):
            product = dot(turned_grad, cols[a * shift : a * shift + AREA, :])
            for b in range(3):
                at = (3 * a + b) * K
                grads[s, at : at + K] = product[:, b * C : (b + 1) * C].astype(BF16)
        grads[s, 9 * K : 10 * K] = dot(bottle[...].T[0:K], branch[...]).astype(BF16)
        grads[s, 10 * K : 11 * K] = dot(turned_grad, ones).astype(BF16)
        grads[s, 11 * K : 12 * K] = jnp.zeros((K, C), BF16)

    def piece_at(index):
        return pl.ds(pl.multiple_of(index * piece, 16), piece)

    slot_me = seg * n + plane_me

    def group_copy(src, dst, send_sem, recv_sem, device):
        return pltpu.make_async_remote_copy(
            src_ref=src, dst_ref=dst, send_sem=send_sem, recv_sem=recv_sem, device_id=device, device_id_type=MESH
        )

    def plane_copy(s, step):
        return group_copy(
            grads.at[s, piece_at(plane_index(step))],
            plane_recv.at[slot_me],
            plane_send_sem.at[s, step],
            plane_recv_sem.at[slot_me],
            plane_peer(s, step),
        )

    def plane_start(s):
        for step in plane_steps:
            plane_copy(s, step).start()

        @pl.when(seg != s)
        def _():
            plane_copy(s, 0).start()

        @pl.when(seg == s)
        def _():
            plane_recv[slot_me] = grads[s, piece_at(plane_me), :]

    def plane_sent(s):
        for step in plane_steps:
            plane_copy(s, step).wait_send()

        @pl.when(seg != s)
        def _():
            plane_copy(s, 0).wait_send()

    def arrive(dst, send_sem, recv_sem, index):
        group_copy(dst.at[index], dst.at[index], send_sem, recv_sem.at[index], sibling).wait_recv()

    def plane_wait():
        @pl.loop(1, 2 * n)
        def _(step):
            arrive(plane_recv, plane_send_sem.at[0, 0], plane_recv_sem, (slot_me + step) % (2 * n))

    def near_copy(step):
        mine = near_recv.at[row_hi]
        return group_copy(mine, mine, near_send_sem.at[step], near_recv_sem.at[row_hi], near_peer(step))

    def far_copy(step):
        mine = far_recv.at[col_hi]
        return group_copy(mine, mine, far_send_sem.at[step], far_recv_sem.at[col_hi], far_peer(step))

    def all_copy(step):
        mine = total_recv.at[plane_me]
        return group_copy(mine, mine, all_send_sem.at[step], all_recv_sem.at[plane_me], plane_peer(seg, step))

    def add_up(buffer, count):
        total = buffer[0].astype(F32)
        for i in range(1, count):
            total = total + buffer[i].astype(F32)
        return total

    def near_start():
        plane_wait()
        near_recv[row_hi] = add_up(plane_recv, 2 * n).astype(BF16)
        for step in range(1, part):
            near_copy(step).start()

    def far_start():
        for step in range(1, part):
            arrive(near_recv, near_send_sem.at[step], near_recv_sem, (row_hi + step) % part)
        far_recv[col_hi] = add_up(near_recv, part).astype(BF16)
        for step in range(1, part):
            far_copy(step).start()

    weight_gradients(1, gp1, cols_8, shift1, bottle1, branch1)
    pl.semaphore_wait(partner, 1)
    plane_start(1)
    fill_centre(work_f, pad_9, D1, same)

    halo_wait(*halo2)

    unpack_wide(recv_e2, recv_c2, pad_9)
    spread(pad_9, cols_g, D1)

    @pl.loop(0, AREA // chunk)
    def _(i):
        base = i * chunk
        total = None
        for a in range(3):
            term = dot(cols_g[rows_at(base, a * shift1), :], back1[a])
            total = term if total is None else total + term
        branch = branch1[rows_at(base), :].astype(F32)
        live = hidden1[rows_at(base), :].astype(F32) > 0
        own = (branch + jnp.where(live, total[:, 0:C], 0.0)).astype(BF16).astype(F32)
        turned = (branch + jnp.where(live, total[:, C : 2 * C], 0.0)).astype(BF16).astype(F32)
        mean = ((own + turned) * 0.5).astype(BF16)
        branch0[rows_at(base), :] = mean
        grad = jnp.where(pre0[rows_at(base), :] > 0, dot(mean, proj_twice[0], NT), 0.0)
        work_f[rows_at(base), :] = grad
        gp0[rows_at(base), :] = grad.astype(BF16)

    weight_gradients(0, gp0, cols_a, shift0, bottle0, branch0)

    plane_start(0)

    pack_narrow(work_f, gp0_e, gp0_c)
    sources3 = tuple(gp0_e.at[k] for k in range(4)) + tuple(gp0_c.at[k] for k in range(4))
    halo3 = (3, sources3, recv_e3, recv_c3)
    halo_start(*halo3)
    fill_centre(work_f, pad_a, D0, same)

    near_start()

    far_start()

    halo_wait(*halo3)

    unpack_narrow(recv_e3, recv_c3, pad_a, same)
    spread(pad_a, cols_b, D0)

    @pl.loop(0, AREA // chunk)
    def _(i):
        base = i * chunk
        total = None
        for a in range(3):
            term = dot(cols_b[rows_at(base, a * shift0), :], back0[a])
            total = term if total is None else total + term
        branch = branch0[rows_at(base), :].astype(F32)
        live = own_f[rows_at(base), :] > 0
        out_grad[rows_at(base), :] = (branch + jnp.where(live, total, 0.0)).astype(BF16)

    pl.when(off_diagonal)(lambda: mirror_copy(sum_t, sum_m, 0).wait_send())
    pl.when(off_diagonal)(lambda: mirror_copy(cot_t.at[0:288], cot_m.at[0:288], 1).wait_send())
    pl.when(off_diagonal)(lambda: mirror_copy(cot_t.at[288:AREA], cot_m.at[288:AREA], 3).wait_send())
    weights_copy.wait_send()
    for halo in (halo0, halo1, halo2, halo3):
        halo_sent(*halo)
    plane_sent(0)
    plane_sent(1)

    for step in range(1, part):
        arrive(far_recv, far_send_sem.at[step], far_recv_sem, (col_hi + step) % part)

    total_recv[plane_me] = add_up(far_recv, part).astype(BF16)
    for step in plane_steps:
        all_copy(step).start()
    for step in range(1, part):
        near_copy(step).wait_send()
        far_copy(step).wait_send()

    @pl.loop(1, n)
    def _(step):
        arrive(total_recv, all_send_sem.at[step], all_recv_sem, (plane_me + step) % n)

    for step in plane_steps:
        all_copy(step).wait_send()


def write(factor, grad, total, out_grad, out_conv, out_bias, out_proj, sums, bias, sems):
    first = pltpu.make_async_copy(grad, out_grad, sems.at[0])
    first.start()
    pieces, piece = total.shape[0], total.shape[1]
    for i in range(pieces):
        sums[i * piece : (i + 1) * piece] = total[i].astype(F32) * factor
    bias[...] = sums[10 * K : 11 * K].T[0:1]
    copies = [
        pltpu.make_async_copy(sums.at[0:CONV_ROWS], out_conv, sems.at[1]),
        pltpu.make_async_copy(bias, out_bias, sems.at[2]),
        pltpu.make_async_copy(sums.at[9 * K : 10 * K], out_proj, sems.at[3]),
    ]
    for copy in copies:
        copy.start()
    for copy in [first] + copies:
        copy.wait()


def solution(mesh):
    n = mesh.shape["row"]
    cells = mesh.shape["segment"] * (SIDE * n) * (SIDE * n)
    factor = float(np.float32(1.0) / np.sqrt(np.float32(cells)))
    piece = GRAD_ROWS // n
    part = int(round(n**0.5))
    vmem = pltpu.VMEM
    scratch = [
        vmem((AREA, C), BF16),
        vmem((AREA, C), BF16),
        vmem((1, K), BF16),
        vmem((2, PACK_ROWS, C), BF16),
        vmem((3, 2 * K, 3 * C), BF16),
        vmem((3, 2 * K, 3 * C), BF16),
        vmem((3, 3 * C, 2 * C), BF16),
        vmem((3, 3 * C, C), BF16),
        vmem((2 * K, C), BF16),
        vmem((2, 2 * K, C), BF16),
        vmem((AREA, C), F32),
        vmem((AREA, C), F32),
        vmem((16, C), F32),
        vmem((AREA, C), BF16),
        vmem((AREA, C), BF16),
        vmem((AREA, C), BF16),
        vmem((AREA, C), BF16),
        vmem((4, D0 * SIDE, C), BF16),
        vmem((4, 16, C), BF16),
        vmem((4, D0 * SIDE, C), BF16),
        vmem((4, 16, C), BF16),
        vmem((AREA, C), BF16),
        vmem((2, D1 * SIDE, C), BF16),
        vmem((4, D1 * D1, C), BF16),
        vmem((4, D1 * SIDE, C), BF16),
        vmem((4, D1 * D1, C), BF16),
        vmem((AREA, C), BF16),
        vmem((2, D1 * SIDE, C), BF16),
        vmem((4, D1 * D1, C), BF16),
        vmem((4, D1 * SIDE, C), BF16),
        vmem((4, D1 * D1, C), BF16),
        vmem((AREA, C), BF16),
        vmem((4, D0 * SIDE, C), BF16),
        vmem((4, 16, C), BF16),
        vmem((4, D0 * SIDE, C), BF16),
        vmem((4, 16, C), BF16),
        vmem(((SIDE + 2 * D0) * WIDE, C), F32),
        vmem(((SIDE + 2 * D1) * WIDE, C), F32),
        vmem(((SIDE + 2 * D1) * WIDE, C), F32),
        vmem(((SIDE + 2 * D0) * SIDE, 3 * C), BF16),
        vmem(((SIDE + 2 * D0) * SIDE, 3 * C), BF16),
        vmem(((SIDE + 2 * D1) * SIDE, 3 * C), BF16),
        vmem(((SIDE + 2 * D1) * SIDE, 3 * C), BF16),
        vmem((AREA, C), F32),
        vmem((AREA, C), BF16),
        vmem((AREA, C), F32),
        vmem((AREA, C), BF16),
        vmem((AREA, C), BF16),
        vmem((AREA, C), BF16),
        vmem((2, GRAD_ROWS, C), BF16),
        vmem((2 * n, piece, C), BF16),
        vmem((part, piece, C), BF16),
        vmem((part, piece, C), BF16),
        pltpu.SemaphoreType.DMA((4, 8)),
        pltpu.SemaphoreType.DMA((4, 8)),
        pltpu.SemaphoreType.DMA((4,)),
        pltpu.SemaphoreType.DMA((4,)),
        pltpu.SemaphoreType.DMA((2, n)),
        pltpu.SemaphoreType.DMA((2 * n,)),
    ] + [pltpu.SemaphoreType.DMA((part,))] * 4 + [pltpu.SemaphoreType.DMA((n,))] * 2
    scratch += [pltpu.SemaphoreType.REGULAR, pltpu.SemaphoreType.DMA((5,))]

    call = pl.pallas_call(
        functools.partial(kernel, n),
        out_shape=(
            jax.ShapeDtypeStruct((AREA, C), BF16),
            jax.ShapeDtypeStruct((n, piece, C), BF16),
        ),
        in_specs=[pl.BlockSpec(memory_space=pltpu.HBM)] * 5,
        out_specs=[pl.BlockSpec(memory_space=pltpu.VMEM)] * 2,
        scratch_shapes=scratch,
        compiler_params=pltpu.CompilerParams(
            collective_id=0, has_side_effects=True, vmem_limit_bytes=40 * 1024 * 1024
        ),
        name="trunk",
    )

    finish = pl.pallas_call(
        functools.partial(write, factor),
        out_shape=(
            jax.ShapeDtypeStruct((AREA, C), BF16),
            jax.ShapeDtypeStruct((CONV_ROWS, C), F32),
            jax.ShapeDtypeStruct((1, K), F32),
            jax.ShapeDtypeStruct((K, C), F32),
        ),
        in_specs=[pl.BlockSpec(memory_space=pltpu.VMEM)] * 2,
        out_specs=[pl.BlockSpec(memory_space=pltpu.HBM)] * 4,
        scratch_shapes=[vmem((GRAD_ROWS, C), F32), vmem((1, K), F32), pltpu.SemaphoreType.DMA((4,))],
        compiler_params=pltpu.CompilerParams(vmem_limit_bytes=8 * 1024 * 1024),
        name="outputs",
    )

    def local(activations, cotangent, conv_weight, conv_bias, out_weight):
        held = [
            pltpu.with_memory_space_constraint(x, pltpu.HBM)
            for x in (
                activations.reshape(AREA, C),
                cotangent.reshape(AREA, C),
                jnp.swapaxes(conv_weight, 2, 3).reshape(CONV_ROWS, C),
                conv_bias,
                out_weight.reshape(K, C),
            )
        ]
        grad, conv, bias, proj = finish(*call(*held))
        return (
            grad.reshape(1, SIDE, SIDE, C),
            jnp.swapaxes(conv.reshape(1, 9, K, C), 2, 3),
            bias,
            proj.reshape(1, K, C),
        )

    in_specs = (
        P("segment", "row", "col", None),
        P("segment", "row", "col", None),
        P("segment", None, None, None),
        P("segment", None),
        P("segment", None, None),
    )
    out_specs = (
        P("segment", "row", "col", None),
        P("segment", None, None, None),
        P("segment", None),
        P("segment", None, None),
    )
    return jax.shard_map(local, mesh=mesh, in_specs=in_specs, out_specs=out_specs, check_vma=False)
```

```python
import functools

import numpy as np

import jax
import jax.numpy as jnp
from jax import lax
from jax.experimental import pallas as pl
from jax.experimental.pallas import tpu as pltpu
from jax.sharding import PartitionSpec as P

MESH = pl.DeviceIdType.MESH
F32 = jnp.float32
BF16 = jnp.bfloat16

SIDE = 24
AREA = SIDE * SIDE
C = 128
K = 64
D0 = 2
D1 = 8
WIDE = 40
CONV_ROWS = 9 * K
PROJ_ROW = CONV_ROWS
BIAS_ROW = CONV_ROWS + K
PACK_ROWS = CONV_ROWS + K + 16
GRAD_BLOCKS = 12
GRAD_ROWS = GRAD_BLOCKS * K
DIRECTIONS = ((-1, 0), (1, 0), (0, -1), (0, 1), (-1, -1), (-1, 1), (1, -1), (1, 1))
OPPOSITE = (1, 0, 3, 2, 7, 6, 5, 4)
NT = (((1,), (1,)), ((), ()))
TN = (((0,), (0,)), ((), ()))


def dot(a, b, dims=(((1,), (0,)), ((), ()))):
    return lax.dot_general(a, b, dims, preferred_element_type=F32)


def kernel(
    n,
    act_in,
    cot_in,
    conv_in,
    bias_in,
    proj_in,
    out_grad,
    total_recv,
    act,
    cot,
    bias_w,
    weights,
    first,
    second,
    back1,
    back0,
    proj_pad,
    proj_twice,
    own_f,
    work_f,
    stage_f,
    sum_t,
    cot_t,
    sum_m,
    cot_m,
    send_e0,
    send_c0,
    recv_e0,
    recv_c0,
    hidden1,
    hid_e,
    hid_c,
    recv_e1,
    recv_c1,
    gp1,
    gp1_e,
    gp1_c,
    recv_e2,
    recv_c2,
    gp0,
    gp0_e,
    gp0_c,
    recv_e3,
    recv_c3,
    pad_a,
    pad_8,
    pad_9,
    cols_a,
    cols_b,
    cols_8,
    cols_g,
    pre0,
    bottle0,
    grad_bot,
    bottle1,
    branch1,
    branch0,
    grads,
    plane_recv,
    near_recv,
    far_recv,
    halo_send,
    halo_recv,
    pair_send,
    pair_recv,
    plane_send_sem,
    plane_recv_sem,
    near_send_sem,
    near_recv_sem,
    far_send_sem,
    far_recv_sem,
    all_send_sem,
    all_recv_sem,
    partner,
    input_sem,
):
    seg = lax.axis_index("segment")
    row = lax.axis_index("row")
    col = lax.axis_index("col")
    part = int(round(n**0.5))
    piece = GRAD_ROWS // n
    row_hi, row_lo = row // part, row % part
    col_hi, col_lo = col // part, col % part
    plane_me = row_lo * part + col_lo
    off_diagonal = row != col
    short = jnp.logical_and(row_hi - col_hi <= 1, col_hi - row_hi <= 1)
    mirror = (seg, col, row)
    sibling = (1 - seg, row, col)

    def hops(step):
        return sum(min(d, part - d) for d in divmod(step, part))

    plane_steps = sorted(range(1, n), key=hops, reverse=True)

    def plane_peer(section, step):
        return (
            section,
            row_hi * part + (row_lo + step // part) % part,
            col_hi * part + (col_lo + step % part) % part,
        )

    def plane_index(step):
        return (row_lo + step // part) % part * part + (col_lo + step % part) % part

    def near_peer(step):
        return (seg, (row_hi + step) % part * part + row_lo, col)

    def far_peer(step):
        return (seg, row, (col_hi + step) % part * part + col_lo)

    def there(k):
        dr, dc = DIRECTIONS[k]
        r, c = row + dr, col + dc
        exists = None
        if dr:
            exists = (r >= 0) if dr < 0 else (r < n)
        if dc:
            side = (c >= 0) if dc < 0 else (c < n)
            exists = side if exists is None else jnp.logical_and(exists, side)
        return exists

    def neighbour(k):
        dr, dc = DIRECTIONS[k]
        return (seg, row + dr, col + dc)

    inputs = [
        pltpu.make_async_copy(src, dst, input_sem.at[i])
        for i, (src, dst) in enumerate(
            (
                (act_in, act),
                (cot_in, cot),
                (conv_in, weights.at[seg, 0:CONV_ROWS]),
                (proj_in, weights.at[seg, PROJ_ROW : PROJ_ROW + K]),
                (bias_in, bias_w),
            )
        )
    ]
    for copy in inputs:
        copy.start()
    barrier = pltpu.get_barrier_semaphore()

    def signal(device):
        pl.semaphore_signal(barrier, inc=1, device_id=device, device_id_type=MESH)

    greeted = jnp.int32(1 + 2 * (part - 1))
    pl.when(off_diagonal)(functools.partial(signal, mirror))
    greeted = greeted + off_diagonal.astype(jnp.int32)
    for step in range(1, part):
        signal(far_peer(step))
        signal(near_peer(step))
    for k in range(7, -1, -1):
        pl.when(there(k))(functools.partial(signal, neighbour(k)))
        greeted = greeted + there(k).astype(jnp.int32)
    signal(sibling)

    strip = D0 * SIDE
    corners_of_tile = ((0, 0), (0, SIDE - D0), (SIDE - D0, 0), (SIDE - D0, SIDE - D0))

    def pack_corners(tile, corners):
        for k, (r, c) in enumerate(corners_of_tile):
            stage_f[...] = jnp.zeros((16, C), F32)
            for i in range(D0):
                start = (r + i) * SIDE + c
                stage_f[i * D0 : (i + 1) * D0] = tile[start : start + D0]
            corners[k] = stage_f[...].astype(BF16)

    def pack_narrow(tile, edges, corners):
        edges[0] = tile[0:strip].astype(BF16)
        edges[1] = tile[AREA - strip : AREA].astype(BF16)
        for k, first_column in ((2, 0), (3, SIDE - D0)):
            columns = [tile[pl.ds(first_column + j, SIDE, stride=SIDE), :] for j in range(D0)]
            edges[k] = jnp.concatenate(columns, axis=0).astype(BF16)
        pack_corners(tile, corners)

    inputs[0].wait()
    own_f[...] = act[...].astype(F32)
    pack_narrow(own_f, send_e0, send_c0)

    pl.semaphore_wait(barrier, greeted)

    def pair_copy(src, dst, index, device):
        return pltpu.make_async_remote_copy(
            src_ref=src,
            dst_ref=dst,
            send_sem=pair_send.at[index],
            recv_sem=pair_recv.at[index],
            device_id=device,
            device_id_type=MESH,
        )

    def mirror_copy(src, dst, index):
        return pair_copy(src, dst, index, mirror)

    def mirror_start(src, dst, index):
        @pl.when(off_diagonal)
        def _():
            mirror_copy(src, dst, index).start()

        @pl.when(jnp.logical_not(off_diagonal))
        def _():
            dst[...] = src[...]

    def mirror_wait(src, dst, index):
        pl.when(off_diagonal)(lambda: mirror_copy(src, dst, index).wait_recv())

    def halo_to(phase, k, slot, device, sources, edges, corners):
        return pltpu.make_async_remote_copy(
            src_ref=sources[k],
            dst_ref=edges.at[slot] if slot < 4 else corners.at[slot - 4],
            send_sem=halo_send.at[phase, k],
            recv_sem=halo_recv.at[phase, slot],
            device_id=device,
            device_id_type=MESH,
        )

    def halo_copy(phase, k, sources, edges, corners):
        return halo_to(phase, k, OPPOSITE[k], neighbour(k), sources, edges, corners)

    def halo_start(*halo):
        for k in range(7, -1, -1):
            pl.when(there(k))(lambda k=k: halo_copy(halo[0], k, *halo[1:]).start())

    def halo_clear(phase, sources, edges, corners):
        for k in range(8):

            @pl.when(jnp.logical_not(there(k)))
            def _():
                ref = edges.at[k] if k < 4 else corners.at[k - 4]
                ref[...] = jnp.zeros_like(ref)

    def arrived(phase, k, edges, corners):
        target = edges.at[k] if k < 4 else corners.at[k - 4]
        return pltpu.make_async_remote_copy(
            src_ref=target,
            dst_ref=target,
            send_sem=halo_send.at[phase, k],
            recv_sem=halo_recv.at[phase, k],
            device_id=neighbour(k),
            device_id_type=MESH,
        )

    def halo_wait(phase, sources, edges, corners):
        for k in range(8):
            pl.when(there(k))(lambda k=k: arrived(phase, k, edges, corners).wait_recv())

    def halo_sent(*halo):
        for k in range(8):
            pl.when(there(k))(lambda k=k: halo_copy(halo[0], k, *halo[1:]).wait_send())

    sources0 = tuple(send_e0.at[k] for k in range(4)) + tuple(send_c0.at[k] for k in range(4))
    halo0 = (0, sources0, recv_e0, recv_c0)
    halo_start(*halo0)

    def turn(flat, out):
        @pl.loop(0, SIDE // 2)
        def _(i):
            two = jnp.concatenate(
                [flat[pl.ds(2 * i, SIDE, stride=SIDE), :], flat[pl.ds(2 * i + 1, SIDE, stride=SIDE), :]], axis=0
            )
            out[pl.ds(pl.multiple_of(i * 2 * SIDE, 16), 2 * SIDE), :] = two.astype(BF16)

    inputs[1].wait()
    work_f[...] = cot[...].astype(F32)
    turn(work_f, cot_t)
    pl.when(short)(lambda: mirror_start(cot_t, cot_m, 1))

    for copy in inputs[2:]:
        copy.wait()
    bias_row = bias_w[...].astype(F32)
    weights[seg, BIAS_ROW : BIAS_ROW + 16] = jnp.broadcast_to(
        jnp.concatenate([bias_row, bias_row], axis=1), (16, 2 * K)
    ).astype(BF16)
    weights_copy = pair_copy(weights.at[seg], weights.at[seg], 2, sibling)
    weights_copy.start()
    halo_clear(*halo0)
    halo_clear(1, None, recv_e1, recv_c1)
    halo_clear(2, None, recv_e2, recv_c2)
    halo_clear(3, None, recv_e3, recv_c3)

    def unpack_narrow(edges, corners, pad, change):
        north = change(edges[0].astype(F32))
        south = change(edges[1].astype(F32))
        west = change(edges[2].astype(F32))
        east = change(edges[3].astype(F32))
        for i in range(D0):
            lines = slice(i * SIDE, (i + 1) * SIDE)
            pad[i * WIDE + 8 : i * WIDE + 8 + SIDE] = north[lines]
            low = (D0 + SIDE + i) * WIDE + 8
            pad[low : low + SIDE] = south[lines]
            pad[pl.ds(D0 * WIDE + 8 - D0 + i, SIDE, stride=WIDE), :] = west[lines]
            pad[pl.ds(D0 * WIDE + 8 + SIDE + i, SIDE, stride=WIDE), :] = east[lines]
        for k, (r, c) in enumerate(((0, 8 - D0), (0, 8 + SIDE), (D0 + SIDE, 8 - D0), (D0 + SIDE, 8 + SIDE))):
            stage_f[...] = change(corners[k].astype(F32))
            for i in range(D0):
                start = (r + i) * WIDE + c
                pad[start : start + D0] = stage_f[i * D0 : (i + 1) * D0]

    def fill_centre(tile, pad, dilation, change):
        for i in range(SIDE):
            start = (dilation + i) * WIDE + 8
            pad[start : start + SIDE] = change(tile[i * SIDE : (i + 1) * SIDE])

    def pack_wide(tile, edges, corners):
        for k, first in ((0, 0), (1, SIDE - D1)):
            edges[k] = jnp.concatenate(
                [tile[i * SIDE + first : i * SIDE + first + D1] for i in range(SIDE)], axis=0
            ).astype(BF16)
        for k, (r, c) in enumerate(((0, 0), (0, SIDE - D1), (SIDE - D1, 0), (SIDE - D1, SIDE - D1))):
            corners[k] = jnp.concatenate(
                [tile[(r + i) * SIDE + c : (r + i) * SIDE + c + D1] for i in range(D1)], axis=0
            ).astype(BF16)

    def wide_sources(flat, edges, corners):
        lines = D1 * SIDE
        return (
            flat.at[0:lines],
            flat.at[AREA - lines : AREA],
            edges.at[0],
            edges.at[1],
        ) + tuple(corners.at[k] for k in range(4))

    def unpack_wide(edges, corners, pad):
        north = edges[0].astype(F32)
        south = edges[1].astype(F32)
        west = edges[2].astype(F32)
        east = edges[3].astype(F32)
        for i in range(D1):
            lines = slice(i * SIDE, (i + 1) * SIDE)
            pad[i * WIDE + D1 : i * WIDE + D1 + SIDE] = north[lines]
            low = (D1 + SIDE + i) * WIDE + D1
            pad[low : low + SIDE] = south[lines]
        for i in range(SIDE):
            lines = slice(i * D1, (i + 1) * D1)
            start = (D1 + i) * WIDE
            pad[start : start + D1] = west[lines]
            pad[start + D1 + SIDE : start + WIDE] = east[lines]
        for k, (r, c) in enumerate(((0, 0), (0, D1 + SIDE), (D1 + SIDE, 0), (D1 + SIDE, D1 + SIDE))):
            corner = corners[k].astype(F32)
            for i in range(D1):
                start = (r + i) * WIDE + c
                pad[start : start + D1] = corner[i * D1 : (i + 1) * D1]

    def spread(pad, cols, dilation):
        for b in range(3):
            first = 8 + (b - 1) * dilation
            for i in range(0, SIDE + 2 * dilation, 2):
                two = jnp.concatenate(
                    [pad[(i + h) * WIDE + first : (i + h) * WIDE + first + SIDE] for h in range(2)], axis=0
                )
                cols[i * SIDE : (i + 2) * SIDE, b * C : (b + 1) * C] = two.astype(BF16)

    same = lambda x: x
    relu = lambda x: jnp.maximum(x, 0.0)

    fill_centre(own_f, pad_a, D0, relu)
    for ref in (first, back1, back0, proj_pad):
        ref[...] = jnp.zeros_like(ref)
    weights_copy.wait_recv()

    proj_pad[0:K] = weights[0, PROJ_ROW : PROJ_ROW + K]
    for s in range(2):
        for h in range(2):
            proj_twice[s, h * K : (h + 1) * K] = weights[s, PROJ_ROW : PROJ_ROW + K]
    tap = lambda a, b: slice((3 * a + b) * K, (3 * a + b + 1) * K)
    for a in range(3):
        for b in range(3):
            lanes = slice(b * C, (b + 1) * C)
            own, turned = slice(b * C, b * C + K), slice(b * C + K, (b + 1) * C)
            first[a, 0:K, lanes] = weights[0, tap(a, b)]
            second[a, 0:K, lanes] = weights[1, tap(a, b)]
            second[a, K : 2 * K, lanes] = weights[1, tap(b, a)]
            back0[a, own] = weights[0, tap(2 - a, 2 - b)]
            back1[a, own, 0:C] = weights[1, tap(2 - a, 2 - b)]
            back1[a, turned, C : 2 * C] = weights[1, tap(2 - b, 2 - a)]

    halo_wait(*halo0)
    unpack_narrow(recv_e0, recv_c0, pad_a, relu)
    spread(pad_a, cols_a, D0)

    chunk = 288
    shift0 = D0 * SIDE
    shift1 = D1 * SIDE

    def rows_at(base, extra=0):
        return pl.ds(pl.multiple_of(base + extra, 16), chunk)

    bias0 = weights[0, BIAS_ROW : BIAS_ROW + 16].astype(F32)[0:1]
    bias1 = weights[1, BIAS_ROW : BIAS_ROW + 16].astype(F32)[0:1]

    @pl.loop(0, AREA // chunk)
    def _(i):
        base = i * chunk
        total = bias0
        for a in range(3):
            total = total + dot(cols_a[rows_at(base, a * shift0), :], first[a], NT)
        pre0[rows_at(base), :] = total
        bottle = jnp.maximum(total, 0.0).astype(BF16)
        bottle0[rows_at(base), :] = bottle
        branch_sum = (own_f[rows_at(base), :] + dot(bottle, proj_pad[...])).astype(BF16)
        work_f[rows_at(base), :] = branch_sum.astype(F32)

    turn(work_f, sum_t)
    mirror_start(sum_t, sum_m, 0)
    pl.when(jnp.logical_not(short))(lambda: mirror_start(cot_t, cot_m, 1))

    mirror_wait(sum_t, sum_m, 0)

    @pl.loop(0, AREA // chunk)
    def _(i):
        at = rows_at(i * chunk)
        sym = ((work_f[at, :] + sum_m[at, :].astype(F32)) * 0.5).astype(BF16)
        live = jnp.maximum(sym, jnp.zeros_like(sym))
        hidden1[at, :] = live
        work_f[at, :] = live.astype(F32)

    pack_wide(work_f, hid_e, hid_c)
    halo1 = (1, wide_sources(hidden1, hid_e, hid_c), recv_e1, recv_c1)
    halo_start(*halo1)
    fill_centre(work_f, pad_8, D1, same)

    mirror_wait(cot_t, cot_m, 1)

    @pl.loop(0, AREA // chunk)
    def _(i):
        at = rows_at(i * chunk)
        branch = ((cot[at, :].astype(F32) + cot_m[at, :].astype(F32)) * 0.5).astype(BF16)
        branch1[at, :] = branch
        grad_bot[at, :] = dot(branch, proj_twice[1], NT)

    halo_wait(*halo1)

    pl.semaphore_signal(partner, inc=1, device_id=sibling, device_id_type=MESH)

    unpack_wide(recv_e1, recv_c1, pad_8)
    spread(pad_8, cols_8, D1)

    @pl.loop(0, AREA // chunk)
    def _(i):
        base = i * chunk
        total = bias1
        for a in range(3):
            total = total + dot(cols_8[rows_at(base, a * shift1), :], second[a], NT)
        bottle1[rows_at(base), :] = jnp.maximum(total, 0.0).astype(BF16)
        grad = jnp.where(total > 0, grad_bot[rows_at(base), :], 0.0)
        work_f[rows_at(base), :] = grad
        gp1[rows_at(base), :] = grad.astype(BF16)

    pack_wide(work_f, gp1_e, gp1_c)
    halo2 = (2, wide_sources(gp1, gp1_e, gp1_c), recv_e2, recv_c2)
    halo_start(*halo2)

    ones = jnp.ones((AREA, C), BF16)

    def weight_gradients(s, grad_pre, cols, shift, bottle, branch):
        turned_grad = grad_pre[...].T[0:K]
        for a in range(3):
            product = dot(turned_grad, cols[a * shift : a * shift + AREA, :])
            for b in range(3):
                at = (3 * a + b) * K
                grads[s, at : at + K] = product[:, b * C : (b + 1) * C].astype(BF16)
        grads[s, 9 * K : 10 * K] = dot(bottle[...].T[0:K], branch[...]).astype(BF16)
        grads[s, 10 * K : 11 * K] = dot(turned_grad, ones).astype(BF16)
        grads[s, 11 * K : 12 * K] = jnp.zeros((K, C), BF16)

    def piece_at(index):
        return pl.ds(pl.multiple_of(index * piece, 16), piece)

    slot_me = seg * n + plane_me

    def group_copy(src, dst, send_sem, recv_sem, device):
        return pltpu.make_async_remote_copy(
            src_ref=src, dst_ref=dst, send_sem=send_sem, recv_sem=recv_sem, device_id=device, device_id_type=MESH
        )

    def plane_copy(s, step):
        return group_copy(
            grads.at[s, piece_at(plane_index(step))],
            plane_recv.at[slot_me],
            plane_send_sem.at[s, step],
            plane_recv_sem.at[slot_me],
            plane_peer(s, step),
        )

    def plane_start(s):
        for step in plane_steps:
            plane_copy(s, step).start()

        @pl.when(seg != s)
        def _():
            plane_copy(s, 0).start()

        @pl.when(seg == s)
        def _():
            plane_recv[slot_me] = grads[s, piece_at(plane_me), :]

    def plane_sent(s):
        for step in plane_steps:
            plane_copy(s, step).wait_send()

        @pl.when(seg != s)
        def _():
            plane_copy(s, 0).wait_send()

    def arrive(dst, send_sem, recv_sem, index):
        group_copy(dst.at[index], dst.at[index], send_sem, recv_sem.at[index], sibling).wait_recv()

    def plane_wait():
        @pl.loop(1, 2 * n)
        def _(step):
            arrive(plane_recv, plane_send_sem.at[0, 0], plane_recv_sem, (slot_me + step) % (2 * n))

    def near_copy(step):
        mine = near_recv.at[row_hi]
        return group_copy(mine, mine, near_send_sem.at[step], near_recv_sem.at[row_hi], near_peer(step))

    def far_copy(step):
        mine = far_recv.at[col_hi]
        return group_copy(mine, mine, far_send_sem.at[step], far_recv_sem.at[col_hi], far_peer(step))

    def all_copy(step):
        mine = total_recv.at[plane_me]
        return group_copy(mine, mine, all_send_sem.at[step], all_recv_sem.at[plane_me], plane_peer(seg, step))

    def add_up(buffer, count):
        total = buffer[0].astype(F32)
        for i in range(1, count):
            total = total + buffer[i].astype(F32)
        return total

    def near_start():
        plane_wait()
        near_recv[row_hi] = add_up(plane_recv, 2 * n).astype(BF16)
        for step in range(1, part):
            near_copy(step).start()

    def far_start():
        for step in range(1, part):
            arrive(near_recv, near_send_sem.at[step], near_recv_sem, (row_hi + step) % part)
        far_recv[col_hi] = add_up(near_recv, part).astype(BF16)
        for step in range(1, part):
            far_copy(step).start()

    weight_gradients(1, gp1, cols_8, shift1, bottle1, branch1)
    pl.semaphore_wait(partner, 1)
    plane_start(1)
    fill_centre(work_f, pad_9, D1, same)

    halo_wait(*halo2)

    unpack_wide(recv_e2, recv_c2, pad_9)
    spread(pad_9, cols_g, D1)

    @pl.loop(0, AREA // chunk)
    def _(i):
        base = i * chunk
        total = None
        for a in range(3):
            term = dot(cols_g[rows_at(base, a * shift1), :], back1[a])
            total = term if total is None else total + term
        branch = branch1[rows_at(base), :].astype(F32)
        live = hidden1[rows_at(base), :].astype(F32) > 0
        own = (branch + jnp.where(live, total[:, 0:C], 0.0)).astype(BF16).astype(F32)
        turned = (branch + jnp.where(live, total[:, C : 2 * C], 0.0)).astype(BF16).astype(F32)
        mean = ((own + turned) * 0.5).astype(BF16)
        branch0[rows_at(base), :] = mean
        grad = jnp.where(pre0[rows_at(base), :] > 0, dot(mean, proj_twice[0], NT), 0.0)
        work_f[rows_at(base), :] = grad
        gp0[rows_at(base), :] = grad.astype(BF16)

    weight_gradients(0, gp0, cols_a, shift0, bottle0, branch0)

    plane_start(0)

    pack_narrow(work_f, gp0_e, gp0_c)
    sources3 = tuple(gp0_e.at[k] for k in range(4)) + tuple(gp0_c.at[k] for k in range(4))
    halo3 = (3, sources3, recv_e3, recv_c3)
    halo_start(*halo3)
    fill_centre(work_f, pad_a, D0, same)

    near_start()

    far_start()

    halo_wait(*halo3)

    unpack_narrow(recv_e3, recv_c3, pad_a, same)
    spread(pad_a, cols_b, D0)

    @pl.loop(0, AREA // chunk)
    def _(i):
        base = i * chunk
        total = None
        for a in range(3):
            term = dot(cols_b[rows_at(base, a * shift0), :], back0[a])
            total = term if total is None else total + term
        branch = branch0[rows_at(base), :].astype(F32)
        live = own_f[rows_at(base), :] > 0
        out_grad[rows_at(base), :] = (branch + jnp.where(live, total, 0.0)).astype(BF16)

    pl.when(off_diagonal)(lambda: mirror_copy(sum_t, sum_m, 0).wait_send())
    pl.when(off_diagonal)(lambda: mirror_copy(cot_t, cot_m, 1).wait_send())
    weights_copy.wait_send()
    for halo in (halo0, halo1, halo2, halo3):
        halo_sent(*halo)
    plane_sent(0)
    plane_sent(1)

    for step in range(1, part):
        arrive(far_recv, far_send_sem.at[step], far_recv_sem, (col_hi + step) % part)

    total_recv[plane_me] = add_up(far_recv, part).astype(BF16)
    for step in plane_steps:
        all_copy(step).start()
    for step in range(1, part):
        near_copy(step).wait_send()
        far_copy(step).wait_send()

    @pl.loop(1, n)
    def _(step):
        arrive(total_recv, all_send_sem.at[step], all_recv_sem, (plane_me + step) % n)

    for step in plane_steps:
        all_copy(step).wait_send()


def write(factor, grad, total, out_grad, out_conv, out_bias, out_proj, sums, bias, sems):
    first = pltpu.make_async_copy(grad, out_grad, sems.at[0])
    first.start()
    pieces, piece = total.shape[0], total.shape[1]
    for i in range(pieces):
        sums[i * piece : (i + 1) * piece] = total[i].astype(F32) * factor
    bias[...] = sums[10 * K : 11 * K].T[0:1]
    copies = [
        pltpu.make_async_copy(sums.at[0:CONV_ROWS], out_conv, sems.at[1]),
        pltpu.make_async_copy(bias, out_bias, sems.at[2]),
        pltpu.make_async_copy(sums.at[9 * K : 10 * K], out_proj, sems.at[3]),
    ]
    for copy in copies:
        copy.start()
    for copy in [first] + copies:
        copy.wait()


def solution(mesh):
    n = mesh.shape["row"]
    cells = mesh.shape["segment"] * (SIDE * n) * (SIDE * n)
    factor = float(np.float32(1.0) / np.sqrt(np.float32(cells)))
    piece = GRAD_ROWS // n
    part = int(round(n**0.5))
    vmem = pltpu.VMEM
    scratch = [
        vmem((AREA, C), BF16),
        vmem((AREA, C), BF16),
        vmem((1, K), BF16),
        vmem((2, PACK_ROWS, C), BF16),
        vmem((3, 2 * K, 3 * C), BF16),
        vmem((3, 2 * K, 3 * C), BF16),
        vmem((3, 3 * C, 2 * C), BF16),
        vmem((3, 3 * C, C), BF16),
        vmem((2 * K, C), BF16),
        vmem((2, 2 * K, C), BF16),
        vmem((AREA, C), F32),
        vmem((AREA, C), F32),
        vmem((16, C), F32),
        vmem((AREA, C), BF16),
        vmem((AREA, C), BF16),
        vmem((AREA, C), BF16),
        vmem((AREA, C), BF16),
        vmem((4, D0 * SIDE, C), BF16),
        vmem((4, 16, C), BF16),
        vmem((4, D0 * SIDE, C), BF16),
        vmem((4, 16, C), BF16),
        vmem((AREA, C), BF16),
        vmem((2, D1 * SIDE, C), BF16),
        vmem((4, D1 * D1, C), BF16),
        vmem((4, D1 * SIDE, C), BF16),
        vmem((4, D1 * D1, C), BF16),
        vmem((AREA, C), BF16),
        vmem((2, D1 * SIDE, C), BF16),
        vmem((4, D1 * D1, C), BF16),
        vmem((4, D1 * SIDE, C), BF16),
        vmem((4, D1 * D1, C), BF16),
        vmem((AREA, C), BF16),
        vmem((4, D0 * SIDE, C), BF16),
        vmem((4, 16, C), BF16),
        vmem((4, D0 * SIDE, C), BF16),
        vmem((4, 16, C), BF16),
        vmem(((SIDE + 2 * D0) * WIDE, C), F32),
        vmem(((SIDE + 2 * D1) * WIDE, C), F32),
        vmem(((SIDE + 2 * D1) * WIDE, C), F32),
        vmem(((SIDE + 2 * D0) * SIDE, 3 * C), BF16),
        vmem(((SIDE + 2 * D0) * SIDE, 3 * C), BF16),
        vmem(((SIDE + 2 * D1) * SIDE, 3 * C), BF16),
        vmem(((SIDE + 2 * D1) * SIDE, 3 * C), BF16),
        vmem((AREA, C), F32),
        vmem((AREA, C), BF16),
        vmem((AREA, C), F32),
        vmem((AREA, C), BF16),
        vmem((AREA, C), BF16),
        vmem((AREA, C), BF16),
        vmem((2, GRAD_ROWS, C), BF16),
        vmem((2 * n, piece, C), BF16),
        vmem((part, piece, C), BF16),
        vmem((part, piece, C), BF16),
        pltpu.SemaphoreType.DMA((4, 8)),
        pltpu.SemaphoreType.DMA((4, 8)),
        pltpu.SemaphoreType.DMA((4,)),
        pltpu.SemaphoreType.DMA((4,)),
        pltpu.SemaphoreType.DMA((2, n)),
        pltpu.SemaphoreType.DMA((2 * n,)),
    ] + [pltpu.SemaphoreType.DMA((part,))] * 4 + [pltpu.SemaphoreType.DMA((n,))] * 2
    scratch += [pltpu.SemaphoreType.REGULAR, pltpu.SemaphoreType.DMA((5,))]

    call = pl.pallas_call(
        functools.partial(kernel, n),
        out_shape=(
            jax.ShapeDtypeStruct((AREA, C), BF16),
            jax.ShapeDtypeStruct((n, piece, C), BF16),
        ),
        in_specs=[pl.BlockSpec(memory_space=pltpu.HBM)] * 5,
        out_specs=[pl.BlockSpec(memory_space=pltpu.VMEM)] * 2,
        scratch_shapes=scratch,
        compiler_params=pltpu.CompilerParams(
            collective_id=0, has_side_effects=True, vmem_limit_bytes=40 * 1024 * 1024
        ),
        name="trunk",
    )

    finish = pl.pallas_call(
        functools.partial(write, factor),
        out_shape=(
            jax.ShapeDtypeStruct((AREA, C), BF16),
            jax.ShapeDtypeStruct((CONV_ROWS, C), F32),
            jax.ShapeDtypeStruct((1, K), F32),
            jax.ShapeDtypeStruct((K, C), F32),
        ),
        in_specs=[pl.BlockSpec(memory_space=pltpu.VMEM)] * 2,
        out_specs=[pl.BlockSpec(memory_space=pltpu.HBM)] * 4,
        scratch_shapes=[vmem((GRAD_ROWS, C), F32), vmem((1, K), F32), pltpu.SemaphoreType.DMA((4,))],
        compiler_params=pltpu.CompilerParams(vmem_limit_bytes=8 * 1024 * 1024),
        name="outputs",
    )

    def local(activations, cotangent, conv_weight, conv_bias, out_weight):
        held = [
            pltpu.with_memory_space_constraint(x, pltpu.HBM)
            for x in (
                activations.reshape(AREA, C),
                cotangent.reshape(AREA, C),
                jnp.swapaxes(conv_weight, 2, 3).reshape(CONV_ROWS, C),
                conv_bias,
                out_weight.reshape(K, C),
            )
        ]
        grad, conv, bias, proj = finish(*call(*held))
        return (
            grad.reshape(1, SIDE, SIDE, C),
            jnp.swapaxes(conv.reshape(1, 9, K, C), 2, 3),
            bias,
            proj.reshape(1, K, C),
        )

    in_specs = (
        P("segment", "row", "col", None),
        P("segment", "row", "col", None),
        P("segment", None, None, None),
        P("segment", None),
        P("segment", None, None),
    )
    out_specs = (
        P("segment", "row", "col", None),
        P("segment", None, None, None),
        P("segment", None),
        P("segment", None, None),
    )
    return jax.shard_map(local, mesh=mesh, in_specs=in_specs, out_specs=out_specs, check_vma=False)
```
